32 devices in a mesh: dp: 16 (over z, x, core), mp: 2 (over y).
Axes of the slice: x: 2, y: 2, z: 4, core: 2. Of those that a mesh axis runs over, the one named last changes fastest.
Arguments:
- frames: bfloat16 [49152, 1024], P(('dp', 'mp')), may hold values from -6 to 6
- text_states: bfloat16 [4096, 768], P('dp'), may hold values from -6 to 6
- clip_lengths: int32 [32, 4], P('dp'), may hold values from 1 to 768, 1536 in all within a row
- text_lengths: int32 [32, 4], P('dp'), may hold values from 1 to 64, 128 in all within a row
- cotangent: bfloat16 [49152, 1024], P(('dp', 'mp')), may hold values from -6 to 6
- self_gain: float32 [1024], replicated, may hold values from 0.25 to 1.75
- self_shift: float32 [1024], replicated, may hold values from -2 to 2
- self_query: bfloat16 [1024, 1024], P(None, 'mp'), may hold values from -0.1875 to 0.1875
- self_key: bfloat16 [1024, 1024], P(None, 'mp'), may hold values from -0.1875 to 0.1875
- self_value: bfloat16 [1024, 1024], P(None, 'mp'), may hold values from -0.1875 to 0.1875
- self_out: bfloat16 [1024, 1024], P('mp'), may hold values from -0.75 to 0.75
- cross_gain: float32 [1024], replicated, may hold values from 0.25 to 1.75
- cross_shift: float32 [1024], replicated, may hold values from -2 to 2
- cross_query: bfloat16 [1024, 1024], P(None, 'mp'), may hold values from -0.1875 to 0.1875
- cross_key: bfloat16 [1024, 1024], P(None, 'mp'), may hold values from -0.1875 to 0.1875
- cross_value: bfloat16 [1024, 1024], P(None, 'mp'), may hold values from -0.1875 to 0.1875
- cross_out: bfloat16 [1024, 1024], P('mp'), may hold values from -0.5 to 0.5
- text_weight: bfloat16 [768, 1024], P(None, 'mp'), may hold values from -0.21875 to 0.21875
- text_bias: float32 [1024], P('mp'), may hold values from -3 to 3
- feed_gain: float32 [1024], replicated, may hold values from 0.25 to 1.75
- feed_shift: float32 [1024], replicated, may hold values from -2 to 2
- feed_in: bfloat16 [1024, 4096], P(None, 'mp'), may hold values from -0.1875 to 0.1875
- feed_out: bfloat16 [4096, 1024], P('mp'), may hold values from -0.09375 to 0.09375
Outputs:
- output: bfloat16 [49152, 1024], P(('dp', 'mp'))
- frames_grad: float32 [49152, 1024], P(('dp', 'mp'))
- text_grad: float32 [4096, 768], P('dp')
- self_gain_grad: float32 [1024], replicated
- self_shift_grad: float32 [1024], replicated
- self_query_grad: float32 [1024, 1024], P(None, 'mp')
- self_key_grad: float32 [1024, 1024], P(None, 'mp')
- self_value_grad: float32 [1024, 1024], P(None, 'mp')
- self_out_grad: float32 [1024, 1024], P('mp')
- cross_gain_grad: float32 [1024], replicated
- cross_shift_grad: float32 [1024], replicated
- cross_query_grad: float32 [1024, 1024], P(None, 'mp')
- cross_key_grad: float32 [1024, 1024], P(None, 'mp')
- cross_value_grad: float32 [1024, 1024], P(None, 'mp')
- cross_out_grad: float32 [1024, 1024], P('mp')
- text_weight_grad: float32 [768, 1024], P(None, 'mp')
- text_bias_grad: float32 [1024], P('mp')
- feed_gain_grad: float32 [1024], replicated
- feed_shift_grad: float32 [1024], replicated
- feed_in_grad: float32 [1024, 4096], P(None, 'mp')
- feed_out_grad: float32 [4096, 1024], P('mp')
The draws below stay inside these ranges and needn't reach their ends.
Inputs may be any that keep to these rules, and one draw needn't show every extreme that they name: `clip_lengths`: each row's 4 clip lengths sum to 1536, and its longest clip has exactly 768 frames. `text_lengths`: each row's 4 prompt lengths sum to 128, and its longest prompt has exactly 64 tokens; prompt k belongs to clip k of the same row.
All inputs are finite; a program needn't handle non-finite values.
Results may differ from the reference program's by a relative error of at most 0.022.
Values may be sent and summed in bfloat16 or wider, within the bound.
A program may use at most 512 MiB of HBM per device.

```python
import math
import jax
import jax.numpy as jnp
import numpy as np
from jax import lax

D = 1024
HEAD_DIM = 64
FF = 4096
TEXT_D = 768
ROW_LEN = 1536
CLIPS = 4
TXT_ROW = 128
CLIP_MOST = 768
TXT_MOST = 64
ROWS = 32
FRAMES = 49152
TEXT = 4096


def steps_of(key, extent, split, least, largest):
    loudness, own = 1.0, jax.random.fold_in(key, 6)
    for axis_at, parts in split:
        draws = jnp.exp(jax.random.uniform(jax.random.fold_in(own, axis_at), (parts,), jnp.float32, least / len(split), largest / len(split)))
        loudness = loudness * jnp.repeat(draws, extent[axis_at] // parts).reshape([-1 if axis == axis_at else 1 for axis in range(len(extent))])
    return loudness


def profile(count, total, limit, lean):
    weights = [(1 << 20) // math.isqrt(standing ** lean) + 1 for standing in range(2, count + 1)]
    rest, given = total - limit - (count - 1), [1] * (count - 1)
    while rest > 0:
        candidates = [i for i in range(count - 1) if given[i] < limit]
        whole, remaining = sum([weights[i] for i in candidates]), rest
        for i in candidates:
            addition = min(limit - given[i], max(1, remaining * weights[i] // whole), rest)
            given[i] = given[i] + addition
            rest = rest - addition
    return np.array([limit] + given)


def uneven_parts(rng, amount, total, reach, skew):
    if amount == 2:
        one = jax.random.randint(rng, (), max(1, total - reach), min(reach, total - 1) + 1)
        return jnp.stack([one, total - one])
    tallies = jnp.asarray(profile(amount, total, reach, skew), jnp.int32)
    pairs = (amount - 1) // 2
    source_of, sink = tallies[1:1 + 2 * pairs:2], tallies[2:2 + 2 * pairs:2]
    slack = jnp.minimum(source_of - 1, reach - sink)
    moved = jax.random.randint(jax.random.fold_in(rng, 1), (pairs,), 0, 1 << 20) % (slack + 1)
    tallies = tallies.at[1:1 + 2 * pairs:2].set(source_of - moved).at[2:2 + 2 * pairs:2].set(sink + moved)
    return tallies[jax.random.permutation(jax.random.fold_in(rng, 2), amount)]


def gaussian(own_key, shape, spread, limit, pieces=(), kind=jnp.bfloat16):
    result = jax.random.normal(own_key, shape, jnp.float32) * spread
    if len(pieces) > 0:
        result = steps_of(own_key, shape, pieces, -0.22, 0.18) * result
    return jnp.clip(result, min=-limit, max=limit).astype(kind)


def setup_inputs(seed: int = 0) -> dict:
    arg_keys = jax.random.split(jax.random.key(seed), 24)
    frames = gaussian(arg_keys[0], (FRAMES, D), 1.0, 6.0, ((0, 32),))
    text_states = gaussian(arg_keys[1], (TEXT, TEXT_D), 1.0, 6.0, ((0, 16),))
    clip_lengths = jax.vmap(lambda own: uneven_parts(own, CLIPS, ROW_LEN, CLIP_MOST, 2))(jax.random.split(arg_keys[2], ROWS)).reshape((ROWS, CLIPS)).astype(jnp.int32)
    text_lengths = jax.vmap(lambda own: uneven_parts(own, CLIPS, TXT_ROW, TXT_MOST, 1))(jax.random.split(arg_keys[3], ROWS)).reshape((ROWS, CLIPS)).astype(jnp.int32)
    cotangent = gaussian(arg_keys[4], (FRAMES, D), 1.0, 6.0, ((0, 32),))
    self_gain = jnp.clip(1.0 + 0.15 * jax.random.normal(arg_keys[5], (D,), jnp.float32), 0.25, 1.75)
    self_shift = gaussian(arg_keys[6], (D,), 0.3, 2.0, (), jnp.float32)
    self_query = gaussian(arg_keys[7], (D, D), D ** -0.5, 0.1875, ((1, 2),))
    self_key = gaussian(arg_keys[8], (D, D), D ** -0.5, 0.1875, ((1, 2),))
    self_value = gaussian(arg_keys[9], (D, D), D ** -0.5, 0.1875, ((1, 2),))
    self_out = gaussian(arg_keys[10], (D, D), (D // 16) ** -0.5, 0.75, ((0, 2),))
    cross_gain = jnp.clip(1.0 + 0.15 * jax.random.normal(arg_keys[11], (D,), jnp.float32), 0.25, 1.75)
    cross_shift = gaussian(arg_keys[12], (D,), 0.3, 2.0, (), jnp.float32)
    cross_query = gaussian(arg_keys[13], (D, D), D ** -0.5, 0.1875, ((1, 2),))
    cross_key = gaussian(arg_keys[14], (D, D), D ** -0.5, 0.1875, ((1, 2),))
    cross_value = gaussian(arg_keys[15], (D, D), D ** -0.5, 0.1875, ((1, 2),))
    cross_out = gaussian(arg_keys[16], (D, D), (D // 8) ** -0.5, 0.5, ((0, 2),))
    text_weight = gaussian(arg_keys[17], (TEXT_D, D), TEXT_D ** -0.5, 0.21875, ((1, 2),))
    text_bias = gaussian(arg_keys[18], (D,), 0.5, 3.0, ((0, 2),), jnp.float32)
    feed_gain = jnp.clip(1.0 + 0.15 * jax.random.normal(arg_keys[19], (D,), jnp.float32), 0.25, 1.75)
    feed_shift = gaussian(arg_keys[20], (D,), 0.3, 2.0, (), jnp.float32)
    feed_in = gaussian(arg_keys[21], (D, FF), D ** -0.5, 0.1875, ((1, 2),))
    feed_out = gaussian(arg_keys[22], (FF, D), FF ** -0.5, 0.09375, ((0, 2),))
    return dict(frames=frames, text_states=text_states, clip_lengths=clip_lengths, text_lengths=text_lengths, cotangent=cotangent, self_gain=self_gain, self_shift=self_shift, self_query=self_query, self_key=self_key, self_value=self_value, self_out=self_out, cross_gain=cross_gain, cross_shift=cross_shift, cross_query=cross_query, cross_key=cross_key, cross_value=cross_value, cross_out=cross_out, text_weight=text_weight, text_bias=text_bias, feed_gain=feed_gain, feed_shift=feed_shift, feed_in=feed_in, feed_out=feed_out)


@jax.custom_vjp
def low(v):
    return lax.optimization_barrier(v.astype(jnp.bfloat16)).astype(jnp.float32)

@jax.custom_vjp
def low_back(v):
    return v

def low_keep(v):
    return (low(v), None)

def low_pass(kept, grad):
    return (grad,)

def back_keep(v):
    return (v, None)

def back_low(kept, grad):
    return (low(grad),)
low.defvjp(low_keep, low_pass)
low_back.defvjp(back_keep, back_low)
EPSILON = 1e-05
MASKED = -1e+30
PRECISE = lax.Precision.HIGHEST

def matmul(left_side, right_side):
    return jnp.dot(left_side, right_side, precision=PRECISE)

def layer_norm(tensor, norm_gain, norm_shift):
    average = lax.optimization_barrier(jnp.mean(tensor, axis=-1, keepdims=True))
    centered = tensor - average
    variance = lax.optimization_barrier(jnp.mean(centered * centered, axis=-1, keepdims=True))
    return centered * lax.rsqrt(variance + EPSILON) * norm_gain + norm_shift

def segment_ids(lengths, positions):
    bounds = jnp.cumsum(lengths, axis=-1)
    places = jnp.arange(positions, dtype=jnp.int32)
    return lax.optimization_barrier(jnp.sum((places[None, :, None] >= bounds[:, None, :]).astype(jnp.int32), axis=-1))

def split_heads(tensor, row_count):
    return tensor.reshape(row_count, tensor.shape[0] // row_count, tensor.shape[1] // HEAD_DIM, HEAD_DIM)

def attend(queries, key_heads, values, allowed):
    scores = jnp.einsum('qhd,khd->hqk', queries, key_heads, precision=PRECISE) * HEAD_DIM ** (-0.5)
    scores = low_back(scores)
    scores = jnp.where(allowed[None], scores, MASKED)
    soft_weights = low(jax.nn.softmax(scores, axis=-1))
    return jnp.einsum('hqk,khd->qhd', soft_weights, values, precision=PRECISE)

def self_row(inputs):
    queries, key_heads, values, segments = inputs
    places = jnp.arange(segments.shape[0], dtype=jnp.int32)
    allowed = (segments[:, None] == segments[None, :]) & (places[:, None] >= places[None, :])
    return attend(queries, key_heads, values, allowed)

def cross_row(inputs):
    queries, key_heads, values, segments, text_segments = inputs
    return attend(queries, key_heads, values, segments[:, None] == text_segments[None, :])

def forward(clip_segs, text_segs, frames, text_states, self_gain, self_shift, self_query, self_key, self_value, self_out, cross_gain, cross_shift, cross_query, cross_key, cross_value, cross_out, text_weight, text_bias, feed_gain, feed_shift, feed_in, feed_out):
    row_count = clip_segs.shape[0]
    self_rows = low(layer_norm(frames, self_gain, self_shift))
    self_queries = low(low_back(matmul(self_rows, self_query)))
    self_keys = low(low_back(matmul(self_rows, self_key)))
    self_values = low(low_back(matmul(self_rows, self_value)))
    self_context = lax.map(jax.checkpoint(self_row), (split_heads(self_queries, row_count), split_heads(self_keys, row_count), split_heads(self_values, row_count), clip_segs))
    self_context = low(low_back(self_context.reshape(self_queries.shape)))
    middle = frames + low_back(matmul(self_context, self_out))
    cross_rows = low(layer_norm(middle, cross_gain, cross_shift))
    text_full = low(low_back(matmul(text_states, text_weight) + text_bias))
    cross_queries = low(low_back(matmul(cross_rows, cross_query)))
    cross_keys = low(low_back(matmul(text_full, cross_key)))
    cross_values = low(low_back(matmul(text_full, cross_value)))
    cross_context = lax.map(jax.checkpoint(cross_row), (split_heads(cross_queries, row_count), split_heads(cross_keys, row_count), split_heads(cross_values, row_count), clip_segs, text_segs))
    cross_context = low(low_back(cross_context.reshape(cross_queries.shape)))
    after_cross = middle + low_back(matmul(cross_context, cross_out))
    feed_rows = low(layer_norm(after_cross, feed_gain, feed_shift))
    hidden = low_back(matmul(feed_rows, feed_in))
    active = low(jax.nn.gelu(hidden, approximate=False))
    return after_cross + low_back(matmul(active, feed_out))

def reference(frames, text_states, clip_lengths, text_lengths, cotangent, self_gain, self_shift, self_query, self_key, self_value, self_out, cross_gain, cross_shift, cross_query, cross_key, cross_value, cross_out, text_weight, text_bias, feed_gain, feed_shift, feed_in, feed_out):
    clip_segs = segment_ids(clip_lengths, ROW_LEN)
    text_segs = segment_ids(text_lengths, TXT_ROW)

    def whole_layer(*inputs):
        return forward(clip_segs, text_segs, *inputs)
    floats = (frames.astype(jnp.float32), text_states.astype(jnp.float32), self_gain.astype(jnp.float32), self_shift.astype(jnp.float32), self_query.astype(jnp.float32), self_key.astype(jnp.float32), self_value.astype(jnp.float32), self_out.astype(jnp.float32), cross_gain.astype(jnp.float32), cross_shift.astype(jnp.float32), cross_query.astype(jnp.float32), cross_key.astype(jnp.float32), cross_value.astype(jnp.float32), cross_out.astype(jnp.float32), text_weight.astype(jnp.float32), text_bias.astype(jnp.float32), feed_gain.astype(jnp.float32), feed_shift.astype(jnp.float32), feed_in.astype(jnp.float32), feed_out.astype(jnp.float32))
    output, pullback = jax.vjp(whole_layer, *floats)
    gradients = pullback(cotangent.astype(jnp.float32))
    return (output.astype(jnp.bfloat16), gradients[0], gradients[1], gradients[2], gradients[3], gradients[4], gradients[5], gradients[6], gradients[7], gradients[8], gradients[9], gradients[10], gradients[11], gradients[12], gradients[13], gradients[14], gradients[15], gradients[16], gradients[17], gradients[18], gradients[19])
```

```python
import functools
from functools import reduce

import jax
import jax.numpy as jnp
from jax import lax
from jax.experimental import pallas as pl
from jax.experimental.pallas import tpu as pltpu
from jax.sharding import PartitionSpec as P

HEAD_DIM = 64
ROW_LEN = 1536
TXT_ROW = 128


EPSILON = 1e-05
MASKED = -1e30


def product(left_side, right_side):
    return jnp.dot(left_side, right_side, preferred_element_type=jnp.float32)


def against(left_side, right_side):
    return lax.dot_general(
        left_side, right_side, (((1,), (1,)), ((), ())), preferred_element_type=jnp.float32
    )


def outer_sum(left_side, right_side):
    return lax.dot_general(
        left_side, right_side, (((0,), (0,)), ((), ())), preferred_element_type=jnp.float32
    )


def exact_gelu(tensor):
    return jax.nn.gelu(tensor, approximate=False)


def segment_ids(lengths, positions):
    bounds = jnp.cumsum(lengths, axis=-1)
    places = jnp.arange(positions, dtype=jnp.int32)
    return jnp.sum((places[None, :, None] >= bounds[:, None, :]).astype(jnp.int32), axis=-1)


def split_heads(tensor, row_count):
    return tensor.reshape(
        row_count, tensor.shape[0] // row_count, tensor.shape[1] // HEAD_DIM, HEAD_DIM
    )


def norm_parts(tensor):
    average = jnp.mean(tensor, axis=-1, keepdims=True)
    centered = tensor - average
    inverse = lax.rsqrt(jnp.mean(centered * centered, axis=-1, keepdims=True) + EPSILON)
    return (centered * inverse, inverse)


def norm_back(gradient, standard, inverse, norm_gain):
    scaled = gradient * norm_gain
    first_mean = jnp.mean(scaled, axis=-1, keepdims=True)
    second_mean = jnp.mean(scaled * standard, axis=-1, keepdims=True)
    return (
        inverse * (scaled - first_mean - standard * second_mean),
        jnp.sum(gradient * standard, axis=0),
        jnp.sum(gradient, axis=0),
    )


def spread_rows(tensor):
    return lax.all_gather(tensor, "mp", axis=0, tiled=True)


def spread_cotangent(tensor):
    return lax.all_gather(tensor, "mp", axis=0, tiled=True)


def branch_sum(left_side, right_side):
    return lax.psum_scatter(product(left_side, right_side), "mp", scatter_dimension=0, tiled=True)


def input_grads(factor_pairs):
    partials = [against(left_side, right_side) for left_side, right_side in factor_pairs]
    return lax.psum_scatter(reduce(jnp.add, partials), "mp", scatter_dimension=0, tiled=True)


def attend_forward(queries, key_heads, values, allowed):
    scores = jnp.einsum(
        "rqhd,rkhd->rhqk", queries, key_heads, preferred_element_type=jnp.float32
    ) * HEAD_DIM ** (-0.5)
    scores = jnp.where(allowed[:, None], scores, MASKED)
    row_max = jnp.max(scores, axis=-1, keepdims=True)
    shifted = jnp.exp(scores - row_max)
    totals = jnp.sum(shifted, axis=-1, keepdims=True)
    soft_weights = (shifted / totals).astype(jnp.bfloat16)
    context = jnp.einsum(
        "rhqk,rkhd->rqhd", soft_weights, values, preferred_element_type=jnp.float32
    )
    return (context, row_max + jnp.log(totals))


def attend_back(queries, key_heads, values, allowed, log_totals, grad_context):
    score_scale = HEAD_DIM ** (-0.5)
    scores = (
        jnp.einsum("rqhd,rkhd->rhqk", queries, key_heads, preferred_element_type=jnp.float32)
        * score_scale
    )
    scores = jnp.where(allowed[:, None], scores, MASKED)
    soft_weights = jnp.exp(scores - log_totals)
    grad_soft = jnp.einsum(
        "rqhd,rkhd->rhqk", grad_context, values, preferred_element_type=jnp.float32
    )
    row_inner = jnp.sum(grad_soft * soft_weights, axis=-1, keepdims=True)
    grad_scores = (soft_weights * (grad_soft - row_inner)).astype(jnp.bfloat16)
    grad_query = (
        jnp.einsum("rhqk,rkhd->rqhd", grad_scores, key_heads, preferred_element_type=jnp.float32)
        * score_scale
    )
    grad_keys = (
        jnp.einsum("rhqk,rqhd->rkhd", grad_scores, queries, preferred_element_type=jnp.float32)
        * score_scale
    )
    grad_values = jnp.einsum(
        "rhqk,rqhd->rkhd",
        soft_weights.astype(jnp.bfloat16),
        grad_context,
        preferred_element_type=jnp.float32,
    )
    return (grad_query, grad_keys, grad_values)


def self_allowed(segments, start_at, stop_at):
    places = jnp.arange(stop_at, dtype=jnp.int32)
    same_clip = segments[:, start_at:stop_at, None] == segments[:, None, :stop_at]
    return same_clip & (places[start_at:stop_at, None] >= places[None, :])[None]


def self_forward(queries, key_heads, values, segments):
    block_size = min(512, queries.shape[1])
    contexts = []
    log_totals = []
    for start_at in range(0, queries.shape[1], block_size):
        stop_at = start_at + block_size
        context, log_total = attend_forward(
            queries[:, start_at:stop_at],
            key_heads[:, :stop_at],
            values[:, :stop_at],
            self_allowed(segments, start_at, stop_at),
        )
        contexts.append(context)
        log_totals.append(log_total)
    return (jnp.concatenate(contexts, axis=1), jnp.concatenate(log_totals, axis=2))


def self_back(queries, key_heads, values, segments, log_totals, grad_context):
    block_size = min(512, queries.shape[1])
    query_parts = []
    grad_keys = jnp.zeros(key_heads.shape, jnp.float32)
    grad_values = jnp.zeros(values.shape, jnp.float32)
    for start_at in range(0, queries.shape[1], block_size):
        stop_at = start_at + block_size
        grad_query, key_part, value_part = attend_back(
            queries[:, start_at:stop_at],
            key_heads[:, :stop_at],
            values[:, :stop_at],
            self_allowed(segments, start_at, stop_at),
            log_totals[:, :, start_at:stop_at],
            grad_context[:, start_at:stop_at],
        )
        query_parts.append(grad_query)
        grad_keys = grad_keys.at[:, :stop_at].add(key_part)
        grad_values = grad_values.at[:, :stop_at].add(value_part)
    return (jnp.concatenate(query_parts, axis=1), grad_keys, grad_values)


def body(
    frames,
    text_states,
    clip_lengths,
    text_lengths,
    cotangent,
    self_gain,
    self_shift,
    self_query,
    self_key,
    self_value,
    self_out,
    cross_gain,
    cross_shift,
    cross_query,
    cross_key,
    cross_value,
    cross_out,
    text_weight,
    text_bias,
    feed_gain,
    feed_shift,
    feed_in,
    feed_out,
):
    row_count = clip_lengths.shape[0]
    clip_segs = segment_ids(clip_lengths, ROW_LEN)
    text_segs = segment_ids(text_lengths, TXT_ROW)
    residual = frames.astype(jnp.float32)
    self_standard, self_inverse = norm_parts(residual)
    self_rows = spread_rows((self_standard * self_gain + self_shift).astype(jnp.bfloat16))
    self_queries = product(self_rows, self_query).astype(jnp.bfloat16)
    self_keys = product(self_rows, self_key).astype(jnp.bfloat16)
    self_values = product(self_rows, self_value).astype(jnp.bfloat16)
    self_context, self_logs = self_forward(
        split_heads(self_queries, row_count),
        split_heads(self_keys, row_count),
        split_heads(self_values, row_count),
        clip_segs,
    )
    self_context = self_context.reshape(self_queries.shape).astype(jnp.bfloat16)
    middle = residual + branch_sum(self_context, self_out)
    cross_standard, cross_inverse = norm_parts(middle)
    cross_rows = spread_rows((cross_standard * cross_gain + cross_shift).astype(jnp.bfloat16))
    text_part = (product(text_states, text_weight) + text_bias).astype(jnp.bfloat16)
    text_full = lax.all_gather(text_part, "mp", axis=1, tiled=True)
    cross_queries = product(cross_rows, cross_query).astype(jnp.bfloat16)
    cross_keys = product(text_full, cross_key).astype(jnp.bfloat16)
    cross_values = product(text_full, cross_value).astype(jnp.bfloat16)
    cross_allowed = clip_segs[:, :, None] == text_segs[:, None, :]
    cross_context, cross_logs = attend_forward(
        split_heads(cross_queries, row_count),
        split_heads(cross_keys, row_count),
        split_heads(cross_values, row_count),
        cross_allowed,
    )
    cross_context = cross_context.reshape(cross_queries.shape).astype(jnp.bfloat16)
    after_cross = middle + branch_sum(cross_context, cross_out)
    feed_standard, feed_inverse = norm_parts(after_cross)
    feed_normed = (feed_standard * feed_gain + feed_shift).astype(jnp.bfloat16)
    feed_rows = spread_rows(feed_normed)
    hidden = product(feed_rows, feed_in)
    active, gelu_back = jax.vjp(exact_gelu, hidden)
    active = active.astype(jnp.bfloat16)
    output = after_cross + branch_sum(active, feed_out)
    grad_output = cotangent.astype(jnp.float32)
    feed_cotangent = grad_output.astype(jnp.bfloat16)
    grad_rows = spread_cotangent(feed_cotangent)
    feed_out_grad = outer_sum(active, grad_rows)
    grad_hidden = gelu_back(against(grad_rows, feed_out))[0].astype(jnp.bfloat16)
    feed_in_grad = outer_sum(feed_rows, grad_hidden)
    grad_feed_normed = input_grads(((grad_hidden, feed_in),))
    grad_norm, feed_gain_grad, feed_shift_grad = norm_back(
        grad_feed_normed, feed_standard, feed_inverse, feed_gain
    )
    grad_after = grad_output + grad_norm
    cross_cotangent = spread_cotangent(grad_after.astype(jnp.bfloat16))
    cross_out_grad = outer_sum(cross_context, cross_cotangent)
    grad_context = against(cross_cotangent, cross_out).astype(jnp.bfloat16)
    grad_queries, grad_keys, grad_values = attend_back(
        split_heads(cross_queries, row_count),
        split_heads(cross_keys, row_count),
        split_heads(cross_values, row_count),
        cross_allowed,
        cross_logs,
        split_heads(grad_context, row_count),
    )
    grad_queries = grad_queries.reshape(cross_queries.shape).astype(jnp.bfloat16)
    grad_keys = grad_keys.reshape(cross_keys.shape).astype(jnp.bfloat16)
    grad_values = grad_values.reshape(cross_values.shape).astype(jnp.bfloat16)
    cross_query_grad = outer_sum(cross_rows, grad_queries)
    cross_key_grad = outer_sum(text_full, grad_keys)
    cross_value_grad = outer_sum(text_full, grad_values)
    grad_text_full = against(grad_keys, cross_key) + against(grad_values, cross_value)
    grad_text = lax.psum_scatter(
        grad_text_full.astype(jnp.bfloat16), "mp", scatter_dimension=1, tiled=True
    )
    text_weight_grad = outer_sum(text_states, grad_text)
    text_bias_grad = jnp.sum(grad_text.astype(jnp.float32), axis=0)
    text_grad = lax.psum(against(grad_text, text_weight).astype(jnp.bfloat16), "mp").astype(
        jnp.float32
    )
    grad_cross_normed = input_grads(((grad_queries, cross_query),))
    grad_norm, cross_gain_grad, cross_shift_grad = norm_back(
        grad_cross_normed, cross_standard, cross_inverse, cross_gain
    )
    grad_middle = grad_after + grad_norm
    self_cotangent = spread_cotangent(grad_middle.astype(jnp.bfloat16))
    self_out_grad = outer_sum(self_context, self_cotangent)
    grad_context = against(self_cotangent, self_out).astype(jnp.bfloat16)
    grad_queries, grad_keys, grad_values = self_back(
        split_heads(self_queries, row_count),
        split_heads(self_keys, row_count),
        split_heads(self_values, row_count),
        clip_segs,
        self_logs,
        split_heads(grad_context, row_count),
    )
    grad_queries = grad_queries.reshape(self_queries.shape).astype(jnp.bfloat16)
    grad_keys = grad_keys.reshape(self_keys.shape).astype(jnp.bfloat16)
    grad_values = grad_values.reshape(self_values.shape).astype(jnp.bfloat16)
    self_query_grad = outer_sum(self_rows, grad_queries)
    self_key_grad = outer_sum(self_rows, grad_keys)
    self_value_grad = outer_sum(self_rows, grad_values)
    grad_self_normed = input_grads(
        ((grad_queries, self_query), (grad_keys, self_key), (grad_values, self_value))
    )
    grad_norm, self_gain_grad, self_shift_grad = norm_back(
        grad_self_normed, self_standard, self_inverse, self_gain
    )
    frames_grad = grad_middle + grad_norm
    (
        self_query_grad,
        self_key_grad,
        self_value_grad,
        self_out_grad,
        cross_query_grad,
        cross_key_grad,
        cross_value_grad,
        cross_out_grad,
        text_weight_grad,
        text_bias_grad,
        feed_in_grad,
        feed_out_grad,
    ) = (
        lax.psum(self_query_grad.astype(jnp.bfloat16), "dp").astype(jnp.float32),
        lax.psum(self_key_grad.astype(jnp.bfloat16), "dp").astype(jnp.float32),
        lax.psum(self_value_grad.astype(jnp.bfloat16), "dp").astype(jnp.float32),
        lax.psum(self_out_grad.astype(jnp.bfloat16), "dp").astype(jnp.float32),
        lax.psum(cross_query_grad.astype(jnp.bfloat16), "dp").astype(jnp.float32),
        lax.psum(cross_key_grad.astype(jnp.bfloat16), "dp").astype(jnp.float32),
        lax.psum(cross_value_grad.astype(jnp.bfloat16), "dp").astype(jnp.float32),
        lax.psum(cross_out_grad.astype(jnp.bfloat16), "dp").astype(jnp.float32),
        lax.psum(text_weight_grad.astype(jnp.bfloat16), "dp").astype(jnp.float32),
        lax.psum(text_bias_grad.astype(jnp.bfloat16), "dp").astype(jnp.float32),
        lax.psum(feed_in_grad.astype(jnp.bfloat16), "dp").astype(jnp.float32),
        lax.psum(feed_out_grad.astype(jnp.bfloat16), "dp").astype(jnp.float32),
    )
    (
        self_gain_grad,
        self_shift_grad,
        cross_gain_grad,
        cross_shift_grad,
        feed_gain_grad,
        feed_shift_grad,
    ) = lax.psum(
        (
            self_gain_grad,
            self_shift_grad,
            cross_gain_grad,
            cross_shift_grad,
            feed_gain_grad,
            feed_shift_grad,
        ),
        ("dp", "mp"),
    )
    return (
        output.astype(jnp.bfloat16),
        frames_grad,
        text_grad,
        self_gain_grad,
        self_shift_grad,
        self_query_grad,
        self_key_grad,
        self_value_grad,
        self_out_grad,
        cross_gain_grad,
        cross_shift_grad,
        cross_query_grad,
        cross_key_grad,
        cross_value_grad,
        cross_out_grad,
        text_weight_grad,
        text_bias_grad,
        feed_gain_grad,
        feed_shift_grad,
        feed_in_grad,
        feed_out_grad,
    )


LOG2E=1.4426950408889634
SCALE2=LOG2E*HEAD_DIM**-0.5
BQ=256
SPAN=768

def dot(a,b,ca,cb):
    return lax.dot_general(a,b,(((ca,),(cb,)),((),())),preferred_element_type=jnp.float32)

def starts_of(bounds_ref, places):
    start=jnp.zeros_like(places)
    for k in range(3):
        start=jnp.where(places>=bounds_ref[k],bounds_ref[k],start)
    return start

def self_fwd_kernel(bounds_ref,q_ref,k_ref,v_ref,o_ref,lse_ref,*,ahead=2):
    low=lax.broadcasted_iota(jnp.int32,(1,128),1)<HEAD_DIM
    vt=jnp.transpose(v_ref[...])
    pad=jnp.ones((16,ROW_LEN),jnp.bfloat16)
    vts=[jnp.concatenate([vt[64*h:64*h+64],pad],0) for h in range(2)]
    def span(i):
        return max(0,BQ*i-SPAN),BQ*(i+1)
    def scores(i,h):
        k0,k1=span(i)
        q=q_ref[BQ*i:k1,:]
        qh=jnp.where(low==(h==0),q,jnp.zeros_like(q))
        places=BQ*i+lax.broadcasted_iota(jnp.int32,(1,BQ),1)
        keys=k0+lax.broadcasted_iota(jnp.int32,(k1-k0,BQ),0)
        allowed=(keys>=starts_of(bounds_ref,places))&(keys<=places)
        return jnp.where(allowed,dot(k_ref[k0:k1,:],qh,1,1),MASKED)
    items=[(i,h) for i in range(ROW_LEN//BQ) for h in range(2)]
    queue=[scores(*it) for it in items[:ahead]]
    outs=[]
    for n,(i,h) in enumerate(items):
        if n+ahead<len(items):
            queue.append(scores(*items[n+ahead]))
        s=queue.pop(0)
        k0,k1=span(i)
        m=jnp.max(s,axis=0,keepdims=True)
        p=jnp.exp2((s-m)*SCALE2)
        o=dot(vts[h][:,k0:k1],p.astype(jnp.bfloat16),1,0)
        l=o[64:65]
        outs.append(o[:64]*(1.0/l))
        lse_ref[0,h:h+1,BQ*i:k1]=m*SCALE2+jnp.log2(l)
        if h==1:
            o_ref[BQ*i:k1,:]=jnp.transpose(jnp.concatenate(outs,0)).astype(jnp.bfloat16)
            outs=[]

def row_self_forward(bounds,q,k,v):
    pairs=q.shape[1]//128
    spec=pl.BlockSpec((ROW_LEN,128),lambda h:(0,h))
    return pl.pallas_call(self_fwd_kernel,grid=(pairs,),
        in_specs=[pl.BlockSpec(memory_space=pltpu.SMEM),spec,spec,spec],
        out_specs=[spec,pl.BlockSpec((1,2,ROW_LEN),lambda h:(h,0,0))],
        out_shape=[jax.ShapeDtypeStruct(q.shape,jnp.bfloat16),jax.ShapeDtypeStruct((pairs,2,ROW_LEN),jnp.float32)],
        compiler_params=pltpu.CompilerParams(vmem_limit_bytes=40<<20),
        name="self_forward",
        cost_estimate=pl.CostEstimate(flops=pairs*2*18*256*256*64*4*4,bytes_accessed=pairs*4*1536*256,transcendentals=0),
    )(bounds,q,k,v)

def self_bwd_kernel(bounds_ref,q_ref,k_ref,v_ref,o_ref,g_ref,lse_ref,dq_ref,dk_ref,dv_ref,acc_ref,d_ref,*,mode,ahead=1):
    low=lax.broadcasted_iota(jnp.int32,(1,128),1)<HEAD_DIM
    n=ROW_LEN//BQ
    for i in range(n):
        sl=slice(BQ*i,BQ*(i+1))
        t=jnp.transpose(g_ref[sl,:].astype(jnp.float32)*o_ref[sl,:].astype(jnp.float32))
        d_ref[0:1,sl]=jnp.sum(t[:64],axis=0,keepdims=True)
        d_ref[1:2,sl]=jnp.sum(t[64:],axis=0,keepdims=True)
    acc_ref[...]=jnp.zeros_like(acc_ref)
    def span(j):
        return BQ*j,min(ROW_LEN,BQ*(j+1)+SPAN)
    def masked(ref,j,h):
        t=ref[BQ*j:BQ*(j+1),:]
        return jnp.where(low==(h==0),t,jnp.zeros_like(t))
    def scores(j,h):
        q0,q1=span(j)
        places=q0+lax.broadcasted_iota(jnp.int32,(1,q1-q0),1)
        keys=BQ*j+lax.broadcasted_iota(jnp.int32,(BQ,q1-q0),0)
        allowed=(keys>=starts_of(bounds_ref,places))&(keys<=places)
        s=dot(masked(k_ref,j,h),q_ref[q0:q1,:],1,1)*SCALE2-lse_ref[0,h:h+1,q0:q1]
        return jnp.where(allowed,s,MASKED),dot(masked(v_ref,j,h),g_ref[q0:q1,:],1,1)
    items=[(j,h) for j in range(n) for h in range(2)]
    queue=[scores(*it) for it in items[:ahead]]
    dks=[];dvs=[]
    for t,(j,h) in enumerate(items):
        if t+ahead<len(items):
            queue.append(scores(*items[t+ahead]))
        s,dp=queue.pop(0)
        sl=slice(BQ*j,BQ*(j+1))
        q0,q1=span(j)
        p=jnp.exp2(s)
        ds=(p*(dp-d_ref[h:h+1,q0:q1])).astype(jnp.bfloat16)
        dvs.append(dot(p.astype(jnp.bfloat16),g_ref[q0:q1,:],1,0))
        dks.append(dot(ds,q_ref[q0:q1,:],1,0))
        if mode=="t":
            kt=jnp.transpose(k_ref[sl,:])
            acc_ref[64*h:64*h+64,q0:q1]+=dot(kt[64*h:64*h+64],ds,1,0)
        else:
            acc_ref[q0:q1,:]+=dot(ds,masked(k_ref,j,h),0,0)
        if h==1:
            dk_ref[sl,:]=(jnp.where(low,dks[0],dks[1])*HEAD_DIM**-0.5).astype(jnp.bfloat16)
            dv_ref[sl,:]=jnp.where(low,dvs[0],dvs[1]).astype(jnp.bfloat16)
            dks=[];dvs=[]
            acc=jnp.transpose(acc_ref[:,sl]) if mode=="t" else acc_ref[sl,:]
            dq_ref[sl,:]=(acc*HEAD_DIM**-0.5).astype(jnp.bfloat16)

def self_backward(bounds,q,k,v,o,g,lse,mode="t",ahead=1):
    pairs=q.shape[1]//128
    spec=pl.BlockSpec((ROW_LEN,128),lambda h:(0,h))
    sh=jax.ShapeDtypeStruct(q.shape,jnp.bfloat16)
    return pl.pallas_call(functools.partial(self_bwd_kernel,mode=mode,ahead=ahead),grid=(pairs,),
        in_specs=[pl.BlockSpec(memory_space=pltpu.SMEM)]+[spec]*5+[pl.BlockSpec((1,2,ROW_LEN),lambda h:(h,0,0))],
        out_specs=[spec]*3,
        out_shape=[sh]*3,
        scratch_shapes=[pltpu.VMEM((128,ROW_LEN) if mode=="t" else (ROW_LEN,128),jnp.float32),pltpu.VMEM((8,ROW_LEN),jnp.float32)],
        compiler_params=pltpu.CompilerParams(vmem_limit_bytes=48<<20),
        name="self_backward",
        cost_estimate=pl.CostEstimate(flops=pairs*2*18*256*256*64*10*4,bytes_accessed=pairs*8*1536*256,transcendentals=0),
    )(bounds,q,k,v,o,g,lse)

def token_range(cb_ref,tb_ref,places):
    lo=jnp.zeros_like(places); hi=jnp.full_like(places,0)+tb_ref[0]
    for c in range(3):
        past=places>=cb_ref[c]
        lo=jnp.where(past,tb_ref[c],lo)
        hi=jnp.where(past,tb_ref[c+1],hi)
    return lo,hi

def cross_fwd_kernel(cb_ref,tb_ref,q_ref,k_ref,v_ref,o_ref,lse_ref,*,ahead=2,w=512):
    low=lax.broadcasted_iota(jnp.int32,(1,128),1)<HEAD_DIM
    k=k_ref[...]
    vt=jnp.transpose(v_ref[...])
    pad=jnp.ones((16,TXT_ROW),jnp.bfloat16)
    vts=[jnp.concatenate([vt[64*h:64*h+64],pad],0) for h in range(2)]
    khs=[jnp.where(low==(h==0),k,jnp.zeros_like(k)) for h in range(2)]
    def scores(i,h):
        places=w*i+lax.broadcasted_iota(jnp.int32,(1,w),1)
        lo,hi=token_range(cb_ref,tb_ref,places)
        toks=lax.broadcasted_iota(jnp.int32,(TXT_ROW,w),0)
        return jnp.where((toks>=lo)&(toks<hi),dot(khs[h],q_ref[w*i:w*(i+1),:],1,1),MASKED)
    items=[(i,h) for i in range(ROW_LEN//w) for h in range(2)]
    queue=[scores(*it) for it in items[:ahead]]
    outs=[]
    for n,(i,h) in enumerate(items):
        if n+ahead<len(items):
            queue.append(scores(*items[n+ahead]))
        s=queue.pop(0)
        sl=slice(w*i,w*(i+1))
        m=jnp.max(s,axis=0,keepdims=True)
        p=jnp.exp2((s-m)*SCALE2)
        o=dot(vts[h],p.astype(jnp.bfloat16),1,0)
        l=o[64:65]
        outs.append(o[:64]*(1.0/l))
        lse_ref[0,h:h+1,sl]=m*SCALE2+jnp.log2(l)
        if h==1:
            o_ref[sl,:]=jnp.transpose(jnp.concatenate(outs,0)).astype(jnp.bfloat16)
            outs=[]

def cross_forward(cb,tb,q,k,v,**kw):
    pairs=q.shape[1]//128
    spec=pl.BlockSpec((ROW_LEN,128),lambda h:(0,h))
    tspec=pl.BlockSpec((TXT_ROW,128),lambda h:(0,h))
    return pl.pallas_call(functools.partial(cross_fwd_kernel,**kw),grid=(pairs,),
        in_specs=[pl.BlockSpec(memory_space=pltpu.SMEM)]*2+[spec,tspec,tspec],
        out_specs=[spec,pl.BlockSpec((1,2,ROW_LEN),lambda h:(h,0,0))],
        out_shape=[jax.ShapeDtypeStruct(q.shape,jnp.bfloat16),jax.ShapeDtypeStruct((pairs,2,ROW_LEN),jnp.float32)],
        compiler_params=pltpu.CompilerParams(vmem_limit_bytes=32<<20),
        name="cross_forward",
        cost_estimate=pl.CostEstimate(flops=pairs*2*1536*128*64*4*4,bytes_accessed=pairs*2*1536*256,transcendentals=0),
    )(cb,tb,q,k,v)

def cross_bwd_kernel(cb_ref,tb_ref,q_ref,k_ref,v_ref,o_ref,g_ref,lse_ref,dq_ref,dk_ref,dv_ref,d_ref,*,ahead=1,w=512):
    low=lax.broadcasted_iota(jnp.int32,(1,128),1)<HEAD_DIM
    k=k_ref[...]; v=v_ref[...]
    kt=jnp.transpose(k)
    khs=[jnp.where(low==(h==0),k,jnp.zeros_like(k)) for h in range(2)]
    vhs=[jnp.where(low==(h==0),v,jnp.zeros_like(v)) for h in range(2)]
    for i in range(ROW_LEN//256):
        sl=slice(256*i,256*(i+1))
        t=jnp.transpose(g_ref[sl,:].astype(jnp.float32)*o_ref[sl,:].astype(jnp.float32))
        d_ref[0:1,sl]=jnp.sum(t[:64],axis=0,keepdims=True)
        d_ref[1:2,sl]=jnp.sum(t[64:],axis=0,keepdims=True)
    dk=[jnp.zeros((TXT_ROW,128),jnp.float32)]*2
    dv=[jnp.zeros((TXT_ROW,128),jnp.float32)]*2
    def scores(i,h):
        sl=slice(w*i,w*(i+1))
        places=w*i+lax.broadcasted_iota(jnp.int32,(1,w),1)
        lo,hi=token_range(cb_ref,tb_ref,places)
        toks=lax.broadcasted_iota(jnp.int32,(TXT_ROW,w),0)
        s=dot(khs[h],q_ref[sl,:],1,1)*SCALE2-lse_ref[0,h:h+1,sl]
        return jnp.where((toks>=lo)&(toks<hi),s,MASKED),dot(vhs[h],g_ref[sl,:],1,1)
    items=[(i,h) for i in range(ROW_LEN//w) for h in range(2)]
    queue=[scores(*it) for it in items[:ahead]]
    dqs=[]
    for n,(i,h) in enumerate(items):
        if n+ahead<len(items):
            queue.append(scores(*items[n+ahead]))
        s,dp=queue.pop(0)
        sl=slice(w*i,w*(i+1))
        p=jnp.exp2(s)
        ds=(p*(dp-d_ref[h:h+1,sl])).astype(jnp.bfloat16)
        dv[h]=dv[h]+dot(p.astype(jnp.bfloat16),g_ref[sl,:],1,0)
        dk[h]=dk[h]+dot(ds,q_ref[sl,:],1,0)
        dqs.append(dot(kt[64*h:64*h+64],ds,1,0))
        if h==1:
            dq_ref[sl,:]=(jnp.transpose(jnp.concatenate(dqs,axis=0))*HEAD_DIM**-0.5).astype(jnp.bfloat16)
            dqs=[]
    dk_ref[...]=(jnp.where(low,dk[0],dk[1])*HEAD_DIM**-0.5).astype(jnp.bfloat16)
    dv_ref[...]=jnp.where(low,dv[0],dv[1]).astype(jnp.bfloat16)

def cross_backward(cb,tb,q,k,v,o,g,lse,**kw):
    pairs=q.shape[1]//128
    spec=pl.BlockSpec((ROW_LEN,128),lambda h:(0,h))
    tspec=pl.BlockSpec((TXT_ROW,128),lambda h:(0,h))
    sh=jax.ShapeDtypeStruct(q.shape,jnp.bfloat16)
    th=jax.ShapeDtypeStruct(k.shape,jnp.bfloat16)
    return pl.pallas_call(functools.partial(cross_bwd_kernel,**kw),grid=(pairs,),
        in_specs=[pl.BlockSpec(memory_space=pltpu.SMEM)]*2+[spec,tspec,tspec,spec,spec,pl.BlockSpec((1,2,ROW_LEN),lambda h:(h,0,0))],
        out_specs=[spec,tspec,tspec],
        out_shape=[sh,th,th],
        scratch_shapes=[pltpu.VMEM((8,ROW_LEN),jnp.float32)],
        compiler_params=pltpu.CompilerParams(vmem_limit_bytes=32<<20),
        name="cross_backward",
        cost_estimate=pl.CostEstimate(flops=pairs*2*1536*128*64*10*4,bytes_accessed=pairs*4*1536*256,transcendentals=0),
    )(cb,tb,q,k,v,o,g,lse)


INV_SQRT_2PI = 0.3989422804014327


def gelu_pair(hidden):
    size = jnp.abs(hidden)
    density = jnp.exp(hidden * hidden * -0.5) * INV_SQRT_2PI
    t = 1.0 / (1.0 + 0.2316419 * size)
    series = t * (
        0.319381530
        + t * (-0.356563782 + t * (1.781477937 + t * (-1.821255978 + t * 1.330274429)))
    )
    tail = density * series
    below = jnp.where(hidden >= 0, 1.0 - tail, tail)
    return (hidden * below).astype(jnp.bfloat16), (below + hidden * density).astype(jnp.bfloat16)


def row_body(dp, *args):
    (
        frames,
        text_states,
        clip_lengths,
        text_lengths,
        cotangent,
        self_gain,
        self_shift,
        self_query,
        self_key,
        self_value,
        self_out,
        cross_gain,
        cross_shift,
        cross_query,
        cross_key,
        cross_value,
        cross_out,
        text_weight,
        text_bias,
        feed_gain,
        feed_shift,
        feed_in,
        feed_out,
    ) = args
    bf16, f32 = jnp.bfloat16, jnp.float32
    me = lax.axis_index("dp")
    half = lax.axis_index("mp")
    core = me % 2
    rest = dp // 2

    swap_mp = [(0, 1), (1, 0)]
    swap_core = [(i, i ^ 1) for i in range(dp)]

    def over_y(t):
        return lax.ppermute(t, "mp", swap_mp)

    def over_core(t):
        return lax.ppermute(t, "dp", swap_core)

    bits = []
    step = 2
    while step < dp:
        bits.append(step)
        step *= 2

    def over_bit(t, step):
        return lax.ppermute(t, "dp", [(i, i ^ step) for i in range(dp)])

    def half_of(t, which, axis):
        size = t.shape[axis] // 2
        return lax.dynamic_slice_in_dim(t, which * size, size, axis)

    def ordered(first_is_mine, mine, theirs, axis):
        return jnp.concatenate(
            [jnp.where(first_is_mine, mine, theirs), jnp.where(first_is_mine, theirs, mine)], axis
        )

    def fetch(t):
        mine = over_y(half_of(t, core, 0))
        return ordered(core == 0, mine, over_core(mine), 0)

    def reduce_chunk(keeps, sends, splits):
        got = [over_core(t) for t in sends]
        sums = [(k.astype(f32) + g.astype(f32)) for k, g in zip(keeps, got)]
        owns, others = [], []
        for t, axis in zip(sums, splits):
            size = t.shape[axis] // 2
            owns.append(lax.slice_in_dim(t, 0, size, axis=axis).astype(bf16))
            others.append(lax.slice_in_dim(t, size, 2 * size, axis=axis).astype(bf16))
        other = others[0] if len(others) == 1 else jnp.concatenate(others, 0)
        own = owns[0] if len(owns) == 1 else jnp.concatenate(owns, 0)
        arrived = over_y(other)
        now, came = own, arrived
        for step in bits:
            at = (me // step) % 2
            total = lambda which: (
                half_of(now, which, 0).astype(f32) + half_of(came, which, 0).astype(f32)
            ).astype(bf16)
            keep, send = total(at), total(1 - at)
            now, came = keep, over_bit(send, step)
        block = (now.astype(f32) + came.astype(f32)).astype(bf16)
        for step in reversed(bits):
            at = (me // step) % 2
            block = ordered(at == 0, block, over_bit(block, step), 0)
        return block, over_core(block)

    def full_width(mine, theirs, axis):
        return ordered(core == 0, mine.astype(f32), theirs.astype(f32), axis)

    def reduce_small(t):
        t = t + over_core(t)
        t = t + over_y(t)
        for step in bits:
            t = t + over_bit(t, step)
        return t

    def wide_halves(t):
        return half_of(t, core, 1), half_of(t, 1 - core, 1)

    lengths = lax.dynamic_index_in_dim(clip_lengths, half, 0, keepdims=False)
    words = lax.dynamic_index_in_dim(text_lengths, half, 0, keepdims=False)
    clip_bounds, text_bounds = jnp.cumsum(lengths), jnp.cumsum(words)
    text = lax.dynamic_slice_in_dim(text_states, half * TXT_ROW, TXT_ROW, 0)

    matrices = dict(
        self_query=self_query,
        self_key=self_key,
        self_value=self_value,
        self_out=self_out,
        text_weight=text_weight,
        cross_key=cross_key,
        cross_value=cross_value,
        cross_query=cross_query,
        cross_out=cross_out,
        feed_in=feed_in,
        feed_out=feed_out,
    )
    other = {name: fetch(t) for name, t in matrices.items()}
    pairs = {name: (matrices[name], other[name]) for name in matrices}

    residual = frames.astype(f32)
    self_standard, self_inverse = norm_parts(residual)
    self_rows = (self_standard * self_gain + self_shift).astype(bf16)
    self_q = [product(self_rows, w).astype(bf16) for w in pairs["self_query"]]
    self_k = [product(self_rows, w).astype(bf16) for w in pairs["self_key"]]
    self_v = [product(self_rows, w).astype(bf16) for w in pairs["self_value"]]
    self_ctx, self_log = zip(
        *[row_self_forward(clip_bounds, *qkv) for qkv in zip(self_q, self_k, self_v)]
    )
    middle = residual + sum(product(c, w) for c, w in zip(self_ctx, pairs["self_out"]))

    bias_other = over_y(text_bias)
    text_full = ordered(
        half == 0,
        (product(text, text_weight) + text_bias).astype(bf16),
        (product(text, other["text_weight"]) + bias_other).astype(bf16),
        1,
    )
    cross_standard, cross_inverse = norm_parts(middle)
    cross_rows = (cross_standard * cross_gain + cross_shift).astype(bf16)
    cross_q = [product(cross_rows, w).astype(bf16) for w in pairs["cross_query"]]
    cross_k = [product(text_full, w).astype(bf16) for w in pairs["cross_key"]]
    cross_v = [product(text_full, w).astype(bf16) for w in pairs["cross_value"]]
    cross_ctx, cross_log = zip(
        *[
            cross_forward(clip_bounds, text_bounds, *qkv)
            for qkv in zip(cross_q, cross_k, cross_v)
        ]
    )
    after = middle + sum(product(c, w) for c, w in zip(cross_ctx, pairs["cross_out"]))

    feed_standard, feed_inverse = norm_parts(after)
    feed_rows = (feed_standard * feed_gain + feed_shift).astype(bf16)
    active, slope = zip(*[gelu_pair(product(feed_rows, w)) for w in pairs["feed_in"]])
    output = after + sum(product(a, w) for a, w in zip(active, pairs["feed_out"]))
    grad_output = cotangent.astype(f32)
    grad_hidden = [
        (against(cotangent, w) * s.astype(f32)).astype(bf16)
        for w, s in zip(pairs["feed_out"], slope)
    ]
    active_all = jnp.concatenate(active, 1)
    hidden_all = jnp.concatenate(grad_hidden, 1)
    out_keep, out_send = [
        outer_sum(active_all, t).astype(bf16) for t in wide_halves(cotangent)
    ]
    in_keep, in_send = [outer_sum(t, hidden_all).astype(bf16) for t in wide_halves(feed_rows)]
    grad_hidden, out_keep, out_send, in_keep, in_send = lax.optimization_barrier(
        (grad_hidden, out_keep, out_send, in_keep, in_send)
    )
    feed_out_sum = reduce_chunk([out_keep], [out_send], [0])
    feed_in_sum = reduce_chunk([in_keep], [in_send], [1])
    grad_normed = sum(against(g, w) for g, w in zip(grad_hidden, pairs["feed_in"]))
    grad_norm, feed_gain_grad, feed_shift_grad = norm_back(
        grad_normed, feed_standard, feed_inverse, feed_gain
    )
    grad_after = grad_output + grad_norm

    grad_c = grad_after.astype(bf16)
    grad_ctx = [against(grad_c, w).astype(bf16) for w in pairs["cross_out"]]
    grad_q, grad_k, grad_v = zip(
        *[
            cross_backward(clip_bounds, text_bounds, *parts)
            for parts in zip(cross_q, cross_k, cross_v, cross_ctx, grad_ctx, cross_log)
        ]
    )
    grad_text_full = sum(
        against(g, w)
        for g, w in zip(grad_k + grad_v, pairs["cross_key"] + pairs["cross_value"])
    ).astype(bf16)
    text_grad_row = against(
        lax.dynamic_slice_in_dim(grad_text_full, half * 512, 512, 1), text_weight
    ) + against(
        lax.dynamic_slice_in_dim(grad_text_full, (1 - half) * 512, 512, 1), other["text_weight"]
    )
    text_grad_row = text_grad_row.astype(bf16)
    text_grad = ordered(half == 0, text_grad_row, over_y(text_grad_row), 0).astype(f32)
    grad_text_mine = jnp.concatenate(
        [half_of(grad_text_full, half, 1), half_of(grad_text_full, 1 - half, 1)], 1
    )
    ctx_all = jnp.concatenate(cross_ctx, 1)
    chunk = []
    for which in range(2):
        chunk.append(
            [
                outer_sum(wide_halves(cross_rows)[which], jnp.concatenate(grad_q, 1)).astype(bf16),
                outer_sum(wide_halves(text_full)[which], jnp.concatenate(grad_k, 1)).astype(bf16),
                outer_sum(wide_halves(text_full)[which], jnp.concatenate(grad_v, 1)).astype(bf16),
                outer_sum(ctx_all, wide_halves(grad_c)[which]).astype(bf16),
                outer_sum(wide_halves(text)[which], grad_text_mine).astype(bf16),
            ]
        )
    grad_q, chunk = lax.optimization_barrier((grad_q, chunk))
    cross_sum = reduce_chunk(chunk[0], chunk[1], [1, 1, 1, 0, 1])
    grad_normed = sum(against(g, w) for g, w in zip(grad_q, pairs["cross_query"]))
    grad_norm, cross_gain_grad, cross_shift_grad = norm_back(
        grad_normed, cross_standard, cross_inverse, cross_gain
    )
    grad_middle = grad_after + grad_norm
    early = reduce_small(
        jnp.stack(
            [
                feed_gain_grad,
                feed_shift_grad,
                cross_gain_grad,
                cross_shift_grad,
                jnp.sum(grad_text_full.astype(f32), axis=0),
            ]
        )
    )

    grad_s = grad_middle.astype(bf16)
    grad_ctx = [against(grad_s, w).astype(bf16) for w in pairs["self_out"]]
    ctx_all = jnp.concatenate(self_ctx, 1)
    so_keep, so_send = [outer_sum(ctx_all, t).astype(bf16) for t in wide_halves(grad_s)]
    grad_ctx, so_keep, so_send = lax.optimization_barrier((grad_ctx, so_keep, so_send))
    self_out_sum = reduce_chunk([so_keep], [so_send], [0])
    grad_q, grad_k, grad_v = zip(
        *[
            self_backward(clip_bounds, *parts)
            for parts in zip(self_q, self_k, self_v, self_ctx, grad_ctx, self_log)
        ]
    )
    chunk = []
    for which in range(2):
        rows = wide_halves(self_rows)[which]
        chunk.append(
            [
                outer_sum(rows, jnp.concatenate(g, 1)).astype(bf16)
                for g in (grad_q, grad_k, grad_v)
            ]
        )
    self_sum = reduce_chunk(chunk[0], chunk[1], [1, 1, 1])
    grad_normed = sum(
        against(g, w)
        for g, w in zip(
            grad_q + grad_k + grad_v,
            pairs["self_query"] + pairs["self_key"] + pairs["self_value"],
        )
    )
    grad_norm, self_gain_grad, self_shift_grad = norm_back(
        grad_normed, self_standard, self_inverse, self_gain
    )
    frames_grad = grad_middle + grad_norm
    late = reduce_small(jnp.stack([self_gain_grad, self_shift_grad]))

    def part(pair, at, rows, axis):
        return full_width(pair[0][at : at + rows], pair[1][at : at + rows], axis)

    return (
        output.astype(bf16),
        frames_grad,
        text_grad,
        late[0],
        late[1],
        part(self_sum, 0, 512, 0),
        part(self_sum, 512, 512, 0),
        part(self_sum, 1024, 512, 0),
        part(self_out_sum, 0, 512, 1),
        early[2],
        early[3],
        part(cross_sum, 0, 512, 0),
        part(cross_sum, 512, 512, 0),
        part(cross_sum, 1024, 512, 0),
        part(cross_sum, 1536, 512, 1),
        part(cross_sum, 2048, 384, 0),
        lax.dynamic_slice_in_dim(early[4], half * 512, 512, 0),
        early[0],
        early[1],
        part(feed_in_sum, 0, 512, 0),
        part(feed_out_sum, 0, 2048, 1),
    )


def chosen(dp, mp, *args):
    rows_here, frames_here = args[2].shape[0], args[0].shape[0]
    if mp == 2 and dp == 16 and rows_here == mp and frames_here == ROW_LEN:
        return row_body(dp, *args)
    return body(*args)


def solution(mesh):
    return jax.shard_map(
        functools.partial(chosen, mesh.shape["dp"], mesh.shape["mp"]),
        mesh=mesh,
        in_specs=(
            P(("dp", "mp"), None),
            P("dp", None),
            P("dp", None),
            P("dp", None),
            P(("dp", "mp"), None),
            P(),
            P(),
            P(None, "mp"),
            P(None, "mp"),
            P(None, "mp"),
            P("mp", None),
            P(),
            P(),
            P(None, "mp"),
            P(None, "mp"),
            P(None, "mp"),
            P("mp", None),
            P(None, "mp"),
            P("mp"),
            P(),
            P(),
            P(None, "mp"),
            P("mp", None),
        ),
        out_specs=(
            P(("dp", "mp"), None),
            P(("dp", "mp"), None),
            P("dp", None),
            P(),
            P(),
            P(None, "mp"),
            P(None, "mp"),
            P(None, "mp"),
            P("mp", None),
            P(),
            P(),
            P(None, "mp"),
            P(None, "mp"),
            P(None, "mp"),
            P("mp", None),
            P(None, "mp"),
            P("mp"),
            P(),
            P(),
            P(None, "mp"),
            P("mp", None),
        ),
        check_vma=False,
    )
```

```python
import functools
from functools import reduce

import jax
import jax.numpy as jnp
from jax import lax
from jax.experimental import pallas as pl
from jax.experimental.pallas import tpu as pltpu
from jax.sharding import PartitionSpec as P

HEAD_DIM = 64
ROW_LEN = 1536
TXT_ROW = 128


EPSILON = 1e-05
MASKED = -1e30


def product(left_side, right_side):
    return jnp.dot(left_side, right_side, preferred_element_type=jnp.float32)


def against(left_side, right_side):
    return lax.dot_general(
        left_side, right_side, (((1,), (1,)), ((), ())), preferred_element_type=jnp.float32
    )


def outer_sum(left_side, right_side):
    return lax.dot_general(
        left_side, right_side, (((0,), (0,)), ((), ())), preferred_element_type=jnp.float32
    )


def exact_gelu(tensor):
    return jax.nn.gelu(tensor, approximate=False)


def segment_ids(lengths, positions):
    bounds = jnp.cumsum(lengths, axis=-1)
    places = jnp.arange(positions, dtype=jnp.int32)
    return jnp.sum((places[None, :, None] >= bounds[:, None, :]).astype(jnp.int32), axis=-1)


def split_heads(tensor, row_count):
    return tensor.reshape(
        row_count, tensor.shape[0] // row_count, tensor.shape[1] // HEAD_DIM, HEAD_DIM
    )


def norm_parts(tensor):
    average = jnp.mean(tensor, axis=-1, keepdims=True)
    centered = tensor - average
    inverse = lax.rsqrt(jnp.mean(centered * centered, axis=-1, keepdims=True) + EPSILON)
    return (centered * inverse, inverse)


def norm_back(gradient, standard, inverse, norm_gain):
    scaled = gradient * norm_gain
    first_mean = jnp.mean(scaled, axis=-1, keepdims=True)
    second_mean = jnp.mean(scaled * standard, axis=-1, keepdims=True)
    return (
        inverse * (scaled - first_mean - standard * second_mean),
        jnp.sum(gradient * standard, axis=0),
        jnp.sum(gradient, axis=0),
    )


def spread_rows(tensor):
    return lax.all_gather(tensor, "mp", axis=0, tiled=True)


def spread_cotangent(tensor):
    return lax.all_gather(tensor, "mp", axis=0, tiled=True)


def branch_sum(left_side, right_side):
    return lax.psum_scatter(product(left_side, right_side), "mp", scatter_dimension=0, tiled=True)


def input_grads(factor_pairs):
    partials = [against(left_side, right_side) for left_side, right_side in factor_pairs]
    return lax.psum_scatter(reduce(jnp.add, partials), "mp", scatter_dimension=0, tiled=True)


def attend_forward(queries, key_heads, values, allowed):
    scores = jnp.einsum(
        "rqhd,rkhd->rhqk", queries, key_heads, preferred_element_type=jnp.float32
    ) * HEAD_DIM ** (-0.5)
    scores = jnp.where(allowed[:, None], scores, MASKED)
    row_max = jnp.max(scores, axis=-1, keepdims=True)
    shifted = jnp.exp(scores - row_max)
    totals = jnp.sum(shifted, axis=-1, keepdims=True)
    soft_weights = (shifted / totals).astype(jnp.bfloat16)
    context = jnp.einsum(
        "rhqk,rkhd->rqhd", soft_weights, values, preferred_element_type=jnp.float32
    )
    return (context, row_max + jnp.log(totals))


def attend_back(queries, key_heads, values, allowed, log_totals, grad_context):
    score_scale = HEAD_DIM ** (-0.5)
    scores = (
        jnp.einsum("rqhd,rkhd->rhqk", queries, key_heads, preferred_element_type=jnp.float32)
        * score_scale
    )
    scores = jnp.where(allowed[:, None], scores, MASKED)
    soft_weights = jnp.exp(scores - log_totals)
    grad_soft = jnp.einsum(
        "rqhd,rkhd->rhqk", grad_context, values, preferred_element_type=jnp.float32
    )
    row_inner = jnp.sum(grad_soft * soft_weights, axis=-1, keepdims=True)
    grad_scores = (soft_weights * (grad_soft - row_inner)).astype(jnp.bfloat16)
    grad_query = (
        jnp.einsum("rhqk,rkhd->rqhd", grad_scores, key_heads, preferred_element_type=jnp.float32)
        * score_scale
    )
    grad_keys = (
        jnp.einsum("rhqk,rqhd->rkhd", grad_scores, queries, preferred_element_type=jnp.float32)
        * score_scale
    )
    grad_values = jnp.einsum(
        "rhqk,rqhd->rkhd",
        soft_weights.astype(jnp.bfloat16),
        grad_context,
        preferred_element_type=jnp.float32,
    )
    return (grad_query, grad_keys, grad_values)


def self_allowed(segments, start_at, stop_at):
    places = jnp.arange(stop_at, dtype=jnp.int32)
    same_clip = segments[:, start_at:stop_at, None] == segments[:, None, :stop_at]
    return same_clip & (places[start_at:stop_at, None] >= places[None, :])[None]


def self_forward(queries, key_heads, values, segments):
    block_size = min(512, queries.shape[1])
    contexts = []
    log_totals = []
    for start_at in range(0, queries.shape[1], block_size):
        stop_at = start_at + block_size
        context, log_total = attend_forward(
            queries[:, start_at:stop_at],
            key_heads[:, :stop_at],
            values[:, :stop_at],
            self_allowed(segments, start_at, stop_at),
        )
        contexts.append(context)
        log_totals.append(log_total)
    return (jnp.concatenate(contexts, axis=1), jnp.concatenate(log_totals, axis=2))


def self_back(queries, key_heads, values, segments, log_totals, grad_context):
    block_size = min(512, queries.shape[1])
    query_parts = []
    grad_keys = jnp.zeros(key_heads.shape, jnp.float32)
    grad_values = jnp.zeros(values.shape, jnp.float32)
    for start_at in range(0, queries.shape[1], block_size):
        stop_at = start_at + block_size
        grad_query, key_part, value_part = attend_back(
            queries[:, start_at:stop_at],
            key_heads[:, :stop_at],
            values[:, :stop_at],
            self_allowed(segments, start_at, stop_at),
            log_totals[:, :, start_at:stop_at],
            grad_context[:, start_at:stop_at],
        )
        query_parts.append(grad_query)
        grad_keys = grad_keys.at[:, :stop_at].add(key_part)
        grad_values = grad_values.at[:, :stop_at].add(value_part)
    return (jnp.concatenate(query_parts, axis=1), grad_keys, grad_values)


def body(
    frames,
    text_states,
    clip_lengths,
    text_lengths,
    cotangent,
    self_gain,
    self_shift,
    self_query,
    self_key,
    self_value,
    self_out,
    cross_gain,
    cross_shift,
    cross_query,
    cross_key,
    cross_value,
    cross_out,
    text_weight,
    text_bias,
    feed_gain,
    feed_shift,
    feed_in,
    feed_out,
):
    row_count = clip_lengths.shape[0]
    clip_segs = segment_ids(clip_lengths, ROW_LEN)
    text_segs = segment_ids(text_lengths, TXT_ROW)
    residual = frames.astype(jnp.float32)
    self_standard, self_inverse = norm_parts(residual)
    self_rows = spread_rows((self_standard * self_gain + self_shift).astype(jnp.bfloat16))
    self_queries = product(self_rows, self_query).astype(jnp.bfloat16)
    self_keys = product(self_rows, self_key).astype(jnp.bfloat16)
    self_values = product(self_rows, self_value).astype(jnp.bfloat16)
    self_context, self_logs = self_forward(
        split_heads(self_queries, row_count),
        split_heads(self_keys, row_count),
        split_heads(self_values, row_count),
        clip_segs,
    )
    self_context = self_context.reshape(self_queries.shape).astype(jnp.bfloat16)
    middle = residual + branch_sum(self_context, self_out)
    cross_standard, cross_inverse = norm_parts(middle)
    cross_rows = spread_rows((cross_standard * cross_gain + cross_shift).astype(jnp.bfloat16))
    text_part = (product(text_states, text_weight) + text_bias).astype(jnp.bfloat16)
    text_full = lax.all_gather(text_part, "mp", axis=1, tiled=True)
    cross_queries = product(cross_rows, cross_query).astype(jnp.bfloat16)
    cross_keys = product(text_full, cross_key).astype(jnp.bfloat16)
    cross_values = product(text_full, cross_value).astype(jnp.bfloat16)
    cross_allowed = clip_segs[:, :, None] == text_segs[:, None, :]
    cross_context, cross_logs = attend_forward(
        split_heads(cross_queries, row_count),
        split_heads(cross_keys, row_count),
        split_heads(cross_values, row_count),
        cross_allowed,
    )
    cross_context = cross_context.reshape(cross_queries.shape).astype(jnp.bfloat16)
    after_cross = middle + branch_sum(cross_context, cross_out)
    feed_standard, feed_inverse = norm_parts(after_cross)
    feed_normed = (feed_standard * feed_gain + feed_shift).astype(jnp.bfloat16)
    feed_rows = spread_rows(feed_normed)
    hidden = product(feed_rows, feed_in)
    active, gelu_back = jax.vjp(exact_gelu, hidden)
    active = active.astype(jnp.bfloat16)
    output = after_cross + branch_sum(active, feed_out)
    grad_output = cotangent.astype(jnp.float32)
    feed_cotangent = grad_output.astype(jnp.bfloat16)
    grad_rows = spread_cotangent(feed_cotangent)
    feed_out_grad = outer_sum(active, grad_rows)
    grad_hidden = gelu_back(against(grad_rows, feed_out))[0].astype(jnp.bfloat16)
    feed_in_grad = outer_sum(feed_rows, grad_hidden)
    grad_feed_normed = input_grads(((grad_hidden, feed_in),))
    grad_norm, feed_gain_grad, feed_shift_grad = norm_back(
        grad_feed_normed, feed_standard, feed_inverse, feed_gain
    )
    grad_after = grad_output + grad_norm
    cross_cotangent = spread_cotangent(grad_after.astype(jnp.bfloat16))
    cross_out_grad = outer_sum(cross_context, cross_cotangent)
    grad_context = against(cross_cotangent, cross_out).astype(jnp.bfloat16)
    grad_queries, grad_keys, grad_values = attend_back(
        split_heads(cross_queries, row_count),
        split_heads(cross_keys, row_count),
        split_heads(cross_values, row_count),
        cross_allowed,
        cross_logs,
        split_heads(grad_context, row_count),
    )
    grad_queries = grad_queries.reshape(cross_queries.shape).astype(jnp.bfloat16)
    grad_keys = grad_keys.reshape(cross_keys.shape).astype(jnp.bfloat16)
    grad_values = grad_values.reshape(cross_values.shape).astype(jnp.bfloat16)
    cross_query_grad = outer_sum(cross_rows, grad_queries)
    cross_key_grad = outer_sum(text_full, grad_keys)
    cross_value_grad = outer_sum(text_full, grad_values)
    grad_text_full = against(grad_keys, cross_key) + against(grad_values, cross_value)
    grad_text = lax.psum_scatter(
        grad_text_full.astype(jnp.bfloat16), "mp", scatter_dimension=1, tiled=True
    )
    text_weight_grad = outer_sum(text_states, grad_text)
    text_bias_grad = jnp.sum(grad_text.astype(jnp.float32), axis=0)
    text_grad = lax.psum(against(grad_text, text_weight).astype(jnp.bfloat16), "mp").astype(
        jnp.float32
    )
    grad_cross_normed = input_grads(((grad_queries, cross_query),))
    grad_norm, cross_gain_grad, cross_shift_grad = norm_back(
        grad_cross_normed, cross_standard, cross_inverse, cross_gain
    )
    grad_middle = grad_after + grad_norm
    self_cotangent = spread_cotangent(grad_middle.astype(jnp.bfloat16))
    self_out_grad = outer_sum(self_context, self_cotangent)
    grad_context = against(self_cotangent, self_out).astype(jnp.bfloat16)
    grad_queries, grad_keys, grad_values = self_back(
        split_heads(self_queries, row_count),
        split_heads(self_keys, row_count),
        split_heads(self_values, row_count),
        clip_segs,
        self_logs,
        split_heads(grad_context, row_count),
    )
    grad_queries = grad_queries.reshape(self_queries.shape).astype(jnp.bfloat16)
    grad_keys = grad_keys.reshape(self_keys.shape).astype(jnp.bfloat16)
    grad_values = grad_values.reshape(self_values.shape).astype(jnp.bfloat16)
    self_query_grad = outer_sum(self_rows, grad_queries)
    self_key_grad = outer_sum(self_rows, grad_keys)
    self_value_grad = outer_sum(self_rows, grad_values)
    grad_self_normed = input_grads(
        ((grad_queries, self_query), (grad_keys, self_key), (grad_values, self_value))
    )
    grad_norm, self_gain_grad, self_shift_grad = norm_back(
        grad_self_normed, self_standard, self_inverse, self_gain
    )
    frames_grad = grad_middle + grad_norm
    (
        self_query_grad,
        self_key_grad,
        self_value_grad,
        self_out_grad,
        cross_query_grad,
        cross_key_grad,
        cross_value_grad,
        cross_out_grad,
        text_weight_grad,
        text_bias_grad,
        feed_in_grad,
        feed_out_grad,
    ) = (
        lax.psum(self_query_grad.astype(jnp.bfloat16), "dp").astype(jnp.float32),
        lax.psum(self_key_grad.astype(jnp.bfloat16), "dp").astype(jnp.float32),
        lax.psum(self_value_grad.astype(jnp.bfloat16), "dp").astype(jnp.float32),
        lax.psum(self_out_grad.astype(jnp.bfloat16), "dp").astype(jnp.float32),
        lax.psum(cross_query_grad.astype(jnp.bfloat16), "dp").astype(jnp.float32),
        lax.psum(cross_key_grad.astype(jnp.bfloat16), "dp").astype(jnp.float32),
        lax.psum(cross_value_grad.astype(jnp.bfloat16), "dp").astype(jnp.float32),
        lax.psum(cross_out_grad.astype(jnp.bfloat16), "dp").astype(jnp.float32),
        lax.psum(text_weight_grad.astype(jnp.bfloat16), "dp").astype(jnp.float32),
        lax.psum(text_bias_grad.astype(jnp.bfloat16), "dp").astype(jnp.float32),
        lax.psum(feed_in_grad.astype(jnp.bfloat16), "dp").astype(jnp.float32),
        lax.psum(feed_out_grad.astype(jnp.bfloat16), "dp").astype(jnp.float32),
    )
    (
        self_gain_grad,
        self_shift_grad,
        cross_gain_grad,
        cross_shift_grad,
        feed_gain_grad,
        feed_shift_grad,
    ) = lax.psum(
        (
            self_gain_grad,
            self_shift_grad,
            cross_gain_grad,
            cross_shift_grad,
            feed_gain_grad,
            feed_shift_grad,
        ),
        ("dp", "mp"),
    )
    return (
        output.astype(jnp.bfloat16),
        frames_grad,
        text_grad,
        self_gain_grad,
        self_shift_grad,
        self_query_grad,
        self_key_grad,
        self_value_grad,
        self_out_grad,
        cross_gain_grad,
        cross_shift_grad,
        cross_query_grad,
        cross_key_grad,
        cross_value_grad,
        cross_out_grad,
        text_weight_grad,
        text_bias_grad,
        feed_gain_grad,
        feed_shift_grad,
        feed_in_grad,
        feed_out_grad,
    )


LOG2E=1.4426950408889634
SCALE2=LOG2E*HEAD_DIM**-0.5
BQ=256
SPAN=768

def dot(a,b,ca,cb):
    return lax.dot_general(a,b,(((ca,),(cb,)),((),())),preferred_element_type=jnp.float32)

def starts_of(bounds_ref, places):
    start=jnp.zeros_like(places)
    for k in range(3):
        start=jnp.where(places>=bounds_ref[k],bounds_ref[k],start)
    return start

def self_fwd_kernel(bounds_ref,q_ref,k_ref,v_ref,o_ref,lse_ref,*,ahead=2):
    low=lax.broadcasted_iota(jnp.int32,(1,128),1)<HEAD_DIM
    vt=jnp.transpose(v_ref[...])
    pad=jnp.ones((16,ROW_LEN),jnp.bfloat16)
    vts=[jnp.concatenate([vt[64*h:64*h+64],pad],0) for h in range(2)]
    def span(i):
        return max(0,BQ*i-SPAN),BQ*(i+1)
    def scores(i,h):
        k0,k1=span(i)
        q=q_ref[BQ*i:k1,:]
        qh=jnp.where(low==(h==0),q,jnp.zeros_like(q))
        places=BQ*i+lax.broadcasted_iota(jnp.int32,(1,BQ),1)
        keys=k0+lax.broadcasted_iota(jnp.int32,(k1-k0,BQ),0)
        allowed=(keys>=starts_of(bounds_ref,places))&(keys<=places)
        return jnp.where(allowed,dot(k_ref[k0:k1,:],qh,1,1),MASKED)
    items=[(i,h) for i in range(ROW_LEN//BQ) for h in range(2)]
    queue=[scores(*it) for it in items[:ahead]]
    outs=[]
    for n,(i,h) in enumerate(items):
        if n+ahead<len(items):
            queue.append(scores(*items[n+ahead]))
        s=queue.pop(0)
        k0,k1=span(i)
        m=jnp.max(s,axis=0,keepdims=True)
        p=jnp.exp2((s-m)*SCALE2)
        o=dot(vts[h][:,k0:k1],p.astype(jnp.bfloat16),1,0)
        l=o[64:65]
        outs.append(o[:64]*(1.0/l))
        lse_ref[0,h:h+1,BQ*i:k1]=m*SCALE2+jnp.log2(l)
        if h==1:
            o_ref[BQ*i:k1,:]=jnp.transpose(jnp.concatenate(outs,0)).astype(jnp.bfloat16)
            outs=[]

def self_bwd_kernel(bounds_ref,q_ref,k_ref,v_ref,o_ref,g_ref,lse_ref,out_ref,acc_ref,d_ref,*,mode="t",ahead=1):
    low=lax.broadcasted_iota(jnp.int32,(1,128),1)<HEAD_DIM
    n=ROW_LEN//BQ
    pair=pl.program_id(0)
    width=128*pl.num_programs(0)
    def put(which,sl,t):
        at=pl.multiple_of(which*width+pair*128,128)
        out_ref[sl,pl.ds(at,128)]=t.astype(jnp.bfloat16)

    for i in range(n):
        sl=slice(BQ*i,BQ*(i+1))
        t=jnp.transpose(g_ref[sl,:].astype(jnp.float32)*o_ref[sl,:].astype(jnp.float32))
        d_ref[0:1,sl]=jnp.sum(t[:64],axis=0,keepdims=True)
        d_ref[1:2,sl]=jnp.sum(t[64:],axis=0,keepdims=True)
    acc_ref[...]=jnp.zeros_like(acc_ref)
    def span(j):
        return BQ*j,min(ROW_LEN,BQ*(j+1)+SPAN)
    def masked(ref,j,h):
        t=ref[BQ*j:BQ*(j+1),:]
        return jnp.where(low==(h==0),t,jnp.zeros_like(t))
    def scores(j,h):
        q0,q1=span(j)
        places=q0+lax.broadcasted_iota(jnp.int32,(1,q1-q0),1)
        keys=BQ*j+lax.broadcasted_iota(jnp.int32,(BQ,q1-q0),0)
        allowed=(keys>=starts_of(bounds_ref,places))&(keys<=places)
        s=dot(masked(k_ref,j,h),q_ref[q0:q1,:],1,1)*SCALE2-lse_ref[0,h:h+1,q0:q1]
        return jnp.where(allowed,s,MASKED),dot(masked(v_ref,j,h),g_ref[q0:q1,:],1,1)
    items=[(j,h) for j in range(n) for h in range(2)]
    queue=[scores(*it) for it in items[:ahead]]
    dks=[];dvs=[]
    for t,(j,h) in enumerate(items):
        if t+ahead<len(items):
            queue.append(scores(*items[t+ahead]))
        s,dp=queue.pop(0)
        sl=slice(BQ*j,BQ*(j+1))
        q0,q1=span(j)
        p=jnp.exp2(s)
        ds=(p*(dp-d_ref[h:h+1,q0:q1])).astype(jnp.bfloat16)
        dvs.append(dot(p.astype(jnp.bfloat16),g_ref[q0:q1,:],1,0))
        dks.append(dot(ds,q_ref[q0:q1,:],1,0))
        if mode=="t":
            kt=jnp.transpose(k_ref[sl,:])
            acc_ref[64*h:64*h+64,q0:q1]+=dot(kt[64*h:64*h+64],ds,1,0)
        else:
            acc_ref[q0:q1,:]+=dot(ds,masked(k_ref,j,h),0,0)
        if h==1:
            put(1,sl,jnp.where(low,dks[0],dks[1])*HEAD_DIM**-0.5)
            put(2,sl,jnp.where(low,dvs[0],dvs[1]))
            dks=[];dvs=[]
            acc=jnp.transpose(acc_ref[:,sl]) if mode=="t" else acc_ref[sl,:]
            put(0,sl,acc*HEAD_DIM**-0.5)


def group_forward(bounds,qkv):
    width=qkv.shape[1]//3
    pairs=width//128
    spec=lambda t: pl.BlockSpec((ROW_LEN,128),lambda h:(0,t*pairs+h))
    return pl.pallas_call(self_fwd_kernel,grid=(pairs,),
        in_specs=[pl.BlockSpec(memory_space=pltpu.SMEM),spec(0),spec(1),spec(2)],
        out_specs=[spec(0),pl.BlockSpec((1,2,ROW_LEN),lambda h:(h,0,0))],
        out_shape=[jax.ShapeDtypeStruct((ROW_LEN,width),jnp.bfloat16),jax.ShapeDtypeStruct((pairs,2,ROW_LEN),jnp.float32)],
        compiler_params=pltpu.CompilerParams(vmem_limit_bytes=40<<20),
        name="self_forward",
        cost_estimate=pl.CostEstimate(flops=pairs*2*18*256*256*64*4*4,bytes_accessed=pairs*4*1536*256,transcendentals=0),
    )(bounds,qkv,qkv,qkv)

def group_backward(bounds,qkv,o,g,lse,group):
    width=qkv.shape[1]//3
    pairs=width//128
    spec=lambda t: pl.BlockSpec((ROW_LEN,128),lambda h:(0,t*pairs+h))
    return pl.pallas_call(self_bwd_kernel,grid=(pairs,),
        in_specs=[pl.BlockSpec(memory_space=pltpu.SMEM),spec(0),spec(1),spec(2),spec(0),spec(group),pl.BlockSpec((1,2,ROW_LEN),lambda h:(h,0,0))],
        out_specs=pl.BlockSpec((ROW_LEN,3*width),lambda h:(0,0)),
        out_shape=jax.ShapeDtypeStruct(qkv.shape,jnp.bfloat16),
        scratch_shapes=[pltpu.VMEM((128,ROW_LEN),jnp.float32),pltpu.VMEM((8,ROW_LEN),jnp.float32)],
        compiler_params=pltpu.CompilerParams(vmem_limit_bytes=48<<20),
        name="self_backward",
        cost_estimate=pl.CostEstimate(flops=pairs*2*18*256*256*64*10*4,bytes_accessed=pairs*8*1536*256,transcendentals=0),
    )(bounds,qkv,qkv,qkv,o,g,lse)

def token_range(cb_ref,tb_ref,places):
    lo=jnp.zeros_like(places); hi=jnp.full_like(places,0)+tb_ref[0]
    for c in range(3):
        past=places>=cb_ref[c]
        lo=jnp.where(past,tb_ref[c],lo)
        hi=jnp.where(past,tb_ref[c+1],hi)
    return lo,hi


INV_SQRT_2PI = 0.3989422804014327
TB = 256
NB = 512


def mean_row(t):
    return jnp.sum(t, axis=-1, keepdims=True) * (1.0 / t.shape[-1])


def standardise(t):
    centered = t - mean_row(t)
    inverse = lax.rsqrt(mean_row(centered * centered) + EPSILON)
    return centered * inverse, inverse


def norm_input_grad(e, standard, inverse, gain):
    scaled = e * gain
    return inverse * (scaled - mean_row(scaled) - standard * mean_row(scaled * standard))


def column_sums(t):
    return jnp.sum(t, axis=0, keepdims=True)


def gelu_pair(hidden):
    density = jnp.exp2(hidden * hidden * (-0.5 * LOG2E)) * INV_SQRT_2PI
    t = 1.0 / (1.0 + 0.2316419 * jnp.abs(hidden))
    series = t * (
        0.319381530
        + t * (-0.356563782 + t * (1.781477937 + t * (-1.821255978 + t * 1.330274429)))
    )
    tail = density * series
    below = jnp.where(hidden >= 0, 1.0 - tail, tail)
    return hidden * below, below + hidden * density


def mid_forward_kernel(
    count, cb_ref, tb_ref, x_ref, *refs,
):
    ctxs, sos, cqs, cos = [refs[count * t : count * t + count] for t in range(4)]
    (k_ref, v_ref, vec_ref,
     mid_ref, rows_ref, q_ref, cctx_ref, lse_ref, after_ref, feed_ref, feedt_ref, vt_ref) = refs[4 * count :]
    i = pl.program_id(0)
    low = lax.broadcasted_iota(jnp.int32, (1, 128), 1) < HEAD_DIM

    @pl.when(i == 0)
    def _():
        vt_ref[0:1024, :] = jnp.transpose(v_ref[...])
        vt_ref[1024:1040, :] = jnp.ones((16, TXT_ROW), jnp.bfloat16)

    middle = x_ref[...].astype(jnp.float32)
    for c, w in zip(ctxs, sos):
        middle = middle + dot(c[...], w[...], 1, 0)
    mid_ref[...] = middle
    u, _ = standardise(middle)
    rows = (u * vec_ref[0:1, :] + vec_ref[1:2, :]).astype(jnp.bfloat16)
    rows_ref[...] = rows
    at = 0
    for w in cqs:
        n = w.shape[1]
        q_ref[:, at : at + n] = dot(rows, w[...], 1, 0).astype(jnp.bfloat16)
        at += n
    places = TB * i + lax.broadcasted_iota(jnp.int32, (1, TB), 1)
    lo, hi = token_range(cb_ref, tb_ref, places)
    toks = lax.broadcasted_iota(jnp.int32, (TXT_ROW, TB), 0)
    allowed = (toks >= lo) & (toks < hi)

    def scores(head):
        p, h = head // 2, head % 2
        k = k_ref[:, 128 * p : 128 * p + 128]
        kh = jnp.where(low == (h == 0), k, jnp.zeros_like(k))
        return jnp.where(allowed, dot(kh, q_ref[:, 128 * p : 128 * p + 128], 1, 1), MASKED)

    ahead = 3
    queue = [scores(t) for t in range(ahead)]
    outs = []
    ones = vt_ref[1024:1040, :]
    for head in range(16):
        if head + ahead < 16:
            queue.append(scores(head + ahead))
        s = queue.pop(0)
        m = jnp.max(s, axis=0, keepdims=True)
        p = jnp.exp2((s - m) * SCALE2)
        vt = jnp.concatenate([vt_ref[64 * head : 64 * head + 64, :], ones], 0)
        o = dot(vt, p.astype(jnp.bfloat16), 1, 0)
        l = o[64:65]
        outs.append(o[:64] * (1.0 / l))
        lse_ref[head : head + 1, :] = m * SCALE2 + jnp.log2(l)
        if head % 2 == 1:
            pair = head // 2
            cctx_ref[:, 128 * pair : 128 * pair + 128] = jnp.transpose(
                jnp.concatenate(outs, 0)
            ).astype(jnp.bfloat16)
            outs = []
    after = mid_ref[...]
    at = 0
    for w in cos:
        n = w.shape[0]
        after = after + dot(cctx_ref[:, at : at + n], w[...], 1, 0)
        at += n
    after_ref[...] = after
    u, _ = standardise(after)
    feed = (u * vec_ref[2:3, :] + vec_ref[3:4, :]).astype(jnp.bfloat16)
    feed_ref[...] = feed
    feedt_ref[...] = jnp.transpose(feed)


def row_block(n):
    return pl.BlockSpec((TB, n), lambda i: (i, 0))


def whole(t):
    return pl.BlockSpec(t.shape, lambda i: (0,) * t.ndim)


def mid_forward(cb, tb, x, ctxs, sos, cqs, cos, k, v, vec):
    n, d = x.shape
    smem = pl.BlockSpec(memory_space=pltpu.SMEM)
    bf, f = jnp.bfloat16, jnp.float32
    weights = [*sos, *cqs, *cos, k, v, vec]
    return pl.pallas_call(
        functools.partial(mid_forward_kernel, len(ctxs)),
        grid=(n // TB,),
        in_specs=[smem, smem, row_block(d)] + [row_block(c.shape[1]) for c in ctxs] + [whole(w) for w in weights],
        out_specs=[row_block(d)] * 4
        + [pl.BlockSpec((16, TB), lambda i: (0, i))]
        + [row_block(d)] * 2
        + [pl.BlockSpec((d, TB), lambda i: (0, i))],
        out_shape=[jax.ShapeDtypeStruct((n, d), t) for t in (f, bf, bf, bf)]
        + [jax.ShapeDtypeStruct((16, n), f)]
        + [jax.ShapeDtypeStruct((n, d), t) for t in (f, bf)]
        + [jax.ShapeDtypeStruct((d, n), bf)],
        scratch_shapes=[pltpu.VMEM((1040, TXT_ROW), bf)],
        compiler_params=pltpu.CompilerParams(vmem_limit_bytes=56 << 20),
        name="mid_forward",
        cost_estimate=pl.CostEstimate(flops=24 * n * d * d // 2, bytes_accessed=40 * n * d // 2, transcendentals=0),
    )(cb, tb, x, *ctxs, *weights)


def mid_backward_kernel(
    count, cb_ref, tb_ref, e_ref, after_ref, g_ref, mid_ref, q_ref, cctx_ref, lse_ref, *refs,
):
    cos, cqs, sos = [refs[count * t : count * t + count] for t in range(3)]
    (k_ref, v_ref, vec_ref,
     gc_ref, gq_ref, gmid_ref, gs_ref, gctx_ref, dk_ref, dv_ref, sums_ref,
     kt_ref, dka_ref, dva_ref, gcc_ref) = refs[3 * count :]
    i = pl.program_id(0)
    low = lax.broadcasted_iota(jnp.int32, (1, 128), 1) < HEAD_DIM

    @pl.when(i == 0)
    def _():
        kt_ref[...] = jnp.transpose(k_ref[...])
        dka_ref[...] = jnp.zeros_like(dka_ref)
        dva_ref[...] = jnp.zeros_like(dva_ref)
        sums_ref[...] = jnp.zeros_like(sums_ref)

    e = e_ref[...]
    u, inverse = standardise(after_ref[...])
    sums_ref[0:1, :] += column_sums(e * u)
    sums_ref[1:2, :] += column_sums(e)
    g_after = g_ref[...].astype(jnp.float32) + norm_input_grad(e, u, inverse, vec_ref[2:3, :])
    gmid_ref[...] = g_after
    gc = g_after.astype(jnp.bfloat16)
    gc_ref[...] = gc
    at = 0
    for w in cos:
        n = w.shape[0]
        gcc_ref[:, at : at + n] = dot(gc, w[...], 1, 1).astype(jnp.bfloat16)
        at += n
    places = TB * i + lax.broadcasted_iota(jnp.int32, (1, TB), 1)
    lo, hi = token_range(cb_ref, tb_ref, places)
    toks = lax.broadcasted_iota(jnp.int32, (TXT_ROW, TB), 0)
    allowed = (toks >= lo) & (toks < hi)

    def scores(head):
        p, h = head // 2, head % 2
        sl = slice(128 * p, 128 * p + 128)
        pick = lambda t: jnp.where(low == (h == 0), t, jnp.zeros_like(t))
        s = dot(pick(k_ref[:, sl]), q_ref[:, sl], 1, 1) * SCALE2 - lse_ref[head : head + 1, :]
        return jnp.where(allowed, s, MASKED), dot(pick(v_ref[:, sl]), gcc_ref[:, sl], 1, 1)

    ahead = 2
    queue = [scores(t) for t in range(ahead)]
    dqs, dks, dvs = [], [], []
    for head in range(16):
        if head + ahead < 16:
            queue.append(scores(head + ahead))
        p_at, h = head // 2, head % 2
        sl = slice(128 * p_at, 128 * p_at + 128)
        if h == 0:
            t = jnp.transpose(
                gcc_ref[:, sl].astype(jnp.float32) * cctx_ref[:, sl].astype(jnp.float32)
            )
        s, dp = queue.pop(0)
        p = jnp.exp2(s)
        ds = (p * (dp - column_sums(t[64 * h : 64 * h + 64]))).astype(jnp.bfloat16)
        dvs.append(dot(p.astype(jnp.bfloat16), gcc_ref[:, sl], 1, 0))
        dks.append(dot(ds, q_ref[:, sl], 1, 0))
        dqs.append(dot(kt_ref[64 * head : 64 * head + 64, :], ds, 1, 0))
        if h == 1:
            gq_ref[:, sl] = (
                jnp.transpose(jnp.concatenate(dqs, 0)) * HEAD_DIM**-0.5
            ).astype(jnp.bfloat16)
            dka_ref[:, sl] += jnp.where(low, dks[0], dks[1])
            dva_ref[:, sl] += jnp.where(low, dvs[0], dvs[1])
            dqs, dks, dvs = [], [], []
    e = None
    at = 0
    for w in cqs:
        n = w.shape[1]
        part = dot(gq_ref[:, at : at + n], w[...], 1, 1)
        e = part if e is None else e + part
        at += n
    u, inverse = standardise(mid_ref[...])
    sums_ref[2:3, :] += column_sums(e * u)
    sums_ref[3:4, :] += column_sums(e)
    g_middle = gmid_ref[...] + norm_input_grad(e, u, inverse, vec_ref[0:1, :])
    gmid_ref[...] = g_middle
    gs = g_middle.astype(jnp.bfloat16)
    gs_ref[...] = gs
    at = 0
    for w in sos:
        n = w.shape[0]
        gctx_ref[:, at : at + n] = dot(gs, w[...], 1, 1).astype(jnp.bfloat16)
        at += n

    @pl.when(i == pl.num_programs(0) - 1)
    def _():
        dk_ref[...] = (dka_ref[...] * HEAD_DIM**-0.5).astype(jnp.bfloat16)
        dv_ref[...] = dva_ref[...].astype(jnp.bfloat16)


def mid_backward(cb, tb, e, after, g, middle, q, cctx, lse, cos, cqs, sos, k, v, vec):
    n, d = after.shape
    smem = pl.BlockSpec(memory_space=pltpu.SMEM)
    bf, f = jnp.bfloat16, jnp.float32
    weights = [*cos, *cqs, *sos, k, v, vec]
    text = jax.ShapeDtypeStruct((TXT_ROW, d), bf)
    sums = jax.ShapeDtypeStruct((8, d), f)
    return pl.pallas_call(
        functools.partial(mid_backward_kernel, len(cos)),
        grid=(n // TB,),
        in_specs=[smem, smem] + [row_block(d)] * 6 + [pl.BlockSpec((16, TB), lambda i: (0, i))] + [whole(w) for w in weights],
        out_specs=[row_block(d)] * 5 + [whole(text), whole(text), whole(sums)],
        out_shape=[jax.ShapeDtypeStruct((n, d), t) for t in (bf, bf, f, bf, bf)] + [text, text, sums],
        scratch_shapes=[
            pltpu.VMEM((d, TXT_ROW), bf),
            pltpu.VMEM((TXT_ROW, d), f),
            pltpu.VMEM((TXT_ROW, d), f),
            pltpu.VMEM((TB, d), bf),
        ],
        compiler_params=pltpu.CompilerParams(vmem_limit_bytes=58 << 20),
        name="mid_backward",
        cost_estimate=pl.CostEstimate(flops=40 * n * d * d // 2, bytes_accessed=46 * n * d // 2, transcendentals=0),
    )(cb, tb, e, after, g, middle, q, cctx, lse, *weights)


def feed_kernel(
    idx_ref, fr_hbm, frt_hbm, cot_hbm, o_in, e_in, *refs, own, first, last
):
    if own:
        fi_src, fo_src = refs[:2]
        refs = refs[2:]
    else:
        fi_srcs, fo_srcs = refs[:2], refs[2:4]
        refs = refs[4:]
    (o_out, e_out, gi_ref, go_ref, fr_ref, frt_ref, cot_ref, out_ref, acc_o, acc_e,
     fi_buf, fo_buf, act_s, gh_s, wsem, isem, asem) = refs
    p = pl.program_id(0)
    slot = p % 2
    rows = 256
    blocks = fr_hbm.shape[0] // rows

    def weights(step, into, act):
        if own:
            at = pl.multiple_of(idx_ref[step] * NB, NB)
            act(pltpu.make_async_copy(fi_src.at[:, pl.ds(at, NB)], fi_buf.at[into], wsem.at[into, 0]))
            act(pltpu.make_async_copy(fo_src.at[pl.ds(at, NB), :], fo_buf.at[into], wsem.at[into, 1]))
        else:
            for s in range(2):
                @pl.when(step == s)
                def _(s=s):
                    act(pltpu.make_async_copy(fi_srcs[s], fi_buf.at[into], wsem.at[into, 0]))
                    act(pltpu.make_async_copy(fo_srcs[s], fo_buf.at[into], wsem.at[into, 1]))

    def cut(r):
        return slice(rows * r, rows * r + rows)

    def row_in(r):
        return [
            pltpu.make_async_copy(fr_hbm.at[cut(r), :], fr_ref.at[cut(r), :], isem.at[0, r]),
            pltpu.make_async_copy(cot_hbm.at[cut(r), :], cot_ref.at[cut(r), :], isem.at[1, r]),
        ]

    def sums_in(r):
        loads = [pltpu.make_async_copy(o_in.at[cut(r), :], acc_o.at[cut(r), :], asem.at[0, r])]
        if not first:
            loads.append(pltpu.make_async_copy(e_in.at[cut(r), :], acc_e.at[cut(r), :], asem.at[1, r]))
        return loads

    def sums_out(r):
        stores = [pltpu.make_async_copy(acc_e.at[cut(r), :], e_out.at[cut(r), :], asem.at[1, r])]
        source = out_ref if last else acc_o
        stores.append(pltpu.make_async_copy(source.at[cut(r), :], o_out.at[cut(r), :], asem.at[0, r]))
        return stores

    turned = pltpu.make_async_copy(frt_hbm, frt_ref, isem.at[2, 0])

    @pl.when(p == 0)
    def _():
        weights(p, slot, lambda c: c.start())
        for c in row_in(0) + row_in(1) + sums_in(0):
            c.start()
        if first:
            acc_e[...] = jnp.zeros_like(acc_e)
        for c in row_in(0):
            c.wait()

    weights(p, slot, lambda c: c.wait())

    @pl.when(p == 0)
    def _():
        weights(p + 1, 1 - slot, lambda c: c.start())

    fi, fo = fi_buf.at[slot], fo_buf.at[slot]

    def products(r):
        return dot(fr_ref[cut(r), :], fi[...], 1, 0), dot(cot_ref[cut(r), :], fo[...], 1, 1)

    def whole_pass(arriving):
        queue = [products(0)]
        for r in range(blocks):
            if arriving:
                for c in (row_in(r + 1) if r + 1 < blocks else []) + sums_in(r):
                    c.wait()
                for c in (row_in(r + 2) if r + 2 < blocks else []) + (
                    sums_in(r + 1) if r + 1 < blocks else []
                ):
                    c.start()
                if r == 2:
                    turned.start()
            elif r > 0:
                for c in sums_out(r - 1):
                    c.start()
            if r + 1 < blocks:
                queue.append(products(r + 1))
            h, g = queue.pop(0)
            active, slope = gelu_pair(h)
            active = active.astype(jnp.bfloat16)
            gh = (g * slope).astype(jnp.bfloat16)
            act_s[cut(r), :] = active
            gh_s[cut(r), :] = gh
            o_sum = acc_o[cut(r), :] + dot(active, fo[...], 1, 0)
            if last and not arriving:
                out_ref[cut(r), :] = o_sum.astype(jnp.bfloat16)
            else:
                acc_o[cut(r), :] = o_sum
            acc_e[cut(r), :] += dot(gh, fi[...], 1, 1)
        if not arriving:
            for c in sums_out(blocks - 1):
                c.start()
        if arriving:
            turned.wait()
        gi_ref[...] = dot(frt_ref[...], gh_s[...], 1, 0).astype(jnp.bfloat16)
        go_ref[...] = dot(act_s[...], cot_ref[...], 0, 0).astype(jnp.bfloat16)
        if not arriving:
            for r in range(blocks):
                for c in sums_out(r):
                    c.wait()

    @pl.when(p == 0)
    def _():
        whole_pass(True)

    @pl.when(p == 1)
    def _():
        whole_pass(False)


def feed_part(idx, rows, rows_t, cot, o_in, e_in, fis, fos, first, last):
    n, d = rows.shape
    own = len(fis) == 1
    bf, f = jnp.bfloat16, jnp.float32
    hbm = pl.BlockSpec(memory_space=pl.ANY)
    grad = lambda shape: jax.ShapeDtypeStruct(shape, bf)
    blocks = n // 256
    return pl.pallas_call(
        functools.partial(feed_kernel, own=own, first=first, last=last),
        grid_spec=pltpu.PrefetchScalarGridSpec(
            num_scalar_prefetch=1,
            grid=(2,),
            in_specs=[hbm] * (5 + 2 * len(fis)),
            out_specs=[
                hbm,
                hbm,
                pl.BlockSpec((d, NB), lambda p, idx: (0, idx[p] % 2)),
                pl.BlockSpec((NB, d), lambda p, idx: (idx[p] % 2, 0)),
            ],
            scratch_shapes=[
                pltpu.VMEM((n, d), bf),
                pltpu.VMEM((d, n), bf),
                pltpu.VMEM((n, d), bf),
                pltpu.VMEM((n, d) if last else (16, 128), bf),
                pltpu.VMEM((n, d), f),
                pltpu.VMEM((n, d), f),
                pltpu.VMEM((2, d, NB), bf),
                pltpu.VMEM((2, NB, d), bf),
                pltpu.VMEM((n, NB), bf),
                pltpu.VMEM((n, NB), bf),
                pltpu.SemaphoreType.DMA((2, 2)),
                pltpu.SemaphoreType.DMA((3, blocks)),
                pltpu.SemaphoreType.DMA((2, blocks)),
            ],
        ),
        out_shape=[
            jax.ShapeDtypeStruct((n, d), bf if last else f),
            jax.ShapeDtypeStruct((n, d), f),
            grad((d, 2 * NB)),
            grad((2 * NB, d)),
        ],
        compiler_params=pltpu.CompilerParams(vmem_limit_bytes=60 << 20),
        name="feed_last" if last else "feed_first" if first else "feed_more",
        cost_estimate=pl.CostEstimate(flops=24 * n * d * NB, bytes_accessed=48 << 20, transcendentals=0),
    )(idx, rows, rows_t, cot, o_in, e_in, *fis, *fos)


def final_kernel(x_ref, gmid_ref, *refs):
    count = (len(refs) - 3) // 2
    gs, ws = refs[:count], refs[count : 2 * count]
    vec_ref, out_ref, sums_ref = refs[2 * count :]

    @pl.when(pl.program_id(0) == 0)
    def _():
        sums_ref[...] = jnp.zeros_like(sums_ref)

    e = None
    for g, w in zip(gs, ws):
        part = dot(g[...], w[...], 1, 1)
        e = part if e is None else e + part
    u, inverse = standardise(x_ref[...].astype(jnp.float32))
    sums_ref[0:1, :] += column_sums(e * u)
    sums_ref[1:2, :] += column_sums(e)
    out_ref[...] = gmid_ref[...] + norm_input_grad(e, u, inverse, vec_ref[4:5, :])


def final_grads(x, gmid, gs, ws, vec):
    n, d = x.shape
    sums = jax.ShapeDtypeStruct((8, d), jnp.float32)
    return pl.pallas_call(
        final_kernel,
        grid=(n // TB,),
        in_specs=[row_block(d), row_block(d)] + [row_block(g.shape[1]) for g in gs] + [whole(w) for w in ws] + [whole(vec)],
        out_specs=[row_block(d), whole(sums)],
        out_shape=[jax.ShapeDtypeStruct((n, d), jnp.float32), sums],
        compiler_params=pltpu.CompilerParams(vmem_limit_bytes=56 << 20),
        name="frames_gradient",
        cost_estimate=pl.CostEstimate(flops=6 * n * d * d, bytes_accessed=24 * n * d // 2, transcendentals=0),
    )(x, gmid, *gs, *ws, vec)


class Journey:
    def __init__(self, hops):
        self.hops = hops
        self.pending = next(hops)
        self.result = None

    def go(self, tied):
        try:
            self.pending = self.hops.send(tied)
        except StopIteration as end:
            self.pending, self.result = None, end.value


def onward(main, *journeys):
    main, tied = lax.optimization_barrier((main, [j.pending for j in journeys]))
    for journey, sent in zip(journeys, tied):
        journey.go(sent)
    return main


def row_body(dp, *args):
    (
        frames,
        text_states,
        clip_lengths,
        text_lengths,
        cotangent,
        self_gain,
        self_shift,
        self_query,
        self_key,
        self_value,
        self_out,
        cross_gain,
        cross_shift,
        cross_query,
        cross_key,
        cross_value,
        cross_out,
        text_weight,
        text_bias,
        feed_gain,
        feed_shift,
        feed_in,
        feed_out,
    ) = args
    bf16, f32 = jnp.bfloat16, jnp.float32
    me = lax.axis_index("dp")
    half = lax.axis_index("mp")
    core = me % 2
    swap = [(0, 1), (1, 0)]
    steps = [2 << i for i in range(dp.bit_length() - 2)]

    def over_y(t):
        return jax.tree.map(lambda a: lax.ppermute(a, "mp", swap), t)

    def over_bit(t, step):
        return jax.tree.map(lambda a: lax.ppermute(a, "dp", [(i, i ^ step) for i in range(dp)]), t)

    def over_core(t):
        return over_bit(t, 1)

    def piece(t, at, size, axis):
        return lax.dynamic_slice_in_dim(t, at * size, size, axis)

    def ordered(mine_first, mine, theirs, axis):
        return jnp.concatenate(
            [jnp.where(mine_first, mine, theirs), jnp.where(mine_first, theirs, mine)], axis
        )

    def add(*ts):
        return reduce(jnp.add, [t.astype(f32) for t in ts]).astype(bf16)

    def parts_of(ts, step):
        at = (me // step) % 2
        size = ts[0].shape[0] // 2
        return [add(*[piece(t, w, size, 0) for t in ts]) for w in (at, 1 - at)]

    def travel(terms, left):
        for step in left:
            kept, sent = parts_of(terms, step)
            sent = yield sent
            terms = (kept, over_bit(sent, step))
        block = add(*terms)
        for step in reversed(steps):
            block = yield block
            block = ordered((me // step) % 2 == 0, block, over_bit(block, step), 0)
        block = yield block
        return block, over_core(block)

    def travel_y(own, other):
        other = yield other
        return (yield from travel((*own, over_y(other)), steps))

    def travel_small(t):
        for hop in (over_core, over_y, *[functools.partial(over_bit, step=s) for s in steps]):
            t = yield t
            t = t + hop(t)
        return t

    lengths = lax.dynamic_index_in_dim(clip_lengths, half, 0, keepdims=False)
    words = lax.dynamic_index_in_dim(text_lengths, half, 0, keepdims=False)
    clip_bounds, text_bounds = jnp.cumsum(lengths), jnp.cumsum(words)
    zeros = jnp.zeros_like(self_gain)
    vec = jnp.stack(
        [cross_gain, cross_shift, feed_gain, feed_shift, self_gain, zeros, zeros, zeros]
    )

    def quarter(t, which, axis):
        return piece(t, which, t.shape[axis] // 2, axis)

    tie = lax.optimization_barrier
    x_at = (me // 2) % 2

    def shared(mine, axis):
        return quarter(mine, x_at, axis)

    def joined(came, across, axis):
        return ordered(x_at == 0, came, across, axis)

    trio = (self_query, self_key, self_value)
    qkv_c = jnp.concatenate([quarter(t, core, 1) for t in trio], 1)
    qkv_d = jnp.concatenate([quarter(t, 1 - core, 1) for t in trio], 1)
    text_part = (product(text_states, text_weight) + text_bias).astype(bf16)
    qkv_half = shared(qkv_c, 0)
    cut = qkv_half.shape[0] // 2
    frames, text_part, qkv_1, qkv_2 = tie((frames, text_part, qkv_half[:cut], qkv_half[cut:]))
    text_came, qkv_1 = over_y(text_part), over_y(qkv_1)
    standard, _ = norm_parts(frames.astype(f32))
    self_rows = (standard * self_gain + self_shift).astype(bf16)
    qkv, ctx, log = [None] * 4, [None] * 4, [None] * 4
    qkv[0] = product(self_rows, qkv_c).astype(bf16)
    qkv[2] = product(self_rows, qkv_d).astype(bf16)
    qkv[0], qkv[2], text_came, qkv_1, qkv_2 = tie((qkv[0], qkv[2], text_came, qkv_1, qkv_2))
    text_full = ordered(half == 0, text_part, text_came, 1)
    keys_here = product(text_full, cross_key).astype(bf16)
    values_here = product(text_full, cross_value).astype(bf16)
    text_rows = TXT_ROW

    def row_of(t, which):
        return piece(t, which, text_rows, 0)

    kv_send = jnp.concatenate([row_of(keys_here, 1 - half), row_of(values_here, 1 - half)], 1)
    qkv_2, across_1 = over_y(qkv_2), over_bit(qkv_1, 2)
    ctx[0], log[0] = group_forward(clip_bounds, qkv[0])
    so_c, cq_c, co_c = quarter(self_out, core, 0), quarter(cross_query, core, 1), quarter(cross_out, core, 0)
    late = [shared(so_c, 0), shared(cq_c, 0), shared(co_c, 0)]
    ctx[0], qkv[2], qkv_2, across_1, kv_send, late = tie(
        (ctx[0], qkv[2], qkv_2, across_1, kv_send, late)
    )
    across_2 = over_bit(qkv_2, 2)
    kv_came = over_y(kv_send)
    so_h = over_y(late[0])
    ctx[2], log[2] = group_forward(clip_bounds, qkv[2])
    ctx[2], across_2, kv_came, so_h = tie((ctx[2], across_2, kv_came, so_h))
    qkv_oc = joined(jnp.concatenate([qkv_1, qkv_2]), jnp.concatenate([across_1, across_2]), 0)
    qkv_oc, rows_1, so_h = tie((qkv_oc, self_rows, so_h))
    qkv_od = over_core(qkv_oc)
    cq_h, so_x = over_y(late[1]), over_bit(so_h, 2)
    qkv[1] = product(rows_1, qkv_oc).astype(bf16)
    qkv[1], cq_h = tie((qkv[1], cq_h))
    co_h, cq_x = over_y(late[2]), over_bit(cq_h, 2)
    ctx[1], log[1] = group_forward(clip_bounds, qkv[1])
    qkv[3] = product(self_rows, qkv_od).astype(bf16)
    so_oc, cq_oc = joined(so_h, so_x, 0), joined(cq_h, cq_x, 0)
    qkv[3], ctx[1], co_h, so_oc, cq_oc = tie((qkv[3], ctx[1], co_h, so_oc, cq_oc))
    co_x = over_bit(co_h, 2)
    so_od, cq_od = over_core(so_oc), over_core(cq_oc)
    ctx[3], log[3] = group_forward(clip_bounds, qkv[3])
    co_oc = joined(co_h, co_x, 0)
    co_od = over_core(co_oc)
    width = cross_key.shape[1]

    def mixed(mine, theirs):
        mine = row_of(mine, half)
        return jnp.concatenate(
            [quarter(t, w, 1) for w in (core, 1 - core) for t in (mine, theirs)], 1
        )

    keys = mixed(keys_here, kv_came[:, :width])
    values = mixed(values_here, kv_came[:, width:])
    qkv_w = [qkv_c, qkv_oc, qkv_d, qkv_od]
    so = [so_c, so_oc, quarter(self_out, 1 - core, 0), so_od]
    cq = [cq_c, cq_oc, quarter(cross_query, 1 - core, 1), cq_od]
    co = [co_c, co_oc, quarter(cross_out, 1 - core, 0), co_od]
    block = 2 * core + x_at
    fi_s, fo_s = piece(feed_in, block, NB, 1), piece(feed_out, block, NB, 0)
    ctx, so, cq, co, keys, values, fi_s, fo_s = tie((ctx, so, cq, co, keys, values, fi_s, fo_s))
    fi_cx = over_y(fi_s)

    middle, cross_rows, cross_q, cross_ctx, cross_log, after, feed_rows, feed_t = mid_forward(
        clip_bounds, text_bounds, frames, ctx, so, cq, co, keys, values, vec
    )

    feed = (feed_rows, feed_t, cotangent)
    places = lambda *t: jnp.stack(t).astype(jnp.int32)
    feed, fi_cx, fo_s = tie((feed, fi_cx, fo_s))
    fo_cx, fi_cy = over_y(fo_s), over_bit(fi_cx, 2)
    o, e, in_od, out_od = feed_part(
        places(2 - 2 * core, 3 - 2 * core), *feed, after, after, [feed_in], [feed_out], True, False
    )
    o, e, fo_cx, fi_cy = tie((o, e, fo_cx, fi_cy))
    fo_cy = over_bit(fo_cx, 2)
    fi_d = over_core([fi_cx, fi_cy])
    o, e, in_oc, out_oc = feed_part(
        places(2 * core, 2 * core + 1), *feed, o, e, [feed_in], [feed_out], False, False
    )
    o, e, fo_cy, fi_d = tie((o, e, fo_cy, fi_d))
    fo_d = over_core([fo_cx, fo_cy])
    o, e, fo_d, in_od, out_od = tie((o, e, fo_d, in_od, out_od))
    in_og, out_og = over_core([in_od, out_od])
    where = places(x_at, 1 - x_at)
    o, e, in_td, out_td = feed_part(where, *feed, o, e, fi_d, fo_d, False, False)
    o, e, in_og, in_td, out_td = tie((o, e, in_og, in_td, out_td))
    own_low, own_high = parts_of((in_oc, in_og), 2)
    o, e, own_low, own_high = tie((o, e, own_low, own_high))
    in_tg, out_tg = over_core([in_td, out_td])
    own_came = over_bit(own_high, 2)
    output, e, in_tc, out_tc = feed_part(
        where, *feed, o, e, [fi_cx, fi_cy], [fo_cx, fo_cy], False, True
    )
    e, in_tg, out_tg, own_came = tie((e, in_tg, out_tg, own_came))
    other_low, other_high = parts_of((in_tc, in_tg), 2)

    def travel_in():
        sent = yield other_high
        other = yield add(other_low, over_bit(sent, 2))
        return (yield from travel((own_low, own_came, over_y(other)), steps[1:]))

    j_in = Journey(travel_in())
    middle_cut = out_tc.shape[1] // 2
    j_out = []
    for sl in (slice(0, middle_cut), slice(middle_cut, None)):
        j_out.append(
            Journey(
                travel_y((out_oc[:, sl], out_og[:, sl]), add(out_tc[:, sl], out_tg[:, sl]))
            )
        )
    e = onward(e, j_in, j_out[0])

    g_c, grad_q, g_middle, g_s, grad_ctx, grad_k, grad_v, sums = mid_backward(
        clip_bounds,
        text_bounds,
        e,
        after,
        cotangent,
        middle,
        cross_q,
        cross_ctx,
        cross_log,
        co,
        cq,
        so,
        keys,
        values,
        vec,
    )
    small = Journey(travel_small(sums[:4]))
    (g_c, grad_q, g_s, grad_ctx, grad_k, grad_v) = onward(
        (g_c, grad_q, g_s, grad_ctx, grad_k, grad_v), j_out[0], j_out[1], small
    )

    side = width

    def both(big, small):
        out = []
        for at in (0, side):
            t = outer_sum(big, small[:, at : at + side]).astype(bf16)
            out.append((t[:, : side // 2], t[:, side // 2 :]))
        return out

    ctx_all = [jnp.concatenate(ctx[:2], 1), jnp.concatenate(ctx[2:], 1)]
    wide = [both(cross_rows, grad_q), both(g_c, cross_ctx)]
    so_parts = [outer_sum(g_s, t).astype(bf16) for t in ctx_all]
    wide.append([(t[:, : side // 2], t[:, side // 2 :]) for t in so_parts])
    c_keep, c_send = [
        tuple(jnp.concatenate([w[n][m] for w in wide], 1) for m in range(2)) for n in range(2)
    ]

    def split_heads_back(t):
        oc, tc, od, td = [t[:, side // 2 * n : side // 2 * (n + 1)] for n in range(4)]
        return ordered(core == 0, oc, od, 1), ordered(core == 0, tc, td, 1)

    dk_own, dk_other = split_heads_back(grad_k)
    dv_own, dv_other = split_heads_back(grad_v)
    came = over_y(jnp.concatenate([dk_other, dv_other], 1))
    dk = ordered(half == 0, dk_own, came[:, :width], 0)
    dv = ordered(half == 0, dv_own, came[:, width:], 0)
    grad_text = against(dk, cross_key) + against(dv, cross_value)
    mine = piece(grad_text, half, width, 1)
    grad_text = (
        mine + over_y(piece(grad_text, 1 - half, width, 1).astype(bf16)).astype(f32)
    ).astype(bf16)
    text_part = against(grad_text, text_weight).astype(bf16)
    text_grad = text_part.astype(f32) + over_y(text_part).astype(f32)
    tall = text_full.shape[1] - text_states.shape[1]
    text_wide = jnp.concatenate(
        [
            text_states,
            jnp.ones((text_states.shape[0], 1), bf16),
            jnp.zeros((text_states.shape[0], tall - 1), bf16),
        ],
        1,
    )
    text_keep, text_send = [
        jnp.concatenate(
            [
                outer_sum(text_full, quarter(dk, w, 1)),
                outer_sum(text_full, quarter(dv, w, 1)),
                outer_sum(text_wide, quarter(grad_text, w, 1)),
            ],
            1,
        ).astype(bf16)
        for w in (core, 1 - core)
    ]

    grad_ctx, c_send, text_send = tie((grad_ctx, c_send, text_send))
    c_got, text_got = over_core((c_send, text_send))
    grad_ctx = onward(grad_ctx, j_in, *j_out, small)

    grads, parts = [None] * 4, [None] * 4

    def back(n, main):
        grads[n] = group_backward(clip_bounds, qkv[n], ctx[n], main, log[n], n)
        parts[n] = outer_sum(self_rows, grads[n]).astype(bf16)
        main, parts[n] = tie((main, parts[n]))
        return main

    main = back(3, grad_ctx)
    main, c_got, text_got = tie((main, c_got, text_got))
    c_cut = c_keep[0].shape[1] // 2
    j_wide = [
        Journey(
            travel_y((c_keep[0][:, sl], c_got[0][:, sl]), add(c_keep[1][:, sl], c_got[1][:, sl]))
        )
        for sl in (slice(0, c_cut), slice(c_cut, None))
    ]
    j_text = Journey(travel((text_keep, text_got), steps))
    main, parts[3] = tie((main, parts[3]))
    td_got = over_core(parts[3])
    main = onward(main, j_in, *j_out, j_wide[0], j_text, small)
    main = back(1, main)
    main, td_got = tie((main, td_got))
    e_cut = parts[1].shape[0] // 2
    other = add(parts[1], td_got)
    main, other = tie((main, other))
    came_1 = over_y(other[:e_cut])
    main = onward(main, j_in, *j_out, j_text, small)
    main = back(2, main)
    main, parts[2], came_1 = tie((main, parts[2], came_1))
    od_got = over_core(parts[2])
    came_2 = over_y(other[e_cut:])
    main = onward(main, j_in, *j_out, j_wide[0], j_text)
    main = back(0, main)
    main, came_1, came_2, od_got = tie((main, came_1, came_2, od_got))
    j_self = Journey(travel((parts[0], od_got, jnp.concatenate([came_1, came_2])), steps))
    grads = onward(grads, j_in, *j_out, j_wide[0], j_wide[1], j_text, j_self)
    frames_grad, self_sums = final_grads(frames, g_middle, grads, qkv_w, vec)
    last = Journey(travel_small(self_sums[:2]))
    everything = [j_in, *j_out, *j_wide, j_text, j_self, small, last]
    frames_grad = onward(frames_grad, *[j for j in everything if j.result is None])
    for journey in everything:
        while journey.result is None:
            journey.go(journey.pending)
    early, late = small.result, last.result
    everything = None

    def full(result, at, size, axis):
        mine, theirs = [t[:, at : at + size] for t in result]
        return ordered(core == 0, mine, theirs, axis).astype(f32)

    n = side // 2
    wide_sum = [jnp.concatenate([j.result[t] for j in j_wide], 1) for t in range(2)]
    text_sum, self_sum = j_text.result, j_self.result
    out_sum = [jnp.concatenate([j.result[t] for j in j_out], 1) for t in range(2)]
    text_rows_grad = full(text_sum, 2 * n, n, 1)
    return (
        output,
        frames_grad,
        text_grad,
        late[0],
        late[1],
        full(self_sum, 0, n, 1),
        full(self_sum, n, n, 1),
        full(self_sum, 2 * n, n, 1),
        full(wide_sum, 2 * n, n, 1).T,
        early[2],
        early[3],
        full(wide_sum, 0, n, 1),
        full(text_sum, 0, n, 1),
        full(text_sum, n, n, 1),
        full(wide_sum, n, n, 1).T,
        text_rows_grad[: text_states.shape[1]],
        text_rows_grad[text_states.shape[1]],
        early[0],
        early[1],
        full(j_in.result, 0, 2 * NB, 1),
        ordered(core == 0, *out_sum, 0).astype(f32),
    )


def chosen(dp, mp, *args):
    rows_here, frames_here = args[2].shape[0], args[0].shape[0]
    if mp == 2 and dp == 16 and rows_here == mp and frames_here == ROW_LEN:
        return row_body(dp, *args)
    return body(*args)


def solution(mesh):
    return jax.shard_map(
        functools.partial(chosen, mesh.shape["dp"], mesh.shape["mp"]),
        mesh=mesh,
        in_specs=(
            P(("dp", "mp"), None),
            P("dp", None),
            P("dp", None),
            P("dp", None),
            P(("dp", "mp"), None),
            P(),
            P(),
            P(None, "mp"),
            P(None, "mp"),
            P(None, "mp"),
            P("mp", None),
            P(),
            P(),
            P(None, "mp"),
            P(None, "mp"),
            P(None, "mp"),
            P("mp", None),
            P(None, "mp"),
            P("mp"),
            P(),
            P(),
            P(None, "mp"),
            P("mp", None),
        ),
        out_specs=(
            P(("dp", "mp"), None),
            P(("dp", "mp"), None),
            P("dp", None),
            P(),
            P(),
            P(None, "mp"),
            P(None, "mp"),
            P(None, "mp"),
            P("mp", None),
            P(),
            P(),
            P(None, "mp"),
            P(None, "mp"),
            P(None, "mp"),
            P("mp", None),
            P(None, "mp"),
            P("mp"),
            P(),
            P(),
            P(None, "mp"),
            P("mp", None),
        ),
        check_vma=False,
    )
```

```python
import functools
from functools import reduce

import jax
import jax.numpy as jnp
from jax import lax
from jax.experimental import pallas as pl
from jax.experimental.pallas import tpu as pltpu
from jax.sharding import PartitionSpec as P

HEAD_DIM = 64
ROW_LEN = 1536
TXT_ROW = 128


EPSILON = 1e-05
MASKED = -1e30


def product(left_side, right_side):
    return jnp.dot(left_side, right_side, preferred_element_type=jnp.float32)


def against(left_side, right_side):
    return lax.dot_general(
        left_side, right_side, (((1,), (1,)), ((), ())), preferred_element_type=jnp.float32
    )


def outer_sum(left_side, right_side):
    return lax.dot_general(
        left_side, right_side, (((0,), (0,)), ((), ())), preferred_element_type=jnp.float32
    )


def exact_gelu(tensor):
    return jax.nn.gelu(tensor, approximate=False)


def segment_ids(lengths, positions):
    bounds = jnp.cumsum(lengths, axis=-1)
    places = jnp.arange(positions, dtype=jnp.int32)
    return jnp.sum((places[None, :, None] >= bounds[:, None, :]).astype(jnp.int32), axis=-1)


def split_heads(tensor, row_count):
    return tensor.reshape(
        row_count, tensor.shape[0] // row_count, tensor.shape[1] // HEAD_DIM, HEAD_DIM
    )


def norm_parts(tensor):
    average = jnp.mean(tensor, axis=-1, keepdims=True)
    centered = tensor - average
    inverse = lax.rsqrt(jnp.mean(centered * centered, axis=-1, keepdims=True) + EPSILON)
    return (centered * inverse, inverse)


def norm_back(gradient, standard, inverse, norm_gain):
    scaled = gradient * norm_gain
    first_mean = jnp.mean(scaled, axis=-1, keepdims=True)
    second_mean = jnp.mean(scaled * standard, axis=-1, keepdims=True)
    return (
        inverse * (scaled - first_mean - standard * second_mean),
        jnp.sum(gradient * standard, axis=0),
        jnp.sum(gradient, axis=0),
    )


def spread_rows(tensor):
    return lax.all_gather(tensor, "mp", axis=0, tiled=True)


def spread_cotangent(tensor):
    return lax.all_gather(tensor, "mp", axis=0, tiled=True)


def branch_sum(left_side, right_side):
    return lax.psum_scatter(product(left_side, right_side), "mp", scatter_dimension=0, tiled=True)


def input_grads(factor_pairs):
    partials = [against(left_side, right_side) for left_side, right_side in factor_pairs]
    return lax.psum_scatter(reduce(jnp.add, partials), "mp", scatter_dimension=0, tiled=True)


def attend_forward(queries, key_heads, values, allowed):
    scores = jnp.einsum(
        "rqhd,rkhd->rhqk", queries, key_heads, preferred_element_type=jnp.float32
    ) * HEAD_DIM ** (-0.5)
    scores = jnp.where(allowed[:, None], scores, MASKED)
    row_max = jnp.max(scores, axis=-1, keepdims=True)
    shifted = jnp.exp(scores - row_max)
    totals = jnp.sum(shifted, axis=-1, keepdims=True)
    soft_weights = (shifted / totals).astype(jnp.bfloat16)
    context = jnp.einsum(
        "rhqk,rkhd->rqhd", soft_weights, values, preferred_element_type=jnp.float32
    )
    return (context, row_max + jnp.log(totals))


def attend_back(queries, key_heads, values, allowed, log_totals, grad_context):
    score_scale = HEAD_DIM ** (-0.5)
    scores = (
        jnp.einsum("rqhd,rkhd->rhqk", queries, key_heads, preferred_element_type=jnp.float32)
        * score_scale
    )
    scores = jnp.where(allowed[:, None], scores, MASKED)
    soft_weights = jnp.exp(scores - log_totals)
    grad_soft = jnp.einsum(
        "rqhd,rkhd->rhqk", grad_context, values, preferred_element_type=jnp.float32
    )
    row_inner = jnp.sum(grad_soft * soft_weights, axis=-1, keepdims=True)
    grad_scores = (soft_weights * (grad_soft - row_inner)).astype(jnp.bfloat16)
    grad_query = (
        jnp.einsum("rhqk,rkhd->rqhd", grad_scores, key_heads, preferred_element_type=jnp.float32)
        * score_scale
    )
    grad_keys = (
        jnp.einsum("rhqk,rqhd->rkhd", grad_scores, queries, preferred_element_type=jnp.float32)
        * score_scale
    )
    grad_values = jnp.einsum(
        "rhqk,rqhd->rkhd",
        soft_weights.astype(jnp.bfloat16),
        grad_context,
        preferred_element_type=jnp.float32,
    )
    return (grad_query, grad_keys, grad_values)


def self_allowed(segments, start_at, stop_at):
    places = jnp.arange(stop_at, dtype=jnp.int32)
    same_clip = segments[:, start_at:stop_at, None] == segments[:, None, :stop_at]
    return same_clip & (places[start_at:stop_at, None] >= places[None, :])[None]


def self_forward(queries, key_heads, values, segments):
    block_size = min(512, queries.shape[1])
    contexts = []
    log_totals = []
    for start_at in range(0, queries.shape[1], block_size):
        stop_at = start_at + block_size
        context, log_total = attend_forward(
            queries[:, start_at:stop_at],
            key_heads[:, :stop_at],
            values[:, :stop_at],
            self_allowed(segments, start_at, stop_at),
        )
        contexts.append(context)
        log_totals.append(log_total)
    return (jnp.concatenate(contexts, axis=1), jnp.concatenate(log_totals, axis=2))


def self_back(queries, key_heads, values, segments, log_totals, grad_context):
    block_size = min(512, queries.shape[1])
    query_parts = []
    grad_keys = jnp.zeros(key_heads.shape, jnp.float32)
    grad_values = jnp.zeros(values.shape, jnp.float32)
    for start_at in range(0, queries.shape[1], block_size):
        stop_at = start_at + block_size
        grad_query, key_part, value_part = attend_back(
            queries[:, start_at:stop_at],
            key_heads[:, :stop_at],
            values[:, :stop_at],
            self_allowed(segments, start_at, stop_at),
            log_totals[:, :, start_at:stop_at],
            grad_context[:, start_at:stop_at],
        )
        query_parts.append(grad_query)
        grad_keys = grad_keys.at[:, :stop_at].add(key_part)
        grad_values = grad_values.at[:, :stop_at].add(value_part)
    return (jnp.concatenate(query_parts, axis=1), grad_keys, grad_values)


def body(
    frames,
    text_states,
    clip_lengths,
    text_lengths,
    cotangent,
    self_gain,
    self_shift,
    self_query,
    self_key,
    self_value,
    self_out,
    cross_gain,
    cross_shift,
    cross_query,
    cross_key,
    cross_value,
    cross_out,
    text_weight,
    text_bias,
    feed_gain,
    feed_shift,
    feed_in,
    feed_out,
):
    row_count = clip_lengths.shape[0]
    clip_segs = segment_ids(clip_lengths, ROW_LEN)
    text_segs = segment_ids(text_lengths, TXT_ROW)
    residual = frames.astype(jnp.float32)
    self_standard, self_inverse = norm_parts(residual)
    self_rows = spread_rows((self_standard * self_gain + self_shift).astype(jnp.bfloat16))
    self_queries = product(self_rows, self_query).astype(jnp.bfloat16)
    self_keys = product(self_rows, self_key).astype(jnp.bfloat16)
    self_values = product(self_rows, self_value).astype(jnp.bfloat16)
    self_context, self_logs = self_forward(
        split_heads(self_queries, row_count),
        split_heads(self_keys, row_count),
        split_heads(self_values, row_count),
        clip_segs,
    )
    self_context = self_context.reshape(self_queries.shape).astype(jnp.bfloat16)
    middle = residual + branch_sum(self_context, self_out)
    cross_standard, cross_inverse = norm_parts(middle)
    cross_rows = spread_rows((cross_standard * cross_gain + cross_shift).astype(jnp.bfloat16))
    text_part = (product(text_states, text_weight) + text_bias).astype(jnp.bfloat16)
    text_full = lax.all_gather(text_part, "mp", axis=1, tiled=True)
    cross_queries = product(cross_rows, cross_query).astype(jnp.bfloat16)
    cross_keys = product(text_full, cross_key).astype(jnp.bfloat16)
    cross_values = product(text_full, cross_value).astype(jnp.bfloat16)
    cross_allowed = clip_segs[:, :, None] == text_segs[:, None, :]
    cross_context, cross_logs = attend_forward(
        split_heads(cross_queries, row_count),
        split_heads(cross_keys, row_count),
        split_heads(cross_values, row_count),
        cross_allowed,
    )
    cross_context = cross_context.reshape(cross_queries.shape).astype(jnp.bfloat16)
    after_cross = middle + branch_sum(cross_context, cross_out)
    feed_standard, feed_inverse = norm_parts(after_cross)
    feed_normed = (feed_standard * feed_gain + feed_shift).astype(jnp.bfloat16)
    feed_rows = spread_rows(feed_normed)
    hidden = product(feed_rows, feed_in)
    active, gelu_back = jax.vjp(exact_gelu, hidden)
    active = active.astype(jnp.bfloat16)
    output = after_cross + branch_sum(active, feed_out)
    grad_output = cotangent.astype(jnp.float32)
    feed_cotangent = grad_output.astype(jnp.bfloat16)
    grad_rows = spread_cotangent(feed_cotangent)
    feed_out_grad = outer_sum(active, grad_rows)
    grad_hidden = gelu_back(against(grad_rows, feed_out))[0].astype(jnp.bfloat16)
    feed_in_grad = outer_sum(feed_rows, grad_hidden)
    grad_feed_normed = input_grads(((grad_hidden, feed_in),))
    grad_norm, feed_gain_grad, feed_shift_grad = norm_back(
        grad_feed_normed, feed_standard, feed_inverse, feed_gain
    )
    grad_after = grad_output + grad_norm
    cross_cotangent = spread_cotangent(grad_after.astype(jnp.bfloat16))
    cross_out_grad = outer_sum(cross_context, cross_cotangent)
    grad_context = against(cross_cotangent, cross_out).astype(jnp.bfloat16)
    grad_queries, grad_keys, grad_values = attend_back(
        split_heads(cross_queries, row_count),
        split_heads(cross_keys, row_count),
        split_heads(cross_values, row_count),
        cross_allowed,
        cross_logs,
        split_heads(grad_context, row_count),
    )
    grad_queries = grad_queries.reshape(cross_queries.shape).astype(jnp.bfloat16)
    grad_keys = grad_keys.reshape(cross_keys.shape).astype(jnp.bfloat16)
    grad_values = grad_values.reshape(cross_values.shape).astype(jnp.bfloat16)
    cross_query_grad = outer_sum(cross_rows, grad_queries)
    cross_key_grad = outer_sum(text_full, grad_keys)
    cross_value_grad = outer_sum(text_full, grad_values)
    grad_text_full = against(grad_keys, cross_key) + against(grad_values, cross_value)
    grad_text = lax.psum_scatter(
        grad_text_full.astype(jnp.bfloat16), "mp", scatter_dimension=1, tiled=True
    )
    text_weight_grad = outer_sum(text_states, grad_text)
    text_bias_grad = jnp.sum(grad_text.astype(jnp.float32), axis=0)
    text_grad = lax.psum(against(grad_text, text_weight).astype(jnp.bfloat16), "mp").astype(
        jnp.float32
    )
    grad_cross_normed = input_grads(((grad_queries, cross_query),))
    grad_norm, cross_gain_grad, cross_shift_grad = norm_back(
        grad_cross_normed, cross_standard, cross_inverse, cross_gain
    )
    grad_middle = grad_after + grad_norm
    self_cotangent = spread_cotangent(grad_middle.astype(jnp.bfloat16))
    self_out_grad = outer_sum(self_context, self_cotangent)
    grad_context = against(self_cotangent, self_out).astype(jnp.bfloat16)
    grad_queries, grad_keys, grad_values = self_back(
        split_heads(self_queries, row_count),
        split_heads(self_keys, row_count),
        split_heads(self_values, row_count),
        clip_segs,
        self_logs,
        split_heads(grad_context, row_count),
    )
    grad_queries = grad_queries.reshape(self_queries.shape).astype(jnp.bfloat16)
    grad_keys = grad_keys.reshape(self_keys.shape).astype(jnp.bfloat16)
    grad_values = grad_values.reshape(self_values.shape).astype(jnp.bfloat16)
    self_query_grad = outer_sum(self_rows, grad_queries)
    self_key_grad = outer_sum(self_rows, grad_keys)
    self_value_grad = outer_sum(self_rows, grad_values)
    grad_self_normed = input_grads(
        ((grad_queries, self_query), (grad_keys, self_key), (grad_values, self_value))
    )
    grad_norm, self_gain_grad, self_shift_grad = norm_back(
        grad_self_normed, self_standard, self_inverse, self_gain
    )
    frames_grad = grad_middle + grad_norm
    (
        self_query_grad,
        self_key_grad,
        self_value_grad,
        self_out_grad,
        cross_query_grad,
        cross_key_grad,
        cross_value_grad,
        cross_out_grad,
        text_weight_grad,
        text_bias_grad,
        feed_in_grad,
        feed_out_grad,
    ) = (
        lax.psum(self_query_grad.astype(jnp.bfloat16), "dp").astype(jnp.float32),
        lax.psum(self_key_grad.astype(jnp.bfloat16), "dp").astype(jnp.float32),
        lax.psum(self_value_grad.astype(jnp.bfloat16), "dp").astype(jnp.float32),
        lax.psum(self_out_grad.astype(jnp.bfloat16), "dp").astype(jnp.float32),
        lax.psum(cross_query_grad.astype(jnp.bfloat16), "dp").astype(jnp.float32),
        lax.psum(cross_key_grad.astype(jnp.bfloat16), "dp").astype(jnp.float32),
        lax.psum(cross_value_grad.astype(jnp.bfloat16), "dp").astype(jnp.float32),
        lax.psum(cross_out_grad.astype(jnp.bfloat16), "dp").astype(jnp.float32),
        lax.psum(text_weight_grad.astype(jnp.bfloat16), "dp").astype(jnp.float32),
        lax.psum(text_bias_grad.astype(jnp.bfloat16), "dp").astype(jnp.float32),
        lax.psum(feed_in_grad.astype(jnp.bfloat16), "dp").astype(jnp.float32),
        lax.psum(feed_out_grad.astype(jnp.bfloat16), "dp").astype(jnp.float32),
    )
    (
        self_gain_grad,
        self_shift_grad,
        cross_gain_grad,
        cross_shift_grad,
        feed_gain_grad,
        feed_shift_grad,
    ) = lax.psum(
        (
            self_gain_grad,
            self_shift_grad,
            cross_gain_grad,
            cross_shift_grad,
            feed_gain_grad,
            feed_shift_grad,
        ),
        ("dp", "mp"),
    )
    return (
        output.astype(jnp.bfloat16),
        frames_grad,
        text_grad,
        self_gain_grad,
        self_shift_grad,
        self_query_grad,
        self_key_grad,
        self_value_grad,
        self_out_grad,
        cross_gain_grad,
        cross_shift_grad,
        cross_query_grad,
        cross_key_grad,
        cross_value_grad,
        cross_out_grad,
        text_weight_grad,
        text_bias_grad,
        feed_gain_grad,
        feed_shift_grad,
        feed_in_grad,
        feed_out_grad,
    )


LOG2E=1.4426950408889634
SCALE2=LOG2E*HEAD_DIM**-0.5
BQ=256
SPAN=768

def dot(a,b,ca,cb):
    return lax.dot_general(a,b,(((ca,),(cb,)),((),())),preferred_element_type=jnp.float32)

def starts_of(bounds_ref, places):
    start=jnp.zeros_like(places)
    for k in range(3):
        start=jnp.where(places>=bounds_ref[k],bounds_ref[k],start)
    return start

def self_fwd_kernel(bounds_ref,q_ref,k_ref,v_ref,o_ref,lse_ref,*,ahead=2):
    low=lax.broadcasted_iota(jnp.int32,(1,128),1)<HEAD_DIM
    vt=jnp.transpose(v_ref[...])
    pad=jnp.ones((16,ROW_LEN),jnp.bfloat16)
    vts=[jnp.concatenate([vt[64*h:64*h+64],pad],0) for h in range(2)]
    def span(i):
        return max(0,BQ*i-SPAN),BQ*(i+1)
    def scores(i,h):
        k0,k1=span(i)
        q=q_ref[BQ*i:k1,:]
        qh=jnp.where(low==(h==0),q,jnp.zeros_like(q))
        places=BQ*i+lax.broadcasted_iota(jnp.int32,(1,BQ),1)
        keys=k0+lax.broadcasted_iota(jnp.int32,(k1-k0,BQ),0)
        allowed=(keys>=starts_of(bounds_ref,places))&(keys<=places)
        return jnp.where(allowed,dot(k_ref[k0:k1,:],qh,1,1),MASKED)
    items=[(i,h) for i in range(ROW_LEN//BQ) for h in range(2)]
    queue=[scores(*it) for it in items[:ahead]]
    outs=[]
    for n,(i,h) in enumerate(items):
        if n+ahead<len(items):
            queue.append(scores(*items[n+ahead]))
        s=queue.pop(0)
        k0,k1=span(i)
        m=jnp.max(s,axis=0,keepdims=True)
        p=jnp.exp2((s-m)*SCALE2)
        o=dot(vts[h][:,k0:k1],p.astype(jnp.bfloat16),1,0)
        l=o[64:65]
        outs.append(o[:64]*(1.0/l))
        lse_ref[0,h:h+1,BQ*i:k1]=m*SCALE2+jnp.log2(l)
        if h==1:
            o_ref[BQ*i:k1,:]=jnp.transpose(jnp.concatenate(outs,0)).astype(jnp.bfloat16)
            outs=[]

def self_bwd_kernel(bounds_ref,q_ref,k_ref,v_ref,o_ref,g_ref,lse_ref,out_ref,acc_ref,d_ref,*,mode="t",ahead=1):
    low=lax.broadcasted_iota(jnp.int32,(1,128),1)<HEAD_DIM
    n=ROW_LEN//BQ
    pair=pl.program_id(0)
    width=128*pl.num_programs(0)
    def put(which,sl,t):
        at=pl.multiple_of(which*width+pair*128,128)
        out_ref[sl,pl.ds(at,128)]=t.astype(jnp.bfloat16)

    for i in range(n):
        sl=slice(BQ*i,BQ*(i+1))
        t=jnp.transpose(g_ref[sl,:].astype(jnp.float32)*o_ref[sl,:].astype(jnp.float32))
        d_ref[0:1,sl]=jnp.sum(t[:64],axis=0,keepdims=True)
        d_ref[1:2,sl]=jnp.sum(t[64:],axis=0,keepdims=True)
    acc_ref[...]=jnp.zeros_like(acc_ref)
    def span(j):
        return BQ*j,min(ROW_LEN,BQ*(j+1)+SPAN)
    def masked(ref,j,h):
        t=ref[BQ*j:BQ*(j+1),:]
        return jnp.where(low==(h==0),t,jnp.zeros_like(t))
    def scores(j,h):
        q0,q1=span(j)
        places=q0+lax.broadcasted_iota(jnp.int32,(1,q1-q0),1)
        keys=BQ*j+lax.broadcasted_iota(jnp.int32,(BQ,q1-q0),0)
        allowed=(keys>=starts_of(bounds_ref,places))&(keys<=places)
        s=dot(masked(k_ref,j,h),q_ref[q0:q1,:],1,1)*SCALE2-lse_ref[0,h:h+1,q0:q1]
        return jnp.where(allowed,s,MASKED),dot(masked(v_ref,j,h),g_ref[q0:q1,:],1,1)
    items=[(j,h) for j in range(n) for h in range(2)]
    queue=[scores(*it) for it in items[:ahead]]
    dks=[];dvs=[]
    for t,(j,h) in enumerate(items):
        if t+ahead<len(items):
            queue.append(scores(*items[t+ahead]))
        s,dp=queue.pop(0)
        sl=slice(BQ*j,BQ*(j+1))
        q0,q1=span(j)
        p=jnp.exp2(s)
        ds=(p*(dp-d_ref[h:h+1,q0:q1])).astype(jnp.bfloat16)
        dvs.append(dot(p.astype(jnp.bfloat16),g_ref[q0:q1,:],1,0))
        dks.append(dot(ds,q_ref[q0:q1,:],1,0))
        if mode=="t":
            kt=jnp.transpose(k_ref[sl,:])
            acc_ref[64*h:64*h+64,q0:q1]+=dot(kt[64*h:64*h+64],ds,1,0)
        else:
            acc_ref[q0:q1,:]+=dot(ds,masked(k_ref,j,h),0,0)
        if h==1:
            put(1,sl,jnp.where(low,dks[0],dks[1])*HEAD_DIM**-0.5)
            put(2,sl,jnp.where(low,dvs[0],dvs[1]))
            dks=[];dvs=[]
            acc=jnp.transpose(acc_ref[:,sl]) if mode=="t" else acc_ref[sl,:]
            put(0,sl,acc*HEAD_DIM**-0.5)


def group_forward(bounds,qkv):
    width=qkv.shape[1]//3
    pairs=width//128
    spec=lambda t: pl.BlockSpec((ROW_LEN,128),lambda h:(0,t*pairs+h))
    return pl.pallas_call(self_fwd_kernel,grid=(pairs,),
        in_specs=[pl.BlockSpec(memory_space=pltpu.SMEM),spec(0),spec(1),spec(2)],
        out_specs=[spec(0),pl.BlockSpec((1,2,ROW_LEN),lambda h:(h,0,0))],
        out_shape=[jax.ShapeDtypeStruct((ROW_LEN,width),jnp.bfloat16),jax.ShapeDtypeStruct((pairs,2,ROW_LEN),jnp.float32)],
        compiler_params=pltpu.CompilerParams(vmem_limit_bytes=40<<20),
        name="self_forward",
        cost_estimate=pl.CostEstimate(flops=pairs*2*18*256*256*64*4*4,bytes_accessed=pairs*4*1536*256,transcendentals=0),
    )(bounds,qkv,qkv,qkv)

def group_backward(bounds,qkv,o,g,lse,group):
    width=qkv.shape[1]//3
    pairs=width//128
    spec=lambda t: pl.BlockSpec((ROW_LEN,128),lambda h:(0,t*pairs+h))
    return pl.pallas_call(self_bwd_kernel,grid=(pairs,),
        in_specs=[pl.BlockSpec(memory_space=pltpu.SMEM),spec(0),spec(1),spec(2),spec(0),spec(group),pl.BlockSpec((1,2,ROW_LEN),lambda h:(h,0,0))],
        out_specs=pl.BlockSpec((ROW_LEN,3*width),lambda h:(0,0)),
        out_shape=jax.ShapeDtypeStruct(qkv.shape,jnp.bfloat16),
        scratch_shapes=[pltpu.VMEM((128,ROW_LEN),jnp.float32),pltpu.VMEM((8,ROW_LEN),jnp.float32)],
        compiler_params=pltpu.CompilerParams(vmem_limit_bytes=48<<20),
        name="self_backward",
        cost_estimate=pl.CostEstimate(flops=pairs*2*18*256*256*64*10*4,bytes_accessed=pairs*8*1536*256,transcendentals=0),
    )(bounds,qkv,qkv,qkv,o,g,lse)

def token_range(cb_ref,tb_ref,places):
    lo=jnp.zeros_like(places); hi=jnp.full_like(places,0)+tb_ref[0]
    for c in range(3):
        past=places>=cb_ref[c]
        lo=jnp.where(past,tb_ref[c],lo)
        hi=jnp.where(past,tb_ref[c+1],hi)
    return lo,hi


INV_SQRT_2PI = 0.3989422804014327
TB = 256
NB = 512


def mean_row(t):
    return jnp.sum(t, axis=-1, keepdims=True) * (1.0 / t.shape[-1])


def standardise(t):
    centered = t - mean_row(t)
    inverse = lax.rsqrt(mean_row(centered * centered) + EPSILON)
    return centered * inverse, inverse


def norm_input_grad(e, standard, inverse, gain):
    scaled = e * gain
    return inverse * (scaled - mean_row(scaled) - standard * mean_row(scaled * standard))


def column_sums(t):
    return jnp.sum(t, axis=0, keepdims=True)


def gelu_pair(hidden):
    density = jnp.exp2(hidden * hidden * (-0.5 * LOG2E)) * INV_SQRT_2PI
    t = 1.0 / (1.0 + 0.2316419 * jnp.abs(hidden))
    series = t * (
        0.319381530
        + t * (-0.356563782 + t * (1.781477937 + t * (-1.821255978 + t * 1.330274429)))
    )
    tail = density * series
    below = jnp.where(hidden >= 0, 1.0 - tail, tail)
    return hidden * below, below + hidden * density


def mid_forward_kernel(
    count, cb_ref, tb_ref, x_ref, *refs,
):
    ctxs, sos, cqs, cos = [refs[count * t : count * t + count] for t in range(4)]
    (k_ref, v_ref, vec_ref,
     mid_ref, rows_ref, q_ref, cctx_ref, lse_ref, after_ref, feed_ref, feedt_ref, vt_ref) = refs[4 * count :]
    i = pl.program_id(0)
    low = lax.broadcasted_iota(jnp.int32, (1, 128), 1) < HEAD_DIM

    @pl.when(i == 0)
    def _():
        vt_ref[0:1024, :] = jnp.transpose(v_ref[...])
        vt_ref[1024:1040, :] = jnp.ones((16, TXT_ROW), jnp.bfloat16)

    middle = x_ref[...].astype(jnp.float32)
    for c, w in zip(ctxs, sos):
        middle = middle + dot(c[...], w[...], 1, 0)
    mid_ref[...] = middle
    u, _ = standardise(middle)
    rows = (u * vec_ref[0:1, :] + vec_ref[1:2, :]).astype(jnp.bfloat16)
    rows_ref[...] = rows
    at = 0
    for w in cqs:
        n = w.shape[1]
        q_ref[:, at : at + n] = dot(rows, w[...], 1, 0).astype(jnp.bfloat16)
        at += n
    places = TB * i + lax.broadcasted_iota(jnp.int32, (1, TB), 1)
    lo, hi = token_range(cb_ref, tb_ref, places)
    toks = lax.broadcasted_iota(jnp.int32, (TXT_ROW, TB), 0)
    allowed = (toks >= lo) & (toks < hi)

    def scores(head):
        p, h = head // 2, head % 2
        k = k_ref[:, 128 * p : 128 * p + 128]
        kh = jnp.where(low == (h == 0), k, jnp.zeros_like(k))
        return jnp.where(allowed, dot(kh, q_ref[:, 128 * p : 128 * p + 128], 1, 1), MASKED)

    ahead = 3
    queue = [scores(t) for t in range(ahead)]
    outs = []
    ones = vt_ref[1024:1040, :]
    for head in range(16):
        if head + ahead < 16:
            queue.append(scores(head + ahead))
        s = queue.pop(0)
        m = jnp.max(s, axis=0, keepdims=True)
        p = jnp.exp2((s - m) * SCALE2)
        vt = jnp.concatenate([vt_ref[64 * head : 64 * head + 64, :], ones], 0)
        o = dot(vt, p.astype(jnp.bfloat16), 1, 0)
        l = o[64:65]
        outs.append(o[:64] * (1.0 / l))
        lse_ref[head : head + 1, :] = m * SCALE2 + jnp.log2(l)
        if head % 2 == 1:
            pair = head // 2
            cctx_ref[:, 128 * pair : 128 * pair + 128] = jnp.transpose(
                jnp.concatenate(outs, 0)
            ).astype(jnp.bfloat16)
            outs = []
    after = mid_ref[...]
    at = 0
    for w in cos:
        n = w.shape[0]
        after = after + dot(cctx_ref[:, at : at + n], w[...], 1, 0)
        at += n
    after_ref[...] = after
    u, _ = standardise(after)
    feed = (u * vec_ref[2:3, :] + vec_ref[3:4, :]).astype(jnp.bfloat16)
    feed_ref[...] = feed
    feedt_ref[...] = jnp.transpose(feed)


def row_block(n):
    return pl.BlockSpec((TB, n), lambda i: (i, 0))


def whole(t):
    return pl.BlockSpec(t.shape, lambda i: (0,) * t.ndim)


def mid_forward(cb, tb, x, ctxs, sos, cqs, cos, k, v, vec):
    n, d = x.shape
    smem = pl.BlockSpec(memory_space=pltpu.SMEM)
    bf, f = jnp.bfloat16, jnp.float32
    weights = [*sos, *cqs, *cos, k, v, vec]
    return pl.pallas_call(
        functools.partial(mid_forward_kernel, len(ctxs)),
        grid=(n // TB,),
        in_specs=[smem, smem, row_block(d)] + [row_block(c.shape[1]) for c in ctxs] + [whole(w) for w in weights],
        out_specs=[row_block(d)] * 4
        + [pl.BlockSpec((16, TB), lambda i: (0, i))]
        + [row_block(d)] * 2
        + [pl.BlockSpec((d, TB), lambda i: (0, i))],
        out_shape=[jax.ShapeDtypeStruct((n, d), t) for t in (f, bf, bf, bf)]
        + [jax.ShapeDtypeStruct((16, n), f)]
        + [jax.ShapeDtypeStruct((n, d), t) for t in (f, bf)]
        + [jax.ShapeDtypeStruct((d, n), bf)],
        scratch_shapes=[pltpu.VMEM((1040, TXT_ROW), bf)],
        compiler_params=pltpu.CompilerParams(vmem_limit_bytes=56 << 20),
        name="mid_forward",
        cost_estimate=pl.CostEstimate(flops=24 * n * d * d // 2, bytes_accessed=40 * n * d // 2, transcendentals=0),
    )(cb, tb, x, *ctxs, *weights)


def mid_backward_kernel(
    count, cb_ref, tb_ref, e_ref, after_ref, g_ref, mid_ref, q_ref, cctx_ref, lse_ref, *refs,
):
    cos, cqs, sos = [refs[count * t : count * t + count] for t in range(3)]
    (k_ref, v_ref, vec_ref,
     gc_ref, gq_ref, gmid_ref, gs_ref, gctx_ref, dk_ref, dv_ref, sums_ref,
     kt_ref, dka_ref, dva_ref, gcc_ref) = refs[3 * count :]
    i = pl.program_id(0)
    low = lax.broadcasted_iota(jnp.int32, (1, 128), 1) < HEAD_DIM

    @pl.when(i == 0)
    def _():
        kt_ref[...] = jnp.transpose(k_ref[...])
        dka_ref[...] = jnp.zeros_like(dka_ref)
        dva_ref[...] = jnp.zeros_like(dva_ref)
        sums_ref[...] = jnp.zeros_like(sums_ref)

    e = e_ref[...]
    u, inverse = standardise(after_ref[...])
    sums_ref[0:1, :] += column_sums(e * u)
    sums_ref[1:2, :] += column_sums(e)
    g_after = g_ref[...].astype(jnp.float32) + norm_input_grad(e, u, inverse, vec_ref[2:3, :])
    gmid_ref[...] = g_after
    gc = g_after.astype(jnp.bfloat16)
    gc_ref[...] = gc
    at = 0
    for w in cos:
        n = w.shape[0]
        gcc_ref[:, at : at + n] = dot(gc, w[...], 1, 1).astype(jnp.bfloat16)
        at += n
    places = TB * i + lax.broadcasted_iota(jnp.int32, (1, TB), 1)
    lo, hi = token_range(cb_ref, tb_ref, places)
    toks = lax.broadcasted_iota(jnp.int32, (TXT_ROW, TB), 0)
    allowed = (toks >= lo) & (toks < hi)

    def scores(head):
        p, h = head // 2, head % 2
        sl = slice(128 * p, 128 * p + 128)
        pick = lambda t: jnp.where(low == (h == 0), t, jnp.zeros_like(t))
        s = dot(pick(k_ref[:, sl]), q_ref[:, sl], 1, 1) * SCALE2 - lse_ref[head : head + 1, :]
        return jnp.where(allowed, s, MASKED), dot(pick(v_ref[:, sl]), gcc_ref[:, sl], 1, 1)

    ahead = 2
    queue = [scores(t) for t in range(ahead)]
    dqs, dks, dvs = [], [], []
    for head in range(16):
        if head + ahead < 16:
            queue.append(scores(head + ahead))
        p_at, h = head // 2, head % 2
        sl = slice(128 * p_at, 128 * p_at + 128)
        if h == 0:
            t = jnp.transpose(
                gcc_ref[:, sl].astype(jnp.float32) * cctx_ref[:, sl].astype(jnp.float32)
            )
        s, dp = queue.pop(0)
        p = jnp.exp2(s)
        ds = (p * (dp - column_sums(t[64 * h : 64 * h + 64]))).astype(jnp.bfloat16)
        dvs.append(dot(p.astype(jnp.bfloat16), gcc_ref[:, sl], 1, 0))
        dks.append(dot(ds, q_ref[:, sl], 1, 0))
        dqs.append(dot(kt_ref[64 * head : 64 * head + 64, :], ds, 1, 0))
        if h == 1:
            gq_ref[:, sl] = (
                jnp.transpose(jnp.concatenate(dqs, 0)) * HEAD_DIM**-0.5
            ).astype(jnp.bfloat16)
            dka_ref[:, sl] += jnp.where(low, dks[0], dks[1])
            dva_ref[:, sl] += jnp.where(low, dvs[0], dvs[1])
            dqs, dks, dvs = [], [], []
    e = None
    at = 0
    for w in cqs:
        n = w.shape[1]
        part = dot(gq_ref[:, at : at + n], w[...], 1, 1)
        e = part if e is None else e + part
        at += n
    u, inverse = standardise(mid_ref[...])
    sums_ref[2:3, :] += column_sums(e * u)
    sums_ref[3:4, :] += column_sums(e)
    g_middle = gmid_ref[...] + norm_input_grad(e, u, inverse, vec_ref[0:1, :])
    gmid_ref[...] = g_middle
    gs = g_middle.astype(jnp.bfloat16)
    gs_ref[...] = gs
    at = 0
    for w in sos:
        n = w.shape[0]
        gctx_ref[:, at : at + n] = dot(gs, w[...], 1, 1).astype(jnp.bfloat16)
        at += n

    @pl.when(i == pl.num_programs(0) - 1)
    def _():
        dk_ref[...] = (dka_ref[...] * HEAD_DIM**-0.5).astype(jnp.bfloat16)
        dv_ref[...] = dva_ref[...].astype(jnp.bfloat16)


def mid_backward(cb, tb, e, after, g, middle, q, cctx, lse, cos, cqs, sos, k, v, vec):
    n, d = after.shape
    smem = pl.BlockSpec(memory_space=pltpu.SMEM)
    bf, f = jnp.bfloat16, jnp.float32
    weights = [*cos, *cqs, *sos, k, v, vec]
    text = jax.ShapeDtypeStruct((TXT_ROW, d), bf)
    sums = jax.ShapeDtypeStruct((8, d), f)
    return pl.pallas_call(
        functools.partial(mid_backward_kernel, len(cos)),
        grid=(n // TB,),
        in_specs=[smem, smem] + [row_block(d)] * 6 + [pl.BlockSpec((16, TB), lambda i: (0, i))] + [whole(w) for w in weights],
        out_specs=[row_block(d)] * 5 + [whole(text), whole(text), whole(sums)],
        out_shape=[jax.ShapeDtypeStruct((n, d), t) for t in (bf, bf, f, bf, bf)] + [text, text, sums],
        scratch_shapes=[
            pltpu.VMEM((d, TXT_ROW), bf),
            pltpu.VMEM((TXT_ROW, d), f),
            pltpu.VMEM((TXT_ROW, d), f),
            pltpu.VMEM((TB, d), bf),
        ],
        compiler_params=pltpu.CompilerParams(vmem_limit_bytes=58 << 20),
        name="mid_backward",
        cost_estimate=pl.CostEstimate(flops=40 * n * d * d // 2, bytes_accessed=46 * n * d // 2, transcendentals=0),
    )(cb, tb, e, after, g, middle, q, cctx, lse, *weights)


def feed_kernel(idx_ref, fr_ref, frt_ref, cot_ref, o_in, e_in, *refs, own, first, last):
    if own:
        fi_src, fo_src = refs[:2]
        refs = refs[2:]
    else:
        fi_srcs, fo_srcs = refs[:2], refs[2:4]
        refs = refs[4:]
    o_out, e_out, gi_ref, go_ref, acc_o, acc_e, fi_buf, fo_buf, act_s, gh_s, wsem, asem = refs
    p = pl.program_id(0)
    slot = p % 2

    def weights(step, into, act):
        if own:
            at = pl.multiple_of(idx_ref[step] * NB, NB)
            act(pltpu.make_async_copy(fi_src.at[:, pl.ds(at, NB)], fi_buf.at[into], wsem.at[into, 0]))
            act(pltpu.make_async_copy(fo_src.at[pl.ds(at, NB), :], fo_buf.at[into], wsem.at[into, 1]))
        else:
            for s in range(2):
                @pl.when(step == s)
                def _(s=s):
                    act(pltpu.make_async_copy(fi_srcs[s], fi_buf.at[into], wsem.at[into, 0]))
                    act(pltpu.make_async_copy(fo_srcs[s], fo_buf.at[into], wsem.at[into, 1]))

    o_load = pltpu.make_async_copy(o_in, acc_o, asem.at[0])
    if not first:
        e_load = pltpu.make_async_copy(e_in, acc_e, asem.at[1])

    @pl.when(p == 0)
    def _():
        weights(p, slot, lambda c: c.start())
        o_load.start()
        if not first:
            e_load.start()
        else:
            acc_e[...] = jnp.zeros_like(acc_e)

    weights(p, slot, lambda c: c.wait())

    @pl.when(p == 0)
    def _():
        weights(p + 1, 1 - slot, lambda c: c.start())

    @pl.when(p == 0)
    def _():
        o_load.wait()
        if not first:
            e_load.wait()

    fi, fo = fi_buf.at[slot], fo_buf.at[slot]
    rows = 256
    blocks = fr_ref.shape[0] // rows

    def products(r):
        sl = slice(rows * r, rows * r + rows)
        return dot(fr_ref[sl, :], fi[...], 1, 0), dot(cot_ref[sl, :], fo[...], 1, 1)

    ahead = 1
    queue = [products(r) for r in range(ahead)]
    for r in range(blocks):
        if r + ahead < blocks:
            queue.append(products(r + ahead))
        h, g = queue.pop(0)
        sl = slice(rows * r, rows * r + rows)
        active, slope = gelu_pair(h)
        active = active.astype(jnp.bfloat16)
        gh = (g * slope).astype(jnp.bfloat16)
        act_s[sl, :] = active
        gh_s[sl, :] = gh
        acc_o[sl, :] += dot(active, fo[...], 1, 0)
        acc_e[sl, :] += dot(gh, fi[...], 1, 1)
    gi_ref[...] = dot(frt_ref[...], gh_s[...], 1, 0).astype(jnp.bfloat16)
    go_ref[...] = dot(act_s[...], cot_ref[...], 0, 0).astype(jnp.bfloat16)

    @pl.when(p == 1)
    def _():
        e_store = pltpu.make_async_copy(acc_e, e_out, asem.at[1])
        e_store.start()
        if last:
            o_out[...] = acc_o[...].astype(jnp.bfloat16)
        else:
            o_store = pltpu.make_async_copy(acc_o, o_out, asem.at[0])
            o_store.start()
            o_store.wait()
        e_store.wait()


def feed_part(idx, rows, rows_t, cot, o_in, e_in, fis, fos, first, last):
    n, d = rows.shape
    own = len(fis) == 1
    bf, f = jnp.bfloat16, jnp.float32
    hbm = pl.BlockSpec(memory_space=pl.ANY)
    once = lambda shape: pl.BlockSpec(shape, lambda p, idx: (0, 0), pipeline_mode=pl.Buffered(1))
    grad = lambda shape: jax.ShapeDtypeStruct(shape, bf)
    return pl.pallas_call(
        functools.partial(feed_kernel, own=own, first=first, last=last),
        grid_spec=pltpu.PrefetchScalarGridSpec(
            num_scalar_prefetch=1,
            grid=(2,),
            in_specs=[once((n, d)), once((d, n)), once((n, d))] + [hbm] * (2 + 2 * len(fis)),
            out_specs=[
                once((n, d)) if last else hbm,
                hbm,
                pl.BlockSpec((d, NB), lambda p, idx: (0, idx[p] % 2)),
                pl.BlockSpec((NB, d), lambda p, idx: (idx[p] % 2, 0)),
            ],
            scratch_shapes=[
                pltpu.VMEM((n, d), f),
                pltpu.VMEM((n, d), f),
                pltpu.VMEM((2, d, NB), bf),
                pltpu.VMEM((2, NB, d), bf),
                pltpu.VMEM((n, NB), bf),
                pltpu.VMEM((n, NB), bf),
                pltpu.SemaphoreType.DMA((2, 2)),
                pltpu.SemaphoreType.DMA((2,)),
            ],
        ),
        out_shape=[
            jax.ShapeDtypeStruct((n, d), bf if last else f),
            jax.ShapeDtypeStruct((n, d), f),
            grad((d, 2 * NB)),
            grad((2 * NB, d)),
        ],
        compiler_params=pltpu.CompilerParams(vmem_limit_bytes=60 << 20),
        name="feed_last" if last else "feed_first" if first else "feed_more",
        cost_estimate=pl.CostEstimate(flops=24 * n * d * NB, bytes_accessed=48 << 20, transcendentals=0),
    )(idx, rows, rows_t, cot, o_in, e_in, *fis, *fos)


def final_kernel(x_ref, gmid_ref, *refs):
    count = (len(refs) - 3) // 2
    gs, ws = refs[:count], refs[count : 2 * count]
    vec_ref, out_ref, sums_ref = refs[2 * count :]

    @pl.when(pl.program_id(0) == 0)
    def _():
        sums_ref[...] = jnp.zeros_like(sums_ref)

    e = None
    for g, w in zip(gs, ws):
        part = dot(g[...], w[...], 1, 1)
        e = part if e is None else e + part
    u, inverse = standardise(x_ref[...].astype(jnp.float32))
    sums_ref[0:1, :] += column_sums(e * u)
    sums_ref[1:2, :] += column_sums(e)
    out_ref[...] = gmid_ref[...] + norm_input_grad(e, u, inverse, vec_ref[4:5, :])


def final_grads(x, gmid, gs, ws, vec):
    n, d = x.shape
    sums = jax.ShapeDtypeStruct((8, d), jnp.float32)
    return pl.pallas_call(
        final_kernel,
        grid=(n // TB,),
        in_specs=[row_block(d), row_block(d)] + [row_block(g.shape[1]) for g in gs] + [whole(w) for w in ws] + [whole(vec)],
        out_specs=[row_block(d), whole(sums)],
        out_shape=[jax.ShapeDtypeStruct((n, d), jnp.float32), sums],
        compiler_params=pltpu.CompilerParams(vmem_limit_bytes=56 << 20),
        name="frames_gradient",
        cost_estimate=pl.CostEstimate(flops=6 * n * d * d, bytes_accessed=24 * n * d // 2, transcendentals=0),
    )(x, gmid, *gs, *ws, vec)


def pair_at(b):
    return (b % 2) * 4 + (b // 2) % 2 * 2 + b // 4


def spread_feed_kernel(t_ref, in_ref, out_ref):
    n = in_ref.shape[1] // 2
    for c in range(2):
        in_ref[:, n * c : n * c + n] = t_ref[c, :, :n].astype(jnp.float32)
        out_ref[c] = t_ref[c, :, n:].astype(jnp.float32)


def spread_feed(t):
    _, rows, columns = t.shape
    n = columns // 2
    f = jnp.float32
    return pl.pallas_call(
        spread_feed_kernel,
        grid=(8,),
        in_specs=[pl.BlockSpec((2, rows, columns), lambda b: (pair_at(b), 0, 0))],
        out_specs=[
            pl.BlockSpec((rows, 2 * n), lambda b: (b, 0)),
            pl.BlockSpec((2, rows, n), lambda b: (0, b, 0)),
        ],
        out_shape=[
            jax.ShapeDtypeStruct((8 * rows, 2 * n), f),
            jax.ShapeDtypeStruct((2, 8 * rows, n), f),
        ],
        compiler_params=pltpu.CompilerParams(vmem_limit_bytes=32 << 20),
        name="spread_feed",
        cost_estimate=pl.CostEstimate(flops=0, bytes_accessed=6 * t.size, transcendentals=0),
    )(t)


def spread_rest_kernel(t_ref, *refs):
    cq, co, so, ck, cv, tw, q, k, v, tb = refs
    n = cq.shape[1] // 2
    b = pl.program_id(0)

    def both(i):
        return jnp.concatenate(
            [t_ref[c, :, n * i : n * i + n].astype(jnp.float32) for c in range(2)], 1
        )

    for i, ref in ((0, cq), (3, ck), (4, cv), (6, q), (7, k), (8, v)):
        ref[...] = both(i)
    co[...] = jnp.transpose(both(1))
    so[...] = jnp.transpose(both(2))

    @pl.when(b < 6)
    def _():
        tw[...] = both(5)

    @pl.when(b == 6)
    def _():
        tb[...] = both(5)[0:8]


def spread_rest(t, n):
    rows = t.shape[1]
    f = jnp.float32
    wide = pl.BlockSpec((rows, 2 * n), lambda b: (b, 0))
    turned = pl.BlockSpec((2 * n, rows), lambda b: (0, b))
    square = jax.ShapeDtypeStruct((8 * rows, 2 * n), f)
    tall = jax.ShapeDtypeStruct((2 * n, 8 * rows), f)
    return pl.pallas_call(
        spread_rest_kernel,
        grid=(8,),
        in_specs=[pl.BlockSpec((2,) + t.shape[1:], lambda b: (pair_at(b), 0, 0))],
        out_specs=[wide, turned, turned, wide, wide, pl.BlockSpec((rows, 2 * n), lambda b: (jnp.minimum(b, 5), 0))]
        + [wide] * 3
        + [pl.BlockSpec((8, 2 * n), lambda b: (0, 0))],
        out_shape=[square, tall, tall, square, square, jax.ShapeDtypeStruct((6 * rows, 2 * n), f)]
        + [square] * 3
        + [jax.ShapeDtypeStruct((8, 2 * n), f)],
        compiler_params=pltpu.CompilerParams(vmem_limit_bytes=32 << 20),
        name="spread_rest",
        cost_estimate=pl.CostEstimate(flops=0, bytes_accessed=6 * t.size, transcendentals=0),
    )(t)


class Journey:
    def __init__(self, hops):
        self.hops = hops
        self.pending = next(hops)
        self.result = None

    def go(self, tied):
        try:
            self.pending = self.hops.send(tied)
        except StopIteration as end:
            self.pending, self.result = None, end.value


def onward(main, *journeys):
    journeys = [j for j in journeys if j.result is None]
    main, tied = lax.optimization_barrier((main, [j.pending for j in journeys]))
    for journey, sent in zip(journeys, tied):
        journey.go(sent)
    return main


def row_body(dp, *args):
    (
        frames,
        text_states,
        clip_lengths,
        text_lengths,
        cotangent,
        self_gain,
        self_shift,
        self_query,
        self_key,
        self_value,
        self_out,
        cross_gain,
        cross_shift,
        cross_query,
        cross_key,
        cross_value,
        cross_out,
        text_weight,
        text_bias,
        feed_gain,
        feed_shift,
        feed_in,
        feed_out,
    ) = args
    bf16, f32 = jnp.bfloat16, jnp.float32
    me = lax.axis_index("dp")
    half = lax.axis_index("mp")
    core = me % 2
    swap = [(0, 1), (1, 0)]
    steps = [2 << i for i in range(dp.bit_length() - 2)]

    def over_y(t):
        return jax.tree.map(lambda a: lax.ppermute(a, "mp", swap), t)

    def over_bit(t, step):
        return jax.tree.map(lambda a: lax.ppermute(a, "dp", [(i, i ^ step) for i in range(dp)]), t)

    def over_core(t):
        return over_bit(t, 1)

    def piece(t, at, size, axis):
        return lax.dynamic_slice_in_dim(t, at * size, size, axis)

    def ordered(mine_first, mine, theirs, axis):
        return jnp.concatenate(
            [jnp.where(mine_first, mine, theirs), jnp.where(mine_first, theirs, mine)], axis
        )

    def add(*ts):
        return reduce(jnp.add, [t.astype(f32) for t in ts]).astype(bf16)

    def parts_of(ts, step):
        at = (me // step) % 2
        size = ts[0].shape[0] // 2
        return [add(*[piece(t, w, size, 0) for t in ts]) for w in (at, 1 - at)]

    def travel(terms, left):
        for step in left:
            kept, sent = parts_of(terms, step)
            sent = yield sent
            terms = (kept, over_bit(sent, step))
        return add(*terms)

    def travel_y(own, other):
        other = yield other
        return (yield from travel((*own, over_y(other)), steps))

    def travel_small(t):
        for hop in (over_core, over_y, *[functools.partial(over_bit, step=s) for s in steps]):
            t = yield t
            t = t + hop(t)
        return t

    lengths = lax.dynamic_index_in_dim(clip_lengths, half, 0, keepdims=False)
    words = lax.dynamic_index_in_dim(text_lengths, half, 0, keepdims=False)
    clip_bounds, text_bounds = jnp.cumsum(lengths), jnp.cumsum(words)
    zeros = jnp.zeros_like(self_gain)
    vec = jnp.stack(
        [cross_gain, cross_shift, feed_gain, feed_shift, self_gain, zeros, zeros, zeros]
    )

    def quarter(t, which, axis):
        return piece(t, which, t.shape[axis] // 2, axis)

    tie = lax.optimization_barrier
    x_at = (me // 2) % 2

    def shared(mine, axis):
        return quarter(mine, x_at, axis)

    def joined(came, across, axis):
        return ordered(x_at == 0, came, across, axis)

    trio = (self_query, self_key, self_value)
    qkv_c = jnp.concatenate([quarter(t, core, 1) for t in trio], 1)
    qkv_d = jnp.concatenate([quarter(t, 1 - core, 1) for t in trio], 1)
    text_part = (product(text_states, text_weight) + text_bias).astype(bf16)
    qkv_half = shared(qkv_c, 0)
    cut = qkv_half.shape[0] // 2
    frames, text_part, qkv_1, qkv_2 = tie((frames, text_part, qkv_half[:cut], qkv_half[cut:]))
    text_came, qkv_1 = over_y(text_part), over_y(qkv_1)
    standard, _ = norm_parts(frames.astype(f32))
    self_rows = (standard * self_gain + self_shift).astype(bf16)
    qkv, ctx, log = [None] * 4, [None] * 4, [None] * 4
    qkv[0] = product(self_rows, qkv_c).astype(bf16)
    qkv[2] = product(self_rows, qkv_d).astype(bf16)
    qkv[0], qkv[2], text_came, qkv_1, qkv_2 = tie((qkv[0], qkv[2], text_came, qkv_1, qkv_2))
    text_full = ordered(half == 0, text_part, text_came, 1)
    keys_here = product(text_full, cross_key).astype(bf16)
    values_here = product(text_full, cross_value).astype(bf16)
    text_rows = TXT_ROW

    def row_of(t, which):
        return piece(t, which, text_rows, 0)

    kv_send = jnp.concatenate([row_of(keys_here, 1 - half), row_of(values_here, 1 - half)], 1)
    qkv_2, across_1 = over_y(qkv_2), over_bit(qkv_1, 2)
    ctx[0], log[0] = group_forward(clip_bounds, qkv[0])
    so_c, cq_c, co_c = quarter(self_out, core, 0), quarter(cross_query, core, 1), quarter(cross_out, core, 0)
    late = [shared(so_c, 0), shared(cq_c, 0), shared(co_c, 0)]
    ctx[0], qkv[2], qkv_2, across_1, kv_send, late = tie(
        (ctx[0], qkv[2], qkv_2, across_1, kv_send, late)
    )
    across_2 = over_bit(qkv_2, 2)
    kv_came = over_y(kv_send)
    so_h = over_y(late[0])
    ctx[2], log[2] = group_forward(clip_bounds, qkv[2])
    ctx[2], across_2, kv_came, so_h = tie((ctx[2], across_2, kv_came, so_h))
    qkv_oc = joined(jnp.concatenate([qkv_1, qkv_2]), jnp.concatenate([across_1, across_2]), 0)
    qkv_oc, rows_1, so_h = tie((qkv_oc, self_rows, so_h))
    qkv_od = over_core(qkv_oc)
    cq_h, so_x = over_y(late[1]), over_bit(so_h, 2)
    qkv[1] = product(rows_1, qkv_oc).astype(bf16)
    qkv[1], cq_h = tie((qkv[1], cq_h))
    co_h, cq_x = over_y(late[2]), over_bit(cq_h, 2)
    ctx[1], log[1] = group_forward(clip_bounds, qkv[1])
    qkv[3] = product(self_rows, qkv_od).astype(bf16)
    so_oc, cq_oc = joined(so_h, so_x, 0), joined(cq_h, cq_x, 0)
    qkv[3], ctx[1], co_h, so_oc, cq_oc = tie((qkv[3], ctx[1], co_h, so_oc, cq_oc))
    co_x = over_bit(co_h, 2)
    so_od, cq_od = over_core(so_oc), over_core(cq_oc)
    ctx[3], log[3] = group_forward(clip_bounds, qkv[3])
    co_oc = joined(co_h, co_x, 0)
    co_od = over_core(co_oc)
    width = cross_key.shape[1]

    def mixed(mine, theirs):
        mine = row_of(mine, half)
        return jnp.concatenate(
            [quarter(t, w, 1) for w in (core, 1 - core) for t in (mine, theirs)], 1
        )

    keys = mixed(keys_here, kv_came[:, :width])
    values = mixed(values_here, kv_came[:, width:])
    qkv_w = [qkv_c, qkv_oc, qkv_d, qkv_od]
    so = [so_c, so_oc, quarter(self_out, 1 - core, 0), so_od]
    cq = [cq_c, cq_oc, quarter(cross_query, 1 - core, 1), cq_od]
    co = [co_c, co_oc, quarter(cross_out, 1 - core, 0), co_od]
    block = 2 * core + x_at
    fi_s, fo_s = piece(feed_in, block, NB, 1), piece(feed_out, block, NB, 0)
    ctx, so, cq, co, keys, values, fi_s, fo_s = tie((ctx, so, cq, co, keys, values, fi_s, fo_s))
    fi_cx = over_y(fi_s)

    middle, cross_rows, cross_q, cross_ctx, cross_log, after, feed_rows, feed_t = mid_forward(
        clip_bounds, text_bounds, frames, ctx, so, cq, co, keys, values, vec
    )

    feed = (feed_rows, feed_t, cotangent)
    places = lambda *t: jnp.stack(t).astype(jnp.int32)
    feed, fi_cx, fo_s = tie((feed, fi_cx, fo_s))
    fo_cx, fi_cy = over_y(fo_s), over_bit(fi_cx, 2)
    o, e, in_od, out_od = feed_part(
        places(2 - 2 * core, 3 - 2 * core), *feed, after, after, [feed_in], [feed_out], True, False
    )
    o, e, fo_cx, fi_cy = tie((o, e, fo_cx, fi_cy))
    fo_cy = over_bit(fo_cx, 2)
    fi_d = over_core([fi_cx, fi_cy])
    o, e, in_oc, out_oc = feed_part(
        places(2 * core, 2 * core + 1), *feed, o, e, [feed_in], [feed_out], False, False
    )
    o, e, fo_cy, fi_d = tie((o, e, fo_cy, fi_d))
    fo_d = over_core([fo_cx, fo_cy])
    o, e, fo_d, in_od, out_od = tie((o, e, fo_d, in_od, out_od))
    in_og, out_og = over_core([in_od, out_od])
    where = places(x_at, 1 - x_at)
    o, e, in_td, out_td = feed_part(where, *feed, o, e, fi_d, fo_d, False, False)
    o, e, in_og, in_td, out_td = tie((o, e, in_og, in_td, out_td))
    own_low, own_high = parts_of((in_oc, in_og), 2)
    o, e, own_low, own_high = tie((o, e, own_low, own_high))
    in_tg, out_tg = over_core([in_td, out_td])
    own_came = over_bit(own_high, 2)
    output, e, in_tc, out_tc = feed_part(
        where, *feed, o, e, [fi_cx, fi_cy], [fo_cx, fo_cy], False, True
    )
    e, in_tg, out_tg, own_came = tie((e, in_tg, out_tg, own_came))
    other_low, other_high = parts_of((in_tc, in_tg), 2)

    def travel_in():
        sent = yield other_high
        other = yield add(other_low, over_bit(sent, 2))
        return (yield from travel((own_low, own_came, over_y(other)), steps[1:]))

    j_in = Journey(travel_in())
    middle_cut = out_tc.shape[1] // 2
    j_out = []
    for sl in (slice(0, middle_cut), slice(middle_cut, None)):
        j_out.append(
            Journey(
                travel_y((out_oc[:, sl], out_og[:, sl]), add(out_tc[:, sl], out_tg[:, sl]))
            )
        )
    e = onward(e, j_in, j_out[0])

    g_c, grad_q, g_middle, g_s, grad_ctx, grad_k, grad_v, sums = mid_backward(
        clip_bounds,
        text_bounds,
        e,
        after,
        cotangent,
        middle,
        cross_q,
        cross_ctx,
        cross_log,
        co,
        cq,
        so,
        keys,
        values,
        vec,
    )
    small = Journey(travel_small(sums[:4]))
    side = width

    def split_heads_back(t):
        oc, tc, od, td = [t[:, side // 2 * n : side // 2 * (n + 1)] for n in range(4)]
        return ordered(core == 0, oc, od, 1), ordered(core == 0, tc, td, 1)

    dk_own, dk_other = split_heads_back(grad_k)
    dv_own, dv_other = split_heads_back(grad_v)
    g_c, text_hop = tie((g_c, jnp.concatenate([dk_other, dv_other], 1)))
    text_hop = over_y(text_hop)
    (g_c, grad_q, g_s, grad_ctx) = onward(
        (g_c, grad_q, g_s, grad_ctx), j_out[0], j_out[1], small
    )

    def both(big, small):
        out = []
        for at in (0, side):
            t = outer_sum(big, small[:, at : at + side]).astype(bf16)
            out.append((t[:, : side // 2], t[:, side // 2 :]))
        return out

    ctx_all = [jnp.concatenate(ctx[:2], 1), jnp.concatenate(ctx[2:], 1)]
    wide = [both(cross_rows, grad_q), both(g_c, cross_ctx)]
    so_parts = [outer_sum(g_s, t).astype(bf16) for t in ctx_all]
    wide.append([(t[:, : side // 2], t[:, side // 2 :]) for t in so_parts])
    c_keep, c_send = [
        tuple(jnp.concatenate([w[n][m] for w in wide], 1) for m in range(2)) for n in range(2)
    ]

    def split_heads_back(t):
        oc, tc, od, td = [t[:, side // 2 * n : side // 2 * (n + 1)] for n in range(4)]
        return ordered(core == 0, oc, od, 1), ordered(core == 0, tc, td, 1)

    grad_ctx, c_send, text_hop = tie((grad_ctx, c_send, text_hop))
    c_got = over_core(c_send)
    dk = ordered(half == 0, dk_own, text_hop[:, :width], 0)
    dv = ordered(half == 0, dv_own, text_hop[:, width:], 0)
    grad_text = against(dk, cross_key) + against(dv, cross_value)
    text_mine = piece(grad_text, half, width, 1)
    text_hop = piece(grad_text, 1 - half, width, 1).astype(bf16)
    grad_ctx, text_mine, text_hop = tie((grad_ctx, text_mine, text_hop))
    text_hop = over_y(text_hop)
    grad_ctx = onward(grad_ctx, j_in, *j_out, small)

    grads, parts = [None] * 4, [None] * 4

    def back(n, main):
        grads[n] = group_backward(clip_bounds, qkv[n], ctx[n], main, log[n], n)
        parts[n] = outer_sum(self_rows, grads[n]).astype(bf16)
        main, parts[n] = tie((main, parts[n]))
        return main

    main = back(3, grad_ctx)
    main, c_got, text_hop = tie((main, c_got, text_hop))
    grad_text = (text_mine + text_hop.astype(f32)).astype(bf16)
    text_part = against(grad_text, text_weight).astype(bf16)
    tall = text_full.shape[1] - text_states.shape[1]
    text_wide = jnp.concatenate(
        [
            text_states,
            jnp.ones((text_states.shape[0], 1), bf16),
            jnp.zeros((text_states.shape[0], tall - 1), bf16),
        ],
        1,
    )
    text_keep, text_send = [
        jnp.concatenate(
            [
                outer_sum(text_full, quarter(dk, w, 1)),
                outer_sum(text_full, quarter(dv, w, 1)),
                outer_sum(text_wide, quarter(grad_text, w, 1)),
            ],
            1,
        ).astype(bf16)
        for w in (core, 1 - core)
    ]
    c_cut = c_keep[0].shape[1] // 2
    j_wide = [
        Journey(
            travel_y((c_keep[0][:, sl], c_got[0][:, sl]), add(c_keep[1][:, sl], c_got[1][:, sl]))
        )
        for sl in (slice(0, c_cut), slice(c_cut, None))
    ]
    main, parts[3], text_send = tie((main, parts[3], text_send))
    td_got, text_got = over_core(parts[3]), over_core(text_send)
    main = onward(main, j_in, *j_out, j_wide[0], small)
    main = back(1, main)
    main, td_got, text_got = tie((main, td_got, text_got))
    j_text = Journey(travel((text_keep, text_got), steps))
    e_cut = parts[1].shape[0] // 2
    other = add(parts[1], td_got)
    main, other = tie((main, other))
    came_1 = over_y(other[:e_cut])
    main = onward(main, j_in, *j_out, j_text, small)

    def gathered(blocks):
        return lax.all_gather(jnp.concatenate(blocks, 1), "dp", axis=0, tiled=False)

    main = back(2, main)
    main, parts[2], came_1, text_part = tie((main, parts[2], came_1, text_part))
    od_got = over_core(parts[2])
    came_2, text_came = over_y(other[e_cut:]), over_y(text_part)
    main = onward(main, j_wide[0], j_text)
    main, blocks = tie((main, [j.result for j in (j_in, *j_out)]))
    feed_sum = gathered(blocks)
    main = back(0, main)
    main, came_1, came_2, od_got, text_came = tie((main, came_1, came_2, od_got, text_came))
    text_grad = text_part.astype(f32) + text_came.astype(f32)
    j_self = Journey(travel((parts[0], od_got, jnp.concatenate([came_1, came_2])), steps))
    grads = onward(grads, j_wide[0], j_wide[1], j_text, j_self)
    frames_grad, self_sums = final_grads(frames, g_middle, grads, qkv_w, vec)
    last = Journey(travel_small(self_sums[:2]))
    everything = [j_in, *j_out, *j_wide, j_text, j_self, small, last]
    frames_grad = onward(frames_grad, *[j for j in everything if j.result is None])
    for journey in everything:
        while journey.result is None:
            journey.go(journey.pending)
    early, late = small.result, last.result
    rest_sum = gathered([j.result for j in (*j_wide, j_text, j_self)])

    feed_in_grad, feed_out_grad = spread_feed(feed_sum)
    cq_g, co_g, so_g, ck_g, cv_g, text_g, q_g, k_g, v_g, bias_g = spread_rest(rest_sum, side // 2)
    return (
        output,
        frames_grad,
        text_grad,
        late[0],
        late[1],
        q_g,
        k_g,
        v_g,
        so_g,
        early[2],
        early[3],
        cq_g,
        ck_g,
        cv_g,
        co_g,
        text_g,
        bias_g[0],
        early[0],
        early[1],
        feed_in_grad,
        feed_out_grad.reshape(feed_out.shape),
    )


def chosen(dp, mp, *args):
    rows_here, frames_here = args[2].shape[0], args[0].shape[0]
    if mp == 2 and dp == 16 and rows_here == mp and frames_here == ROW_LEN:
        return row_body(dp, *args)
    return body(*args)


def solution(mesh):
    return jax.shard_map(
        functools.partial(chosen, mesh.shape["dp"], mesh.shape["mp"]),
        mesh=mesh,
        in_specs=(
            P(("dp", "mp"), None),
            P("dp", None),
            P("dp", None),
            P("dp", None),
            P(("dp", "mp"), None),
            P(),
            P(),
            P(None, "mp"),
            P(None, "mp"),
            P(None, "mp"),
            P("mp", None),
            P(),
            P(),
            P(None, "mp"),
            P(None, "mp"),
            P(None, "mp"),
            P("mp", None),
            P(None, "mp"),
            P("mp"),
            P(),
            P(),
            P(None, "mp"),
            P("mp", None),
        ),
        out_specs=(
            P(("dp", "mp"), None),
            P(("dp", "mp"), None),
            P("dp", None),
            P(),
            P(),
            P(None, "mp"),
            P(None, "mp"),
            P(None, "mp"),
            P("mp", None),
            P(),
            P(),
            P(None, "mp"),
            P(None, "mp"),
            P(None, "mp"),
            P("mp", None),
            P(None, "mp"),
            P("mp"),
            P(),
            P(),
            P(None, "mp"),
            P("mp", None),
        ),
        check_vma=False,
    )
```

```python
import functools
from functools import reduce

import jax
import jax.numpy as jnp
from jax import lax
from jax.experimental import pallas as pl
from jax.experimental.pallas import tpu as pltpu
from jax.sharding import PartitionSpec as P

HEAD_DIM = 64
ROW_LEN = 1536
TXT_ROW = 128


EPSILON = 1e-05
MASKED = -1e30


def product(left_side, right_side):
    return jnp.dot(left_side, right_side, preferred_element_type=jnp.float32)


def against(left_side, right_side):
    return lax.dot_general(
        left_side, right_side, (((1,), (1,)), ((), ())), preferred_element_type=jnp.float32
    )


def outer_sum(left_side, right_side):
    return lax.dot_general(
        left_side, right_side, (((0,), (0,)), ((), ())), preferred_element_type=jnp.float32
    )


def exact_gelu(tensor):
    return jax.nn.gelu(tensor, approximate=False)


def segment_ids(lengths, positions):
    bounds = jnp.cumsum(lengths, axis=-1)
    places = jnp.arange(positions, dtype=jnp.int32)
    return jnp.sum((places[None, :, None] >= bounds[:, None, :]).astype(jnp.int32), axis=-1)


def split_heads(tensor, row_count):
    return tensor.reshape(
        row_count, tensor.shape[0] // row_count, tensor.shape[1] // HEAD_DIM, HEAD_DIM
    )


def norm_parts(tensor):
    average = jnp.mean(tensor, axis=-1, keepdims=True)
    centered = tensor - average
    inverse = lax.rsqrt(jnp.mean(centered * centered, axis=-1, keepdims=True) + EPSILON)
    return (centered * inverse, inverse)


def norm_back(gradient, standard, inverse, norm_gain):
    scaled = gradient * norm_gain
    first_mean = jnp.mean(scaled, axis=-1, keepdims=True)
    second_mean = jnp.mean(scaled * standard, axis=-1, keepdims=True)
    return (
        inverse * (scaled - first_mean - standard * second_mean),
        jnp.sum(gradient * standard, axis=0),
        jnp.sum(gradient, axis=0),
    )


def spread_rows(tensor):
    return lax.all_gather(tensor, "mp", axis=0, tiled=True)


def spread_cotangent(tensor):
    return lax.all_gather(tensor, "mp", axis=0, tiled=True)


def branch_sum(left_side, right_side):
    return lax.psum_scatter(product(left_side, right_side), "mp", scatter_dimension=0, tiled=True)


def input_grads(factor_pairs):
    partials = [against(left_side, right_side) for left_side, right_side in factor_pairs]
    return lax.psum_scatter(reduce(jnp.add, partials), "mp", scatter_dimension=0, tiled=True)


def attend_forward(queries, key_heads, values, allowed):
    scores = jnp.einsum(
        "rqhd,rkhd->rhqk", queries, key_heads, preferred_element_type=jnp.float32
    ) * HEAD_DIM ** (-0.5)
    scores = jnp.where(allowed[:, None], scores, MASKED)
    row_max = jnp.max(scores, axis=-1, keepdims=True)
    shifted = jnp.exp(scores - row_max)
    totals = jnp.sum(shifted, axis=-1, keepdims=True)
    soft_weights = (shifted / totals).astype(jnp.bfloat16)
    context = jnp.einsum(
        "rhqk,rkhd->rqhd", soft_weights, values, preferred_element_type=jnp.float32
    )
    return (context, row_max + jnp.log(totals))


def attend_back(queries, key_heads, values, allowed, log_totals, grad_context):
    score_scale = HEAD_DIM ** (-0.5)
    scores = (
        jnp.einsum("rqhd,rkhd->rhqk", queries, key_heads, preferred_element_type=jnp.float32)
        * score_scale
    )
    scores = jnp.where(allowed[:, None], scores, MASKED)
    soft_weights = jnp.exp(scores - log_totals)
    grad_soft = jnp.einsum(
        "rqhd,rkhd->rhqk", grad_context, values, preferred_element_type=jnp.float32
    )
    row_inner = jnp.sum(grad_soft * soft_weights, axis=-1, keepdims=True)
    grad_scores = (soft_weights * (grad_soft - row_inner)).astype(jnp.bfloat16)
    grad_query = (
        jnp.einsum("rhqk,rkhd->rqhd", grad_scores, key_heads, preferred_element_type=jnp.float32)
        * score_scale
    )
    grad_keys = (
        jnp.einsum("rhqk,rqhd->rkhd", grad_scores, queries, preferred_element_type=jnp.float32)
        * score_scale
    )
    grad_values = jnp.einsum(
        "rhqk,rqhd->rkhd",
        soft_weights.astype(jnp.bfloat16),
        grad_context,
        preferred_element_type=jnp.float32,
    )
    return (grad_query, grad_keys, grad_values)


def self_allowed(segments, start_at, stop_at):
    places = jnp.arange(stop_at, dtype=jnp.int32)
    same_clip = segments[:, start_at:stop_at, None] == segments[:, None, :stop_at]
    return same_clip & (places[start_at:stop_at, None] >= places[None, :])[None]


def self_forward(queries, key_heads, values, segments):
    block_size = min(512, queries.shape[1])
    contexts = []
    log_totals = []
    for start_at in range(0, queries.shape[1], block_size):
        stop_at = start_at + block_size
        context, log_total = attend_forward(
            queries[:, start_at:stop_at],
            key_heads[:, :stop_at],
            values[:, :stop_at],
            self_allowed(segments, start_at, stop_at),
        )
        contexts.append(context)
        log_totals.append(log_total)
    return (jnp.concatenate(contexts, axis=1), jnp.concatenate(log_totals, axis=2))


def self_back(queries, key_heads, values, segments, log_totals, grad_context):
    block_size = min(512, queries.shape[1])
    query_parts = []
    grad_keys = jnp.zeros(key_heads.shape, jnp.float32)
    grad_values = jnp.zeros(values.shape, jnp.float32)
    for start_at in range(0, queries.shape[1], block_size):
        stop_at = start_at + block_size
        grad_query, key_part, value_part = attend_back(
            queries[:, start_at:stop_at],
            key_heads[:, :stop_at],
            values[:, :stop_at],
            self_allowed(segments, start_at, stop_at),
            log_totals[:, :, start_at:stop_at],
            grad_context[:, start_at:stop_at],
        )
        query_parts.append(grad_query)
        grad_keys = grad_keys.at[:, :stop_at].add(key_part)
        grad_values = grad_values.at[:, :stop_at].add(value_part)
    return (jnp.concatenate(query_parts, axis=1), grad_keys, grad_values)


def body(
    frames,
    text_states,
    clip_lengths,
    text_lengths,
    cotangent,
    self_gain,
    self_shift,
    self_query,
    self_key,
    self_value,
    self_out,
    cross_gain,
    cross_shift,
    cross_query,
    cross_key,
    cross_value,
    cross_out,
    text_weight,
    text_bias,
    feed_gain,
    feed_shift,
    feed_in,
    feed_out,
):
    row_count = clip_lengths.shape[0]
    clip_segs = segment_ids(clip_lengths, ROW_LEN)
    text_segs = segment_ids(text_lengths, TXT_ROW)
    residual = frames.astype(jnp.float32)
    self_standard, self_inverse = norm_parts(residual)
    self_rows = spread_rows((self_standard * self_gain + self_shift).astype(jnp.bfloat16))
    self_queries = product(self_rows, self_query).astype(jnp.bfloat16)
    self_keys = product(self_rows, self_key).astype(jnp.bfloat16)
    self_values = product(self_rows, self_value).astype(jnp.bfloat16)
    self_context, self_logs = self_forward(
        split_heads(self_queries, row_count),
        split_heads(self_keys, row_count),
        split_heads(self_values, row_count),
        clip_segs,
    )
    self_context = self_context.reshape(self_queries.shape).astype(jnp.bfloat16)
    middle = residual + branch_sum(self_context, self_out)
    cross_standard, cross_inverse = norm_parts(middle)
    cross_rows = spread_rows((cross_standard * cross_gain + cross_shift).astype(jnp.bfloat16))
    text_part = (product(text_states, text_weight) + text_bias).astype(jnp.bfloat16)
    text_full = lax.all_gather(text_part, "mp", axis=1, tiled=True)
    cross_queries = product(cross_rows, cross_query).astype(jnp.bfloat16)
    cross_keys = product(text_full, cross_key).astype(jnp.bfloat16)
    cross_values = product(text_full, cross_value).astype(jnp.bfloat16)
    cross_allowed = clip_segs[:, :, None] == text_segs[:, None, :]
    cross_context, cross_logs = attend_forward(
        split_heads(cross_queries, row_count),
        split_heads(cross_keys, row_count),
        split_heads(cross_values, row_count),
        cross_allowed,
    )
    cross_context = cross_context.reshape(cross_queries.shape).astype(jnp.bfloat16)
    after_cross = middle + branch_sum(cross_context, cross_out)
    feed_standard, feed_inverse = norm_parts(after_cross)
    feed_normed = (feed_standard * feed_gain + feed_shift).astype(jnp.bfloat16)
    feed_rows = spread_rows(feed_normed)
    hidden = product(feed_rows, feed_in)
    active, gelu_back = jax.vjp(exact_gelu, hidden)
    active = active.astype(jnp.bfloat16)
    output = after_cross + branch_sum(active, feed_out)
    grad_output = cotangent.astype(jnp.float32)
    feed_cotangent = grad_output.astype(jnp.bfloat16)
    grad_rows = spread_cotangent(feed_cotangent)
    feed_out_grad = outer_sum(active, grad_rows)
    grad_hidden = gelu_back(against(grad_rows, feed_out))[0].astype(jnp.bfloat16)
    feed_in_grad = outer_sum(feed_rows, grad_hidden)
    grad_feed_normed = input_grads(((grad_hidden, feed_in),))
    grad_norm, feed_gain_grad, feed_shift_grad = norm_back(
        grad_feed_normed, feed_standard, feed_inverse, feed_gain
    )
    grad_after = grad_output + grad_norm
    cross_cotangent = spread_cotangent(grad_after.astype(jnp.bfloat16))
    cross_out_grad = outer_sum(cross_context, cross_cotangent)
    grad_context = against(cross_cotangent, cross_out).astype(jnp.bfloat16)
    grad_queries, grad_keys, grad_values = attend_back(
        split_heads(cross_queries, row_count),
        split_heads(cross_keys, row_count),
        split_heads(cross_values, row_count),
        cross_allowed,
        cross_logs,
        split_heads(grad_context, row_count),
    )
    grad_queries = grad_queries.reshape(cross_queries.shape).astype(jnp.bfloat16)
    grad_keys = grad_keys.reshape(cross_keys.shape).astype(jnp.bfloat16)
    grad_values = grad_values.reshape(cross_values.shape).astype(jnp.bfloat16)
    cross_query_grad = outer_sum(cross_rows, grad_queries)
    cross_key_grad = outer_sum(text_full, grad_keys)
    cross_value_grad = outer_sum(text_full, grad_values)
    grad_text_full = against(grad_keys, cross_key) + against(grad_values, cross_value)
    grad_text = lax.psum_scatter(
        grad_text_full.astype(jnp.bfloat16), "mp", scatter_dimension=1, tiled=True
    )
    text_weight_grad = outer_sum(text_states, grad_text)
    text_bias_grad = jnp.sum(grad_text.astype(jnp.float32), axis=0)
    text_grad = lax.psum(against(grad_text, text_weight).astype(jnp.bfloat16), "mp").astype(
        jnp.float32
    )
    grad_cross_normed = input_grads(((grad_queries, cross_query),))
    grad_norm, cross_gain_grad, cross_shift_grad = norm_back(
        grad_cross_normed, cross_standard, cross_inverse, cross_gain
    )
    grad_middle = grad_after + grad_norm
    self_cotangent = spread_cotangent(grad_middle.astype(jnp.bfloat16))
    self_out_grad = outer_sum(self_context, self_cotangent)
    grad_context = against(self_cotangent, self_out).astype(jnp.bfloat16)
    grad_queries, grad_keys, grad_values = self_back(
        split_heads(self_queries, row_count),
        split_heads(self_keys, row_count),
        split_heads(self_values, row_count),
        clip_segs,
        self_logs,
        split_heads(grad_context, row_count),
    )
    grad_queries = grad_queries.reshape(self_queries.shape).astype(jnp.bfloat16)
    grad_keys = grad_keys.reshape(self_keys.shape).astype(jnp.bfloat16)
    grad_values = grad_values.reshape(self_values.shape).astype(jnp.bfloat16)
    self_query_grad = outer_sum(self_rows, grad_queries)
    self_key_grad = outer_sum(self_rows, grad_keys)
    self_value_grad = outer_sum(self_rows, grad_values)
    grad_self_normed = input_grads(
        ((grad_queries, self_query), (grad_keys, self_key), (grad_values, self_value))
    )
    grad_norm, self_gain_grad, self_shift_grad = norm_back(
        grad_self_normed, self_standard, self_inverse, self_gain
    )
    frames_grad = grad_middle + grad_norm
    (
        self_query_grad,
        self_key_grad,
        self_value_grad,
        self_out_grad,
        cross_query_grad,
        cross_key_grad,
        cross_value_grad,
        cross_out_grad,
        text_weight_grad,
        text_bias_grad,
        feed_in_grad,
        feed_out_grad,
    ) = (
        lax.psum(self_query_grad.astype(jnp.bfloat16), "dp").astype(jnp.float32),
        lax.psum(self_key_grad.astype(jnp.bfloat16), "dp").astype(jnp.float32),
        lax.psum(self_value_grad.astype(jnp.bfloat16), "dp").astype(jnp.float32),
        lax.psum(self_out_grad.astype(jnp.bfloat16), "dp").astype(jnp.float32),
        lax.psum(cross_query_grad.astype(jnp.bfloat16), "dp").astype(jnp.float32),
        lax.psum(cross_key_grad.astype(jnp.bfloat16), "dp").astype(jnp.float32),
        lax.psum(cross_value_grad.astype(jnp.bfloat16), "dp").astype(jnp.float32),
        lax.psum(cross_out_grad.astype(jnp.bfloat16), "dp").astype(jnp.float32),
        lax.psum(text_weight_grad.astype(jnp.bfloat16), "dp").astype(jnp.float32),
        lax.psum(text_bias_grad.astype(jnp.bfloat16), "dp").astype(jnp.float32),
        lax.psum(feed_in_grad.astype(jnp.bfloat16), "dp").astype(jnp.float32),
        lax.psum(feed_out_grad.astype(jnp.bfloat16), "dp").astype(jnp.float32),
    )
    (
        self_gain_grad,
        self_shift_grad,
        cross_gain_grad,
        cross_shift_grad,
        feed_gain_grad,
        feed_shift_grad,
    ) = lax.psum(
        (
            self_gain_grad,
            self_shift_grad,
            cross_gain_grad,
            cross_shift_grad,
            feed_gain_grad,
            feed_shift_grad,
        ),
        ("dp", "mp"),
    )
    return (
        output.astype(jnp.bfloat16),
        frames_grad,
        text_grad,
        self_gain_grad,
        self_shift_grad,
        self_query_grad,
        self_key_grad,
        self_value_grad,
        self_out_grad,
        cross_gain_grad,
        cross_shift_grad,
        cross_query_grad,
        cross_key_grad,
        cross_value_grad,
        cross_out_grad,
        text_weight_grad,
        text_bias_grad,
        feed_gain_grad,
        feed_shift_grad,
        feed_in_grad,
        feed_out_grad,
    )


LOG2E=1.4426950408889634
SCALE2=LOG2E*HEAD_DIM**-0.5
BQ=256
SPAN=768

def dot(a,b,ca,cb):
    return lax.dot_general(a,b,(((ca,),(cb,)),((),())),preferred_element_type=jnp.float32)

def starts_of(bounds_ref, places):
    start=jnp.zeros_like(places)
    for k in range(3):
        start=jnp.where(places>=bounds_ref[k],bounds_ref[k],start)
    return start

def self_fwd_kernel(bounds_ref,q_ref,k_ref,v_ref,o_ref,lse_ref,*,ahead=2):
    low=lax.broadcasted_iota(jnp.int32,(1,128),1)<HEAD_DIM
    vt=jnp.transpose(v_ref[...])
    pad=jnp.ones((16,ROW_LEN),jnp.bfloat16)
    vts=[jnp.concatenate([vt[64*h:64*h+64],pad],0) for h in range(2)]
    def span(i):
        return max(0,BQ*i-SPAN),BQ*(i+1)
    def scores(i,h):
        k0,k1=span(i)
        q=q_ref[BQ*i:k1,:]
        qh=jnp.where(low==(h==0),q,jnp.zeros_like(q))
        places=BQ*i+lax.broadcasted_iota(jnp.int32,(1,BQ),1)
        keys=k0+lax.broadcasted_iota(jnp.int32,(k1-k0,BQ),0)
        allowed=(keys>=starts_of(bounds_ref,places))&(keys<=places)
        return jnp.where(allowed,dot(k_ref[k0:k1,:],qh,1,1),MASKED)
    items=[(i,h) for i in range(ROW_LEN//BQ) for h in range(2)]
    queue=[scores(*it) for it in items[:ahead]]
    outs=[]
    for n,(i,h) in enumerate(items):
        if n+ahead<len(items):
            queue.append(scores(*items[n+ahead]))
        s=queue.pop(0)
        k0,k1=span(i)
        m=jnp.max(s,axis=0,keepdims=True)
        p=jnp.exp2((s-m)*SCALE2)
        o=dot(vts[h][:,k0:k1],p.astype(jnp.bfloat16),1,0)
        l=o[64:65]
        outs.append(o[:64]*(1.0/l))
        lse_ref[0,h:h+1,BQ*i:k1]=m*SCALE2+jnp.log2(l)
        if h==1:
            o_ref[BQ*i:k1,:]=jnp.transpose(jnp.concatenate(outs,0)).astype(jnp.bfloat16)
            outs=[]

def self_bwd_kernel(bounds_ref,q_ref,k_ref,v_ref,o_ref,g_ref,lse_ref,out_ref,acc_ref,d_ref,*,mode="t",ahead=1):
    low=lax.broadcasted_iota(jnp.int32,(1,128),1)<HEAD_DIM
    n=ROW_LEN//BQ
    pair=pl.program_id(0)
    width=128*pl.num_programs(0)
    def put(which,sl,t):
        at=pl.multiple_of(which*width+pair*128,128)
        out_ref[sl,pl.ds(at,128)]=t.astype(jnp.bfloat16)

    for i in range(n):
        sl=slice(BQ*i,BQ*(i+1))
        t=jnp.transpose(g_ref[sl,:].astype(jnp.float32)*o_ref[sl,:].astype(jnp.float32))
        d_ref[0:1,sl]=jnp.sum(t[:64],axis=0,keepdims=True)
        d_ref[1:2,sl]=jnp.sum(t[64:],axis=0,keepdims=True)
    acc_ref[...]=jnp.zeros_like(acc_ref)
    def span(j):
        return BQ*j,min(ROW_LEN,BQ*(j+1)+SPAN)
    def masked(ref,j,h):
        t=ref[BQ*j:BQ*(j+1),:]
        return jnp.where(low==(h==0),t,jnp.zeros_like(t))
    def scores(j,h):
        q0,q1=span(j)
        places=q0+lax.broadcasted_iota(jnp.int32,(1,q1-q0),1)
        keys=BQ*j+lax.broadcasted_iota(jnp.int32,(BQ,q1-q0),0)
        allowed=(keys>=starts_of(bounds_ref,places))&(keys<=places)
        s=dot(masked(k_ref,j,h),q_ref[q0:q1,:],1,1)*SCALE2-lse_ref[0,h:h+1,q0:q1]
        return jnp.where(allowed,s,MASKED),dot(masked(v_ref,j,h),g_ref[q0:q1,:],1,1)
    items=[(j,h) for j in range(n) for h in range(2)]
    queue=[scores(*it) for it in items[:ahead]]
    dks=[];dvs=[]
    for t,(j,h) in enumerate(items):
        if t+ahead<len(items):
            queue.append(scores(*items[t+ahead]))
        s,dp=queue.pop(0)
        sl=slice(BQ*j,BQ*(j+1))
        q0,q1=span(j)
        p=jnp.exp2(s)
        ds=(p*(dp-d_ref[h:h+1,q0:q1])).astype(jnp.bfloat16)
        dvs.append(dot(p.astype(jnp.bfloat16),g_ref[q0:q1,:],1,0))
        dks.append(dot(ds,q_ref[q0:q1,:],1,0))
        if mode=="t":
            kt=jnp.transpose(k_ref[sl,:])
            acc_ref[64*h:64*h+64,q0:q1]+=dot(kt[64*h:64*h+64],ds,1,0)
        else:
            acc_ref[q0:q1,:]+=dot(ds,masked(k_ref,j,h),0,0)
        if h==1:
            put(1,sl,jnp.where(low,dks[0],dks[1])*HEAD_DIM**-0.5)
            put(2,sl,jnp.where(low,dvs[0],dvs[1]))
            dks=[];dvs=[]
            acc=jnp.transpose(acc_ref[:,sl]) if mode=="t" else acc_ref[sl,:]
            put(0,sl,acc*HEAD_DIM**-0.5)


def group_forward(bounds,qkv):
    width=qkv.shape[1]//3
    pairs=width//128
    spec=lambda t: pl.BlockSpec((ROW_LEN,128),lambda h:(0,t*pairs+h))
    return pl.pallas_call(self_fwd_kernel,grid=(pairs,),
        in_specs=[pl.BlockSpec(memory_space=pltpu.SMEM),spec(0),spec(1),spec(2)],
        out_specs=[spec(0),pl.BlockSpec((1,2,ROW_LEN),lambda h:(h,0,0))],
        out_shape=[jax.ShapeDtypeStruct((ROW_LEN,width),jnp.bfloat16),jax.ShapeDtypeStruct((pairs,2,ROW_LEN),jnp.float32)],
        compiler_params=pltpu.CompilerParams(vmem_limit_bytes=40<<20),
        name="self_forward",
        cost_estimate=pl.CostEstimate(flops=pairs*2*18*256*256*64*4*4,bytes_accessed=pairs*4*1536*256,transcendentals=0),
    )(bounds,qkv,qkv,qkv)

def group_backward(bounds,qkv,o,g,lse,group):
    width=qkv.shape[1]//3
    pairs=width//128
    spec=lambda t: pl.BlockSpec((ROW_LEN,128),lambda h:(0,t*pairs+h))
    return pl.pallas_call(self_bwd_kernel,grid=(pairs,),
        in_specs=[pl.BlockSpec(memory_space=pltpu.SMEM),spec(0),spec(1),spec(2),spec(0),spec(group),pl.BlockSpec((1,2,ROW_LEN),lambda h:(h,0,0))],
        out_specs=pl.BlockSpec((ROW_LEN,3*width),lambda h:(0,0)),
        out_shape=jax.ShapeDtypeStruct(qkv.shape,jnp.bfloat16),
        scratch_shapes=[pltpu.VMEM((128,ROW_LEN),jnp.float32),pltpu.VMEM((8,ROW_LEN),jnp.float32)],
        compiler_params=pltpu.CompilerParams(vmem_limit_bytes=48<<20),
        name="self_backward",
        cost_estimate=pl.CostEstimate(flops=pairs*2*18*256*256*64*10*4,bytes_accessed=pairs*8*1536*256,transcendentals=0),
    )(bounds,qkv,qkv,qkv,o,g,lse)

def token_range(cb_ref,tb_ref,places):
    lo=jnp.zeros_like(places); hi=jnp.full_like(places,0)+tb_ref[0]
    for c in range(3):
        past=places>=cb_ref[c]
        lo=jnp.where(past,tb_ref[c],lo)
        hi=jnp.where(past,tb_ref[c+1],hi)
    return lo,hi


INV_SQRT_2PI = 0.3989422804014327
TB = 256
NB = 512


def mean_row(t):
    return jnp.sum(t, axis=-1, keepdims=True) * (1.0 / t.shape[-1])


def standardise(t):
    centered = t - mean_row(t)
    inverse = lax.rsqrt(mean_row(centered * centered) + EPSILON)
    return centered * inverse, inverse


def norm_input_grad(e, standard, inverse, gain):
    scaled = e * gain
    return inverse * (scaled - mean_row(scaled) - standard * mean_row(scaled * standard))


def column_sums(t):
    return jnp.sum(t, axis=0, keepdims=True)


def gelu_pair(hidden):
    density = jnp.exp2(hidden * hidden * (-0.5 * LOG2E)) * INV_SQRT_2PI
    t = 1.0 / (1.0 + 0.2316419 * jnp.abs(hidden))
    series = t * (
        0.319381530
        + t * (-0.356563782 + t * (1.781477937 + t * (-1.821255978 + t * 1.330274429)))
    )
    tail = density * series
    below = jnp.where(hidden >= 0, 1.0 - tail, tail)
    return hidden * below, below + hidden * density


def mid_forward_kernel(
    count, cb_ref, tb_ref, x_ref, *refs,
):
    ctxs, sos, cqs, cos = [refs[count * t : count * t + count] for t in range(4)]
    (k_ref, v_ref, vec_ref,
     mid_ref, rows_ref, q_ref, cctx_ref, lse_ref, after_ref, feed_ref, feedt_ref, vt_ref) = refs[4 * count :]
    i = pl.program_id(0)
    low = lax.broadcasted_iota(jnp.int32, (1, 128), 1) < HEAD_DIM

    @pl.when(i == 0)
    def _():
        vt_ref[0:1024, :] = jnp.transpose(v_ref[...])
        vt_ref[1024:1040, :] = jnp.ones((16, TXT_ROW), jnp.bfloat16)

    middle = x_ref[...].astype(jnp.float32)
    for c, w in zip(ctxs, sos):
        middle = middle + dot(c[...], w[...], 1, 0)
    mid_ref[...] = middle
    u, _ = standardise(middle)
    rows = (u * vec_ref[0:1, :] + vec_ref[1:2, :]).astype(jnp.bfloat16)
    rows_ref[...] = rows
    at = 0
    for w in cqs:
        n = w.shape[1]
        q_ref[:, at : at + n] = dot(rows, w[...], 1, 0).astype(jnp.bfloat16)
        at += n
    places = TB * i + lax.broadcasted_iota(jnp.int32, (1, TB), 1)
    lo, hi = token_range(cb_ref, tb_ref, places)
    toks = lax.broadcasted_iota(jnp.int32, (TXT_ROW, TB), 0)
    allowed = (toks >= lo) & (toks < hi)

    def scores(head):
        p, h = head // 2, head % 2
        k = k_ref[:, 128 * p : 128 * p + 128]
        kh = jnp.where(low == (h == 0), k, jnp.zeros_like(k))
        return jnp.where(allowed, dot(kh, q_ref[:, 128 * p : 128 * p + 128], 1, 1), MASKED)

    ahead = 3
    queue = [scores(t) for t in range(ahead)]
    outs = []
    ones = vt_ref[1024:1040, :]
    for head in range(16):
        if head + ahead < 16:
            queue.append(scores(head + ahead))
        s = queue.pop(0)
        m = jnp.max(s, axis=0, keepdims=True)
        p = jnp.exp2((s - m) * SCALE2)
        vt = jnp.concatenate([vt_ref[64 * head : 64 * head + 64, :], ones], 0)
        o = dot(vt, p.astype(jnp.bfloat16), 1, 0)
        l = o[64:65]
        outs.append(o[:64] * (1.0 / l))
        lse_ref[head : head + 1, :] = m * SCALE2 + jnp.log2(l)
        if head % 2 == 1:
            pair = head // 2
            cctx_ref[:, 128 * pair : 128 * pair + 128] = jnp.transpose(
                jnp.concatenate(outs, 0)
            ).astype(jnp.bfloat16)
            outs = []
    after = mid_ref[...]
    at = 0
    for w in cos:
        n = w.shape[0]
        after = after + dot(cctx_ref[:, at : at + n], w[...], 1, 0)
        at += n
    after_ref[...] = after
    u, _ = standardise(after)
    feed = (u * vec_ref[2:3, :] + vec_ref[3:4, :]).astype(jnp.bfloat16)
    feed_ref[...] = feed
    feedt_ref[...] = jnp.transpose(feed)


def row_block(n):
    return pl.BlockSpec((TB, n), lambda i: (i, 0))


def whole(t):
    return pl.BlockSpec(t.shape, lambda i: (0,) * t.ndim)


def mid_forward(cb, tb, x, ctxs, sos, cqs, cos, k, v, vec):
    n, d = x.shape
    smem = pl.BlockSpec(memory_space=pltpu.SMEM)
    bf, f = jnp.bfloat16, jnp.float32
    weights = [*sos, *cqs, *cos, k, v, vec]
    return pl.pallas_call(
        functools.partial(mid_forward_kernel, len(ctxs)),
        grid=(n // TB,),
        in_specs=[smem, smem, row_block(d)] + [row_block(c.shape[1]) for c in ctxs] + [whole(w) for w in weights],
        out_specs=[row_block(d)] * 4
        + [pl.BlockSpec((16, TB), lambda i: (0, i))]
        + [row_block(d)] * 2
        + [pl.BlockSpec((d, TB), lambda i: (0, i))],
        out_shape=[jax.ShapeDtypeStruct((n, d), t) for t in (f, bf, bf, bf)]
        + [jax.ShapeDtypeStruct((16, n), f)]
        + [jax.ShapeDtypeStruct((n, d), t) for t in (f, bf)]
        + [jax.ShapeDtypeStruct((d, n), bf)],
        scratch_shapes=[pltpu.VMEM((1040, TXT_ROW), bf)],
        compiler_params=pltpu.CompilerParams(vmem_limit_bytes=56 << 20),
        name="mid_forward",
        cost_estimate=pl.CostEstimate(flops=24 * n * d * d // 2, bytes_accessed=40 * n * d // 2, transcendentals=0),
    )(cb, tb, x, *ctxs, *weights)


def mid_backward_kernel(
    count, cb_ref, tb_ref, e_ref, after_ref, g_ref, mid_ref, q_ref, cctx_ref, lse_ref, *refs,
):
    cos, cqs, sos = [refs[count * t : count * t + count] for t in range(3)]
    (k_ref, v_ref, vec_ref,
     gc_ref, gq_ref, gmid_ref, gs_ref, gctx_ref, dk_ref, dv_ref, sums_ref,
     kt_ref, dka_ref, dva_ref, gcc_ref) = refs[3 * count :]
    i = pl.program_id(0)
    low = lax.broadcasted_iota(jnp.int32, (1, 128), 1) < HEAD_DIM

    @pl.when(i == 0)
    def _():
        kt_ref[...] = jnp.transpose(k_ref[...])
        dka_ref[...] = jnp.zeros_like(dka_ref)
        dva_ref[...] = jnp.zeros_like(dva_ref)
        sums_ref[...] = jnp.zeros_like(sums_ref)

    e = e_ref[...]
    u, inverse = standardise(after_ref[...])
    sums_ref[0:1, :] += column_sums(e * u)
    sums_ref[1:2, :] += column_sums(e)
    g_after = g_ref[...].astype(jnp.float32) + norm_input_grad(e, u, inverse, vec_ref[2:3, :])
    gmid_ref[...] = g_after
    gc = g_after.astype(jnp.bfloat16)
    gc_ref[...] = gc
    at = 0
    for w in cos:
        n = w.shape[0]
        gcc_ref[:, at : at + n] = dot(gc, w[...], 1, 1).astype(jnp.bfloat16)
        at += n
    places = TB * i + lax.broadcasted_iota(jnp.int32, (1, TB), 1)
    lo, hi = token_range(cb_ref, tb_ref, places)
    toks = lax.broadcasted_iota(jnp.int32, (TXT_ROW, TB), 0)
    allowed = (toks >= lo) & (toks < hi)

    def scores(head):
        p, h = head // 2, head % 2
        sl = slice(128 * p, 128 * p + 128)
        pick = lambda t: jnp.where(low == (h == 0), t, jnp.zeros_like(t))
        s = dot(pick(k_ref[:, sl]), q_ref[:, sl], 1, 1) * SCALE2 - lse_ref[head : head + 1, :]
        return jnp.where(allowed, s, MASKED), dot(pick(v_ref[:, sl]), gcc_ref[:, sl], 1, 1)

    ahead = 2
    queue = [scores(t) for t in range(ahead)]
    dqs, dks, dvs = [], [], []
    for head in range(16):
        if head + ahead < 16:
            queue.append(scores(head + ahead))
        p_at, h = head // 2, head % 2
        sl = slice(128 * p_at, 128 * p_at + 128)
        if h == 0:
            t = jnp.transpose(
                gcc_ref[:, sl].astype(jnp.float32) * cctx_ref[:, sl].astype(jnp.float32)
            )
        s, dp = queue.pop(0)
        p = jnp.exp2(s)
        ds = (p * (dp - column_sums(t[64 * h : 64 * h + 64]))).astype(jnp.bfloat16)
        dvs.append(dot(p.astype(jnp.bfloat16), gcc_ref[:, sl], 1, 0))
        dks.append(dot(ds, q_ref[:, sl], 1, 0))
        dqs.append(dot(kt_ref[64 * head : 64 * head + 64, :], ds, 1, 0))
        if h == 1:
            gq_ref[:, sl] = (
                jnp.transpose(jnp.concatenate(dqs, 0)) * HEAD_DIM**-0.5
            ).astype(jnp.bfloat16)
            dka_ref[:, sl] += jnp.where(low, dks[0], dks[1])
            dva_ref[:, sl] += jnp.where(low, dvs[0], dvs[1])
            dqs, dks, dvs = [], [], []
    e = None
    at = 0
    for w in cqs:
        n = w.shape[1]
        part = dot(gq_ref[:, at : at + n], w[...], 1, 1)
        e = part if e is None else e + part
        at += n
    u, inverse = standardise(mid_ref[...])
    sums_ref[2:3, :] += column_sums(e * u)
    sums_ref[3:4, :] += column_sums(e)
    g_middle = gmid_ref[...] + norm_input_grad(e, u, inverse, vec_ref[0:1, :])
    gmid_ref[...] = g_middle
    gs = g_middle.astype(jnp.bfloat16)
    gs_ref[...] = gs
    at = 0
    for w in sos:
        n = w.shape[0]
        gctx_ref[:, at : at + n] = dot(gs, w[...], 1, 1).astype(jnp.bfloat16)
        at += n

    @pl.when(i == pl.num_programs(0) - 1)
    def _():
        dk_ref[...] = (dka_ref[...] * HEAD_DIM**-0.5).astype(jnp.bfloat16)
        dv_ref[...] = dva_ref[...].astype(jnp.bfloat16)


def mid_backward(cb, tb, e, after, g, middle, q, cctx, lse, cos, cqs, sos, k, v, vec):
    n, d = after.shape
    smem = pl.BlockSpec(memory_space=pltpu.SMEM)
    bf, f = jnp.bfloat16, jnp.float32
    weights = [*cos, *cqs, *sos, k, v, vec]
    text = jax.ShapeDtypeStruct((TXT_ROW, d), bf)
    sums = jax.ShapeDtypeStruct((8, d), f)
    return pl.pallas_call(
        functools.partial(mid_backward_kernel, len(cos)),
        grid=(n // TB,),
        in_specs=[smem, smem] + [row_block(d)] * 6 + [pl.BlockSpec((16, TB), lambda i: (0, i))] + [whole(w) for w in weights],
        out_specs=[row_block(d)] * 5 + [whole(text), whole(text), whole(sums)],
        out_shape=[jax.ShapeDtypeStruct((n, d), t) for t in (bf, bf, f, bf, bf)] + [text, text, sums],
        scratch_shapes=[
            pltpu.VMEM((d, TXT_ROW), bf),
            pltpu.VMEM((TXT_ROW, d), f),
            pltpu.VMEM((TXT_ROW, d), f),
            pltpu.VMEM((TB, d), bf),
        ],
        compiler_params=pltpu.CompilerParams(vmem_limit_bytes=58 << 20),
        name="mid_backward",
        cost_estimate=pl.CostEstimate(flops=40 * n * d * d // 2, bytes_accessed=46 * n * d // 2, transcendentals=0),
    )(cb, tb, e, after, g, middle, q, cctx, lse, *weights)


def feed_kernel(idx_ref, fr_ref, frt_ref, cot_ref, o_in, e_in, *refs, own, first, last):
    if own:
        fi_src, fo_src = refs[:2]
        refs = refs[2:]
    else:
        fi_srcs, fo_srcs = refs[:2], refs[2:4]
        refs = refs[4:]
    o_out, e_out, gi_ref, go_ref, acc_o, acc_e, fi_buf, fo_buf, act_s, gh_s, wsem, asem = refs
    p = pl.program_id(0)
    slot = p % 2

    def weights(step, into, act):
        if own:
            at = pl.multiple_of(idx_ref[step] * NB, NB)
            act(pltpu.make_async_copy(fi_src.at[:, pl.ds(at, NB)], fi_buf.at[into], wsem.at[into, 0]))
            act(pltpu.make_async_copy(fo_src.at[pl.ds(at, NB), :], fo_buf.at[into], wsem.at[into, 1]))
        else:
            for s in range(2):
                @pl.when(step == s)
                def _(s=s):
                    act(pltpu.make_async_copy(fi_srcs[s], fi_buf.at[into], wsem.at[into, 0]))
                    act(pltpu.make_async_copy(fo_srcs[s], fo_buf.at[into], wsem.at[into, 1]))

    o_load = pltpu.make_async_copy(o_in, acc_o, asem.at[0])
    if not first:
        e_load = pltpu.make_async_copy(e_in, acc_e, asem.at[1])

    @pl.when(p == 0)
    def _():
        weights(p, slot, lambda c: c.start())
        o_load.start()
        if not first:
            e_load.start()
        else:
            acc_e[...] = jnp.zeros_like(acc_e)

    weights(p, slot, lambda c: c.wait())

    @pl.when(p == 0)
    def _():
        weights(p + 1, 1 - slot, lambda c: c.start())

    @pl.when(p == 0)
    def _():
        o_load.wait()
        if not first:
            e_load.wait()

    fi, fo = fi_buf.at[slot], fo_buf.at[slot]
    rows = 256
    blocks = fr_ref.shape[0] // rows

    def products(r):
        sl = slice(rows * r, rows * r + rows)
        return dot(fr_ref[sl, :], fi[...], 1, 0), dot(cot_ref[sl, :], fo[...], 1, 1)

    ahead = 1
    queue = [products(r) for r in range(ahead)]
    for r in range(blocks):
        if r + ahead < blocks:
            queue.append(products(r + ahead))
        h, g = queue.pop(0)
        sl = slice(rows * r, rows * r + rows)
        active, slope = gelu_pair(h)
        active = active.astype(jnp.bfloat16)
        gh = (g * slope).astype(jnp.bfloat16)
        act_s[sl, :] = active
        gh_s[sl, :] = gh
        acc_o[sl, :] += dot(active, fo[...], 1, 0)
        acc_e[sl, :] += dot(gh, fi[...], 1, 1)
    gi_ref[...] = dot(frt_ref[...], gh_s[...], 1, 0).astype(jnp.bfloat16)
    go_ref[...] = dot(act_s[...], cot_ref[...], 0, 0).astype(jnp.bfloat16)

    @pl.when(p == 1)
    def _():
        e_store = pltpu.make_async_copy(acc_e, e_out, asem.at[1])
        e_store.start()
        if last:
            o_out[...] = acc_o[...].astype(jnp.bfloat16)
        else:
            o_store = pltpu.make_async_copy(acc_o, o_out, asem.at[0])
            o_store.start()
            o_store.wait()
        e_store.wait()


def feed_part(idx, rows, rows_t, cot, o_in, e_in, fis, fos, first, last):
    n, d = rows.shape
    own = len(fis) == 1
    bf, f = jnp.bfloat16, jnp.float32
    hbm = pl.BlockSpec(memory_space=pl.ANY)
    once = lambda shape: pl.BlockSpec(shape, lambda p, idx: (0, 0), pipeline_mode=pl.Buffered(1))
    grad = lambda shape: jax.ShapeDtypeStruct(shape, bf)
    return pl.pallas_call(
        functools.partial(feed_kernel, own=own, first=first, last=last),
        grid_spec=pltpu.PrefetchScalarGridSpec(
            num_scalar_prefetch=1,
            grid=(2,),
            in_specs=[once((n, d)), once((d, n)), once((n, d))] + [hbm] * (2 + 2 * len(fis)),
            out_specs=[
                once((n, d)) if last else hbm,
                hbm,
                pl.BlockSpec((d, NB), lambda p, idx: (0, idx[p] % 2)),
                pl.BlockSpec((NB, d), lambda p, idx: (idx[p] % 2, 0)),
            ],
            scratch_shapes=[
                pltpu.VMEM((n, d), f),
                pltpu.VMEM((n, d), f),
                pltpu.VMEM((2, d, NB), bf),
                pltpu.VMEM((2, NB, d), bf),
                pltpu.VMEM((n, NB), bf),
                pltpu.VMEM((n, NB), bf),
                pltpu.SemaphoreType.DMA((2, 2)),
                pltpu.SemaphoreType.DMA((2,)),
            ],
        ),
        out_shape=[
            jax.ShapeDtypeStruct((n, d), bf if last else f),
            jax.ShapeDtypeStruct((n, d), f),
            grad((d, 2 * NB)),
            grad((2 * NB, d)),
        ],
        compiler_params=pltpu.CompilerParams(vmem_limit_bytes=60 << 20),
        name="feed_last" if last else "feed_first" if first else "feed_more",
        cost_estimate=pl.CostEstimate(flops=24 * n * d * NB, bytes_accessed=48 << 20, transcendentals=0),
    )(idx, rows, rows_t, cot, o_in, e_in, *fis, *fos)


def final_kernel(x_ref, gmid_ref, *refs):
    count = (len(refs) - 3) // 2
    gs, ws = refs[:count], refs[count : 2 * count]
    vec_ref, out_ref, sums_ref = refs[2 * count :]

    @pl.when(pl.program_id(0) == 0)
    def _():
        sums_ref[...] = jnp.zeros_like(sums_ref)

    e = None
    for g, w in zip(gs, ws):
        part = dot(g[...], w[...], 1, 1)
        e = part if e is None else e + part
    u, inverse = standardise(x_ref[...].astype(jnp.float32))
    sums_ref[0:1, :] += column_sums(e * u)
    sums_ref[1:2, :] += column_sums(e)
    out_ref[...] = gmid_ref[...] + norm_input_grad(e, u, inverse, vec_ref[4:5, :])


def final_grads(x, gmid, gs, ws, vec):
    n, d = x.shape
    sums = jax.ShapeDtypeStruct((8, d), jnp.float32)
    return pl.pallas_call(
        final_kernel,
        grid=(n // TB,),
        in_specs=[row_block(d), row_block(d)] + [row_block(g.shape[1]) for g in gs] + [whole(w) for w in ws] + [whole(vec)],
        out_specs=[row_block(d), whole(sums)],
        out_shape=[jax.ShapeDtypeStruct((n, d), jnp.float32), sums],
        compiler_params=pltpu.CompilerParams(vmem_limit_bytes=56 << 20),
        name="frames_gradient",
        cost_estimate=pl.CostEstimate(flops=6 * n * d * d, bytes_accessed=24 * n * d // 2, transcendentals=0),
    )(x, gmid, *gs, *ws, vec)


def pair_at(b):
    return (b % 2) * 4 + (b // 2) % 2 * 2 + b // 4


def spread_feed_kernel(t_ref, in_ref, out_ref):
    n = in_ref.shape[1] // 2
    for c in range(2):
        in_ref[:, n * c : n * c + n] = t_ref[c, :, :n].astype(jnp.float32)
        out_ref[c] = t_ref[c, :, n:].astype(jnp.float32)


def spread_feed(t):
    _, rows, columns = t.shape
    n = columns // 2
    f = jnp.float32
    return pl.pallas_call(
        spread_feed_kernel,
        grid=(8,),
        in_specs=[pl.BlockSpec((2, rows, columns), lambda b: (pair_at(b), 0, 0))],
        out_specs=[
            pl.BlockSpec((rows, 2 * n), lambda b: (b, 0)),
            pl.BlockSpec((2, rows, n), lambda b: (0, b, 0)),
        ],
        out_shape=[
            jax.ShapeDtypeStruct((8 * rows, 2 * n), f),
            jax.ShapeDtypeStruct((2, 8 * rows, n), f),
        ],
        compiler_params=pltpu.CompilerParams(vmem_limit_bytes=32 << 20),
        name="spread_feed",
        cost_estimate=pl.CostEstimate(flops=0, bytes_accessed=6 * t.size, transcendentals=0),
    )(t)


def spread_rest_kernel(t_ref, *refs):
    cq, co, so, ck, cv, tw, q, k, v, tb = refs
    n = cq.shape[1] // 2
    b = pl.program_id(0)

    def both(i):
        return jnp.concatenate(
            [t_ref[c, :, n * i : n * i + n].astype(jnp.float32) for c in range(2)], 1
        )

    for i, ref in ((0, cq), (3, ck), (4, cv), (6, q), (7, k), (8, v)):
        ref[...] = both(i)
    co[...] = jnp.transpose(both(1))
    so[...] = jnp.transpose(both(2))

    @pl.when(b < 6)
    def _():
        tw[...] = both(5)

    @pl.when(b == 6)
    def _():
        tb[...] = both(5)[0:8]


def spread_rest(t, n):
    rows = t.shape[1]
    f = jnp.float32
    wide = pl.BlockSpec((rows, 2 * n), lambda b: (b, 0))
    turned = pl.BlockSpec((2 * n, rows), lambda b: (0, b))
    square = jax.ShapeDtypeStruct((8 * rows, 2 * n), f)
    tall = jax.ShapeDtypeStruct((2 * n, 8 * rows), f)
    return pl.pallas_call(
        spread_rest_kernel,
        grid=(8,),
        in_specs=[pl.BlockSpec((2,) + t.shape[1:], lambda b: (pair_at(b), 0, 0))],
        out_specs=[wide, turned, turned, wide, wide, pl.BlockSpec((rows, 2 * n), lambda b: (jnp.minimum(b, 5), 0))]
        + [wide] * 3
        + [pl.BlockSpec((8, 2 * n), lambda b: (0, 0))],
        out_shape=[square, tall, tall, square, square, jax.ShapeDtypeStruct((6 * rows, 2 * n), f)]
        + [square] * 3
        + [jax.ShapeDtypeStruct((8, 2 * n), f)],
        compiler_params=pltpu.CompilerParams(vmem_limit_bytes=32 << 20),
        name="spread_rest",
        cost_estimate=pl.CostEstimate(flops=0, bytes_accessed=6 * t.size, transcendentals=0),
    )(t)


class Journey:
    def __init__(self, hops):
        self.hops = hops
        self.pending = next(hops)
        self.result = None

    def go(self, tied):
        try:
            self.pending = self.hops.send(tied)
        except StopIteration as end:
            self.pending, self.result = None, end.value


def onward(main, *journeys):
    journeys = [j for j in journeys if j.result is None]
    main, tied = lax.optimization_barrier((main, [j.pending for j in journeys]))
    for journey, sent in zip(journeys, tied):
        journey.go(sent)
    return main


def row_body(dp, *args):
    (
        frames,
        text_states,
        clip_lengths,
        text_lengths,
        cotangent,
        self_gain,
        self_shift,
        self_query,
        self_key,
        self_value,
        self_out,
        cross_gain,
        cross_shift,
        cross_query,
        cross_key,
        cross_value,
        cross_out,
        text_weight,
        text_bias,
        feed_gain,
        feed_shift,
        feed_in,
        feed_out,
    ) = args
    bf16, f32 = jnp.bfloat16, jnp.float32
    me = lax.axis_index("dp")
    half = lax.axis_index("mp")
    core = me % 2
    swap = [(0, 1), (1, 0)]
    steps = [2 << i for i in range(dp.bit_length() - 2)]

    def over_y(t):
        return jax.tree.map(lambda a: lax.ppermute(a, "mp", swap), t)

    def over_bit(t, step):
        return jax.tree.map(lambda a: lax.ppermute(a, "dp", [(i, i ^ step) for i in range(dp)]), t)

    def over_core(t):
        return over_bit(t, 1)

    def piece(t, at, size, axis):
        return lax.dynamic_slice_in_dim(t, at * size, size, axis)

    def ordered(mine_first, mine, theirs, axis):
        return jnp.concatenate(
            [jnp.where(mine_first, mine, theirs), jnp.where(mine_first, theirs, mine)], axis
        )

    def add(*ts):
        return reduce(jnp.add, [t.astype(f32) for t in ts]).astype(bf16)

    def parts_of(ts, step):
        at = (me // step) % 2
        size = ts[0].shape[0] // 2
        return [add(*[piece(t, w, size, 0) for t in ts]) for w in (at, 1 - at)]

    def travel(terms, left):
        for step in left:
            kept, sent = parts_of(terms, step)
            sent = yield sent
            terms = (kept, over_bit(sent, step))
        return add(*terms)

    def travel_y(own, other):
        other = yield other
        return (yield from travel((*own, over_y(other)), steps))

    def travel_small(t):
        for hop in (over_core, over_y, *[functools.partial(over_bit, step=s) for s in steps]):
            t = yield t
            t = t + hop(t)
        return t

    lengths = lax.dynamic_index_in_dim(clip_lengths, half, 0, keepdims=False)
    words = lax.dynamic_index_in_dim(text_lengths, half, 0, keepdims=False)
    clip_bounds, text_bounds = jnp.cumsum(lengths), jnp.cumsum(words)
    zeros = jnp.zeros_like(self_gain)
    vec = jnp.stack(
        [cross_gain, cross_shift, feed_gain, feed_shift, self_gain, zeros, zeros, zeros]
    )

    def quarter(t, which, axis):
        return piece(t, which, t.shape[axis] // 2, axis)

    tie = lax.optimization_barrier
    x_at = (me // 2) % 2

    def shared(mine, axis):
        return quarter(mine, x_at, axis)

    def joined(came, across, axis):
        return ordered(x_at == 0, came, across, axis)

    trio = (self_query, self_key, self_value)
    qkv_c = jnp.concatenate([quarter(t, core, 1) for t in trio], 1)
    qkv_d = jnp.concatenate([quarter(t, 1 - core, 1) for t in trio], 1)
    text_part = (product(text_states, text_weight) + text_bias).astype(bf16)
    qkv_half = shared(qkv_c, 0)
    cut = qkv_half.shape[0] // 2
    frames, text_part, qkv_1, qkv_2 = tie((frames, text_part, qkv_half[:cut], qkv_half[cut:]))
    text_came, qkv_1 = over_y(text_part), over_y(qkv_1)
    standard, _ = norm_parts(frames.astype(f32))
    self_rows = (standard * self_gain + self_shift).astype(bf16)
    qkv, ctx, log = [None] * 4, [None] * 4, [None] * 4
    qkv[0] = product(self_rows, qkv_c).astype(bf16)
    qkv[2] = product(self_rows, qkv_d).astype(bf16)
    qkv[0], qkv[2], text_came, qkv_1, qkv_2 = tie((qkv[0], qkv[2], text_came, qkv_1, qkv_2))
    text_full = ordered(half == 0, text_part, text_came, 1)
    keys_here = product(text_full, cross_key).astype(bf16)
    values_here = product(text_full, cross_value).astype(bf16)
    text_rows = TXT_ROW

    def row_of(t, which):
        return piece(t, which, text_rows, 0)

    kv_send = jnp.concatenate([row_of(keys_here, 1 - half), row_of(values_here, 1 - half)], 1)
    qkv_2, across_1 = over_y(qkv_2), over_bit(qkv_1, 2)
    ctx[0], log[0] = group_forward(clip_bounds, qkv[0])
    so_c, cq_c, co_c = quarter(self_out, core, 0), quarter(cross_query, core, 1), quarter(cross_out, core, 0)
    late = [shared(so_c, 0), shared(cq_c, 0), shared(co_c, 0)]
    ctx[0], qkv[2], qkv_2, across_1, kv_send, late = tie(
        (ctx[0], qkv[2], qkv_2, across_1, kv_send, late)
    )
    across_2 = over_bit(qkv_2, 2)
    kv_came = over_y(kv_send)
    so_h = over_y(late[0])
    ctx[2], log[2] = group_forward(clip_bounds, qkv[2])
    ctx[2], across_2, kv_came, so_h = tie((ctx[2], across_2, kv_came, so_h))
    qkv_oc = joined(jnp.concatenate([qkv_1, qkv_2]), jnp.concatenate([across_1, across_2]), 0)
    qkv_oc, rows_1, so_h = tie((qkv_oc, self_rows, so_h))
    qkv_od = over_core(qkv_oc)
    cq_h, so_x = over_y(late[1]), over_bit(so_h, 2)
    qkv[1] = product(rows_1, qkv_oc).astype(bf16)
    qkv[1], cq_h = tie((qkv[1], cq_h))
    co_h, cq_x = over_y(late[2]), over_bit(cq_h, 2)
    ctx[1], log[1] = group_forward(clip_bounds, qkv[1])
    qkv[3] = product(self_rows, qkv_od).astype(bf16)
    so_oc, cq_oc = joined(so_h, so_x, 0), joined(cq_h, cq_x, 0)
    qkv[3], ctx[1], co_h, so_oc, cq_oc = tie((qkv[3], ctx[1], co_h, so_oc, cq_oc))
    co_x = over_bit(co_h, 2)
    so_od, cq_od = over_core(so_oc), over_core(cq_oc)
    ctx[3], log[3] = group_forward(clip_bounds, qkv[3])
    co_oc = joined(co_h, co_x, 0)
    co_od = over_core(co_oc)
    width = cross_key.shape[1]

    def mixed(mine, theirs):
        mine = row_of(mine, half)
        return jnp.concatenate(
            [quarter(t, w, 1) for w in (core, 1 - core) for t in (mine, theirs)], 1
        )

    keys = mixed(keys_here, kv_came[:, :width])
    values = mixed(values_here, kv_came[:, width:])
    qkv_w = [qkv_c, qkv_oc, qkv_d, qkv_od]
    so = [so_c, so_oc, quarter(self_out, 1 - core, 0), so_od]
    cq = [cq_c, cq_oc, quarter(cross_query, 1 - core, 1), cq_od]
    co = [co_c, co_oc, quarter(cross_out, 1 - core, 0), co_od]
    block = 2 * core + x_at
    fi_s, fo_s = piece(feed_in, block, NB, 1), piece(feed_out, block, NB, 0)
    ctx, so, cq, co, keys, values, fi_s, fo_s = tie((ctx, so, cq, co, keys, values, fi_s, fo_s))
    fi_cx = over_y(fi_s)

    middle, cross_rows, cross_q, cross_ctx, cross_log, after, feed_rows, feed_t = mid_forward(
        clip_bounds, text_bounds, frames, ctx, so, cq, co, keys, values, vec
    )

    feed = (feed_rows, feed_t, cotangent)
    places = lambda *t: jnp.stack(t).astype(jnp.int32)
    feed, fi_cx, fo_s = tie((feed, fi_cx, fo_s))
    fo_cx, fi_cy = over_y(fo_s), over_bit(fi_cx, 2)
    o, e, in_od, out_od = feed_part(
        places(2 - 2 * core, 3 - 2 * core), *feed, after, after, [feed_in], [feed_out], True, False
    )
    o, e, fo_cx, fi_cy = tie((o, e, fo_cx, fi_cy))
    fo_cy = over_bit(fo_cx, 2)
    fi_d = over_core([fi_cx, fi_cy])
    o, e, in_oc, out_oc = feed_part(
        places(2 * core, 2 * core + 1), *feed, o, e, [feed_in], [feed_out], False, False
    )
    o, e, fo_cy, fi_d = tie((o, e, fo_cy, fi_d))
    fo_d = over_core([fo_cx, fo_cy])
    o, e, fo_d, in_od, out_od = tie((o, e, fo_d, in_od, out_od))
    in_og, out_og = over_core([in_od, out_od])
    where = places(x_at, 1 - x_at)
    o, e, in_td, out_td = feed_part(where, *feed, o, e, fi_d, fo_d, False, False)
    o, e, in_og, in_td, out_td = tie((o, e, in_og, in_td, out_td))
    own_low, own_high = parts_of((in_oc, in_og), 2)
    o, e, own_low, own_high = tie((o, e, own_low, own_high))
    in_tg, out_tg = over_core([in_td, out_td])
    own_came = over_bit(own_high, 2)
    output, e, in_tc, out_tc = feed_part(
        where, *feed, o, e, [fi_cx, fi_cy], [fo_cx, fo_cy], False, True
    )
    e, in_tg, out_tg, own_came = tie((e, in_tg, out_tg, own_came))
    other_low, other_high = parts_of((in_tc, in_tg), 2)

    def travel_in():
        sent = yield other_high
        other = yield add(other_low, over_bit(sent, 2))
        return (yield from travel((own_low, own_came, over_y(other)), steps[1:]))

    j_in = Journey(travel_in())
    middle_cut = out_tc.shape[1] // 2
    j_out = []
    for sl in (slice(0, middle_cut), slice(middle_cut, None)):
        j_out.append(
            Journey(
                travel_y((out_oc[:, sl], out_og[:, sl]), add(out_tc[:, sl], out_tg[:, sl]))
            )
        )
    e = onward(e, j_in, j_out[0])

    g_c, grad_q, g_middle, g_s, grad_ctx, grad_k, grad_v, sums = mid_backward(
        clip_bounds,
        text_bounds,
        e,
        after,
        cotangent,
        middle,
        cross_q,
        cross_ctx,
        cross_log,
        co,
        cq,
        so,
        keys,
        values,
        vec,
    )
    small = Journey(travel_small(sums[:4]))
    side = width

    def split_heads_back(t):
        oc, tc, od, td = [t[:, side // 2 * n : side // 2 * (n + 1)] for n in range(4)]
        return ordered(core == 0, oc, od, 1), ordered(core == 0, tc, td, 1)

    dk_own, dk_other = split_heads_back(grad_k)
    dv_own, dv_other = split_heads_back(grad_v)
    g_c, text_hop = tie((g_c, jnp.concatenate([dk_other, dv_other], 1)))
    text_hop = over_y(text_hop)
    (g_c, grad_q, g_s, grad_ctx) = onward(
        (g_c, grad_q, g_s, grad_ctx), j_out[0], j_out[1], small
    )

    def both(big, small):
        out = []
        for at in (0, side):
            t = outer_sum(big, small[:, at : at + side]).astype(bf16)
            out.append((t[:, : side // 2], t[:, side // 2 :]))
        return out

    ctx_all = [jnp.concatenate(ctx[:2], 1), jnp.concatenate(ctx[2:], 1)]
    wide = [both(cross_rows, grad_q), both(g_c, cross_ctx)]
    wide = onward(wide, j_in, *j_out, small)
    so_parts = [outer_sum(g_s, t).astype(bf16) for t in ctx_all]
    wide.append([(t[:, : side // 2], t[:, side // 2 :]) for t in so_parts])
    c_keep, c_send = [
        tuple(jnp.concatenate([w[n][m] for w in wide], 1) for m in range(2)) for n in range(2)
    ]

    def split_heads_back(t):
        oc, tc, od, td = [t[:, side // 2 * n : side // 2 * (n + 1)] for n in range(4)]
        return ordered(core == 0, oc, od, 1), ordered(core == 0, tc, td, 1)

    grad_ctx, c_send, text_hop = tie((grad_ctx, c_send, text_hop))
    c_got = over_core(c_send)
    dk = ordered(half == 0, dk_own, text_hop[:, :width], 0)
    dv = ordered(half == 0, dv_own, text_hop[:, width:], 0)
    grad_text = against(dk, cross_key) + against(dv, cross_value)
    text_mine = piece(grad_text, half, width, 1)
    text_hop = piece(grad_text, 1 - half, width, 1).astype(bf16)
    grad_ctx, text_mine, text_hop = tie((grad_ctx, text_mine, text_hop))
    text_hop = over_y(text_hop)

    grads, parts = [None] * 4, [None] * 4

    def kernel(n, main):
        grads[n] = group_backward(clip_bounds, qkv[n], ctx[n], main, log[n], n)

    def finish(n, main):
        parts[n] = outer_sum(self_rows, grads[n]).astype(bf16)
        main, parts[n] = tie((main, parts[n]))
        return main

    main = grad_ctx
    kernel(3, main)
    grads[3], c_got, text_hop = tie((grads[3], c_got, text_hop))
    grad_text = (text_mine + text_hop.astype(f32)).astype(bf16)
    text_part = against(grad_text, text_weight).astype(bf16)
    tall = text_full.shape[1] - text_states.shape[1]
    text_wide = jnp.concatenate(
        [
            text_states,
            jnp.ones((text_states.shape[0], 1), bf16),
            jnp.zeros((text_states.shape[0], tall - 1), bf16),
        ],
        1,
    )
    text_keep, text_send = [
        jnp.concatenate(
            [
                outer_sum(text_full, quarter(dk, w, 1)),
                outer_sum(text_full, quarter(dv, w, 1)),
                outer_sum(text_wide, quarter(grad_text, w, 1)),
            ],
            1,
        ).astype(bf16)
        for w in (core, 1 - core)
    ]
    c_cut = c_keep[0].shape[1] // 2
    j_wide = [
        Journey(
            travel_y((c_keep[0][:, sl], c_got[0][:, sl]), add(c_keep[1][:, sl], c_got[1][:, sl]))
        )
        for sl in (slice(0, c_cut), slice(c_cut, None))
    ]
    grads[3] = onward(grads[3], j_in, *j_out, j_wide[0], small)
    main = finish(3, main)
    main, parts[3], text_send = tie((main, parts[3], text_send))
    td_got, text_got = over_core(parts[3]), over_core(text_send)
    kernel(1, main)
    grads[1], td_got, text_got = tie((grads[1], td_got, text_got))
    j_text = Journey(travel((text_keep, text_got), steps))
    grads[1] = onward(grads[1], j_in, *j_out, j_text, small)
    main = finish(1, main)
    e_cut = parts[1].shape[0] // 2
    other = add(parts[1], td_got)
    main, other = tie((main, other))
    came_1 = over_y(other[:e_cut])
    def gathered(blocks):
        return lax.all_gather(jnp.concatenate(blocks, 1), "dp", axis=0, tiled=False)

    kernel(2, main)
    grads[2], came_1, text_part, blocks = tie(
        (grads[2], came_1, text_part, [j.result for j in (j_in, *j_out)])
    )
    feed_sum = gathered(blocks)
    grads[2] = onward(grads[2], j_wide[0], j_text)
    main = finish(2, main)
    od_got = over_core(parts[2])
    came_2, text_came = over_y(other[e_cut:]), over_y(text_part)
    kernel(0, main)
    grads[0], came_1, came_2, od_got, text_came = tie(
        (grads[0], came_1, came_2, od_got, text_came)
    )
    grads[0] = onward(grads[0], *j_wide, j_text)
    main = finish(0, main)
    text_grad = text_part.astype(f32) + text_came.astype(f32)
    j_self = Journey(travel((parts[0], od_got, jnp.concatenate([came_1, came_2])), steps))
    grads = onward(grads, j_self)
    frames_grad, self_sums = final_grads(frames, g_middle, grads, qkv_w, vec)
    last = Journey(travel_small(self_sums[:2]))
    everything = [j_in, *j_out, *j_wide, j_text, j_self, small, last]
    frames_grad = onward(frames_grad, *[j for j in everything if j.result is None])
    for journey in everything:
        while journey.result is None:
            journey.go(journey.pending)
    early, late = small.result, last.result
    rest_sum = gathered([j.result for j in (*j_wide, j_text, j_self)])

    feed_in_grad, feed_out_grad = spread_feed(feed_sum)
    cq_g, co_g, so_g, ck_g, cv_g, text_g, q_g, k_g, v_g, bias_g = spread_rest(rest_sum, side // 2)
    return (
        output,
        frames_grad,
        text_grad,
        late[0],
        late[1],
        q_g,
        k_g,
        v_g,
        so_g,
        early[2],
        early[3],
        cq_g,
        ck_g,
        cv_g,
        co_g,
        text_g,
        bias_g[0],
        early[0],
        early[1],
        feed_in_grad,
        feed_out_grad.reshape(feed_out.shape),
    )


def chosen(dp, mp, *args):
    rows_here, frames_here = args[2].shape[0], args[0].shape[0]
    if mp == 2 and dp == 16 and rows_here == mp and frames_here == ROW_LEN:
        return row_body(dp, *args)
    return body(*args)


def solution(mesh):
    return jax.shard_map(
        functools.partial(chosen, mesh.shape["dp"], mesh.shape["mp"]),
        mesh=mesh,
        in_specs=(
            P(("dp", "mp"), None),
            P("dp", None),
            P("dp", None),
            P("dp", None),
            P(("dp", "mp"), None),
            P(),
            P(),
            P(None, "mp"),
            P(None, "mp"),
            P(None, "mp"),
            P("mp", None),
            P(),
            P(),
            P(None, "mp"),
            P(None, "mp"),
            P(None, "mp"),
            P("mp", None),
            P(None, "mp"),
            P("mp"),
            P(),
            P(),
            P(None, "mp"),
            P("mp", None),
        ),
        out_specs=(
            P(("dp", "mp"), None),
            P(("dp", "mp"), None),
            P("dp", None),
            P(),
            P(),
            P(None, "mp"),
            P(None, "mp"),
            P(None, "mp"),
            P("mp", None),
            P(),
            P(),
            P(None, "mp"),
            P(None, "mp"),
            P(None, "mp"),
            P("mp", None),
            P(None, "mp"),
            P("mp"),
            P(),
            P(),
            P(None, "mp"),
            P("mp", None),
        ),
        check_vma=False,
    )
```

```python
import functools
from functools import reduce

import jax
import jax.numpy as jnp
from jax import lax
from jax.experimental import pallas as pl
from jax.experimental.pallas import tpu as pltpu
from jax.sharding import PartitionSpec as P

HEAD_DIM = 64
ROW_LEN = 1536
TXT_ROW = 128


EPSILON = 1e-05
MASKED = -1e30


def product(left_side, right_side):
    return jnp.dot(left_side, right_side, preferred_element_type=jnp.float32)


def against(left_side, right_side):
    return lax.dot_general(
        left_side, right_side, (((1,), (1,)), ((), ())), preferred_element_type=jnp.float32
    )


def outer_sum(left_side, right_side):
    return lax.dot_general(
        left_side, right_side, (((0,), (0,)), ((), ())), preferred_element_type=jnp.float32
    )


def exact_gelu(tensor):
    return jax.nn.gelu(tensor, approximate=False)


def segment_ids(lengths, positions):
    bounds = jnp.cumsum(lengths, axis=-1)
    places = jnp.arange(positions, dtype=jnp.int32)
    return jnp.sum((places[None, :, None] >= bounds[:, None, :]).astype(jnp.int32), axis=-1)


def split_heads(tensor, row_count):
    return tensor.reshape(
        row_count, tensor.shape[0] // row_count, tensor.shape[1] // HEAD_DIM, HEAD_DIM
    )


def norm_parts(tensor):
    average = jnp.mean(tensor, axis=-1, keepdims=True)
    centered = tensor - average
    inverse = lax.rsqrt(jnp.mean(centered * centered, axis=-1, keepdims=True) + EPSILON)
    return (centered * inverse, inverse)


def norm_back(gradient, standard, inverse, norm_gain):
    scaled = gradient * norm_gain
    first_mean = jnp.mean(scaled, axis=-1, keepdims=True)
    second_mean = jnp.mean(scaled * standard, axis=-1, keepdims=True)
    return (
        inverse * (scaled - first_mean - standard * second_mean),
        jnp.sum(gradient * standard, axis=0),
        jnp.sum(gradient, axis=0),
    )


def spread_rows(tensor):
    return lax.all_gather(tensor, "mp", axis=0, tiled=True)


def spread_cotangent(tensor):
    return lax.all_gather(tensor, "mp", axis=0, tiled=True)


def branch_sum(left_side, right_side):
    return lax.psum_scatter(product(left_side, right_side), "mp", scatter_dimension=0, tiled=True)


def input_grads(factor_pairs):
    partials = [against(left_side, right_side) for left_side, right_side in factor_pairs]
    return lax.psum_scatter(reduce(jnp.add, partials), "mp", scatter_dimension=0, tiled=True)


def attend_forward(queries, key_heads, values, allowed):
    scores = jnp.einsum(
        "rqhd,rkhd->rhqk", queries, key_heads, preferred_element_type=jnp.float32
    ) * HEAD_DIM ** (-0.5)
    scores = jnp.where(allowed[:, None], scores, MASKED)
    row_max = jnp.max(scores, axis=-1, keepdims=True)
    shifted = jnp.exp(scores - row_max)
    totals = jnp.sum(shifted, axis=-1, keepdims=True)
    soft_weights = (shifted / totals).astype(jnp.bfloat16)
    context = jnp.einsum(
        "rhqk,rkhd->rqhd", soft_weights, values, preferred_element_type=jnp.float32
    )
    return (context, row_max + jnp.log(totals))


def attend_back(queries, key_heads, values, allowed, log_totals, grad_context):
    score_scale = HEAD_DIM ** (-0.5)
    scores = (
        jnp.einsum("rqhd,rkhd->rhqk", queries, key_heads, preferred_element_type=jnp.float32)
        * score_scale
    )
    scores = jnp.where(allowed[:, None], scores, MASKED)
    soft_weights = jnp.exp(scores - log_totals)
    grad_soft = jnp.einsum(
        "rqhd,rkhd->rhqk", grad_context, values, preferred_element_type=jnp.float32
    )
    row_inner = jnp.sum(grad_soft * soft_weights, axis=-1, keepdims=True)
    grad_scores = (soft_weights * (grad_soft - row_inner)).astype(jnp.bfloat16)
    grad_query = (
        jnp.einsum("rhqk,rkhd->rqhd", grad_scores, key_heads, preferred_element_type=jnp.float32)
        * score_scale
    )
    grad_keys = (
        jnp.einsum("rhqk,rqhd->rkhd", grad_scores, queries, preferred_element_type=jnp.float32)
        * score_scale
    )
    grad_values = jnp.einsum(
        "rhqk,rqhd->rkhd",
        soft_weights.astype(jnp.bfloat16),
        grad_context,
        preferred_element_type=jnp.float32,
    )
    return (grad_query, grad_keys, grad_values)


def self_allowed(segments, start_at, stop_at):
    places = jnp.arange(stop_at, dtype=jnp.int32)
    same_clip = segments[:, start_at:stop_at, None] == segments[:, None, :stop_at]
    return same_clip & (places[start_at:stop_at, None] >= places[None, :])[None]


def self_forward(queries, key_heads, values, segments):
    block_size = min(512, queries.shape[1])
    contexts = []
    log_totals = []
    for start_at in range(0, queries.shape[1], block_size):
        stop_at = start_at + block_size
        context, log_total = attend_forward(
            queries[:, start_at:stop_at],
            key_heads[:, :stop_at],
            values[:, :stop_at],
            self_allowed(segments, start_at, stop_at),
        )
        contexts.append(context)
        log_totals.append(log_total)
    return (jnp.concatenate(contexts, axis=1), jnp.concatenate(log_totals, axis=2))


def self_back(queries, key_heads, values, segments, log_totals, grad_context):
    block_size = min(512, queries.shape[1])
    query_parts = []
    grad_keys = jnp.zeros(key_heads.shape, jnp.float32)
    grad_values = jnp.zeros(values.shape, jnp.float32)
    for start_at in range(0, queries.shape[1], block_size):
        stop_at = start_at + block_size
        grad_query, key_part, value_part = attend_back(
            queries[:, start_at:stop_at],
            key_heads[:, :stop_at],
            values[:, :stop_at],
            self_allowed(segments, start_at, stop_at),
            log_totals[:, :, start_at:stop_at],
            grad_context[:, start_at:stop_at],
        )
        query_parts.append(grad_query)
        grad_keys = grad_keys.at[:, :stop_at].add(key_part)
        grad_values = grad_values.at[:, :stop_at].add(value_part)
    return (jnp.concatenate(query_parts, axis=1), grad_keys, grad_values)


def body(
    frames,
    text_states,
    clip_lengths,
    text_lengths,
    cotangent,
    self_gain,
    self_shift,
    self_query,
    self_key,
    self_value,
    self_out,
    cross_gain,
    cross_shift,
    cross_query,
    cross_key,
    cross_value,
    cross_out,
    text_weight,
    text_bias,
    feed_gain,
    feed_shift,
    feed_in,
    feed_out,
):
    row_count = clip_lengths.shape[0]
    clip_segs = segment_ids(clip_lengths, ROW_LEN)
    text_segs = segment_ids(text_lengths, TXT_ROW)
    residual = frames.astype(jnp.float32)
    self_standard, self_inverse = norm_parts(residual)
    self_rows = spread_rows((self_standard * self_gain + self_shift).astype(jnp.bfloat16))
    self_queries = product(self_rows, self_query).astype(jnp.bfloat16)
    self_keys = product(self_rows, self_key).astype(jnp.bfloat16)
    self_values = product(self_rows, self_value).astype(jnp.bfloat16)
    self_context, self_logs = self_forward(
        split_heads(self_queries, row_count),
        split_heads(self_keys, row_count),
        split_heads(self_values, row_count),
        clip_segs,
    )
    self_context = self_context.reshape(self_queries.shape).astype(jnp.bfloat16)
    middle = residual + branch_sum(self_context, self_out)
    cross_standard, cross_inverse = norm_parts(middle)
    cross_rows = spread_rows((cross_standard * cross_gain + cross_shift).astype(jnp.bfloat16))
    text_part = (product(text_states, text_weight) + text_bias).astype(jnp.bfloat16)
    text_full = lax.all_gather(text_part, "mp", axis=1, tiled=True)
    cross_queries = product(cross_rows, cross_query).astype(jnp.bfloat16)
    cross_keys = product(text_full, cross_key).astype(jnp.bfloat16)
    cross_values = product(text_full, cross_value).astype(jnp.bfloat16)
    cross_allowed = clip_segs[:, :, None] == text_segs[:, None, :]
    cross_context, cross_logs = attend_forward(
        split_heads(cross_queries, row_count),
        split_heads(cross_keys, row_count),
        split_heads(cross_values, row_count),
        cross_allowed,
    )
    cross_context = cross_context.reshape(cross_queries.shape).astype(jnp.bfloat16)
    after_cross = middle + branch_sum(cross_context, cross_out)
    feed_standard, feed_inverse = norm_parts(after_cross)
    feed_normed = (feed_standard * feed_gain + feed_shift).astype(jnp.bfloat16)
    feed_rows = spread_rows(feed_normed)
    hidden = product(feed_rows, feed_in)
    active, gelu_back = jax.vjp(exact_gelu, hidden)
    active = active.astype(jnp.bfloat16)
    output = after_cross + branch_sum(active, feed_out)
    grad_output = cotangent.astype(jnp.float32)
    feed_cotangent = grad_output.astype(jnp.bfloat16)
    grad_rows = spread_cotangent(feed_cotangent)
    feed_out_grad = outer_sum(active, grad_rows)
    grad_hidden = gelu_back(against(grad_rows, feed_out))[0].astype(jnp.bfloat16)
    feed_in_grad = outer_sum(feed_rows, grad_hidden)
    grad_feed_normed = input_grads(((grad_hidden, feed_in),))
    grad_norm, feed_gain_grad, feed_shift_grad = norm_back(
        grad_feed_normed, feed_standard, feed_inverse, feed_gain
    )
    grad_after = grad_output + grad_norm
    cross_cotangent = spread_cotangent(grad_after.astype(jnp.bfloat16))
    cross_out_grad = outer_sum(cross_context, cross_cotangent)
    grad_context = against(cross_cotangent, cross_out).astype(jnp.bfloat16)
    grad_queries, grad_keys, grad_values = attend_back(
        split_heads(cross_queries, row_count),
        split_heads(cross_keys, row_count),
        split_heads(cross_values, row_count),
        cross_allowed,
        cross_logs,
        split_heads(grad_context, row_count),
    )
    grad_queries = grad_queries.reshape(cross_queries.shape).astype(jnp.bfloat16)
    grad_keys = grad_keys.reshape(cross_keys.shape).astype(jnp.bfloat16)
    grad_values = grad_values.reshape(cross_values.shape).astype(jnp.bfloat16)
    cross_query_grad = outer_sum(cross_rows, grad_queries)
    cross_key_grad = outer_sum(text_full, grad_keys)
    cross_value_grad = outer_sum(text_full, grad_values)
    grad_text_full = against(grad_keys, cross_key) + against(grad_values, cross_value)
    grad_text = lax.psum_scatter(
        grad_text_full.astype(jnp.bfloat16), "mp", scatter_dimension=1, tiled=True
    )
    text_weight_grad = outer_sum(text_states, grad_text)
    text_bias_grad = jnp.sum(grad_text.astype(jnp.float32), axis=0)
    text_grad = lax.psum(against(grad_text, text_weight).astype(jnp.bfloat16), "mp").astype(
        jnp.float32
    )
    grad_cross_normed = input_grads(((grad_queries, cross_query),))
    grad_norm, cross_gain_grad, cross_shift_grad = norm_back(
        grad_cross_normed, cross_standard, cross_inverse, cross_gain
    )
    grad_middle = grad_after + grad_norm
    self_cotangent = spread_cotangent(grad_middle.astype(jnp.bfloat16))
    self_out_grad = outer_sum(self_context, self_cotangent)
    grad_context = against(self_cotangent, self_out).astype(jnp.bfloat16)
    grad_queries, grad_keys, grad_values = self_back(
        split_heads(self_queries, row_count),
        split_heads(self_keys, row_count),
        split_heads(self_values, row_count),
        clip_segs,
        self_logs,
        split_heads(grad_context, row_count),
    )
    grad_queries = grad_queries.reshape(self_queries.shape).astype(jnp.bfloat16)
    grad_keys = grad_keys.reshape(self_keys.shape).astype(jnp.bfloat16)
    grad_values = grad_values.reshape(self_values.shape).astype(jnp.bfloat16)
    self_query_grad = outer_sum(self_rows, grad_queries)
    self_key_grad = outer_sum(self_rows, grad_keys)
    self_value_grad = outer_sum(self_rows, grad_values)
    grad_self_normed = input_grads(
        ((grad_queries, self_query), (grad_keys, self_key), (grad_values, self_value))
    )
    grad_norm, self_gain_grad, self_shift_grad = norm_back(
        grad_self_normed, self_standard, self_inverse, self_gain
    )
    frames_grad = grad_middle + grad_norm
    (
        self_query_grad,
        self_key_grad,
        self_value_grad,
        self_out_grad,
        cross_query_grad,
        cross_key_grad,
        cross_value_grad,
        cross_out_grad,
        text_weight_grad,
        text_bias_grad,
        feed_in_grad,
        feed_out_grad,
    ) = (
        lax.psum(self_query_grad.astype(jnp.bfloat16), "dp").astype(jnp.float32),
        lax.psum(self_key_grad.astype(jnp.bfloat16), "dp").astype(jnp.float32),
        lax.psum(self_value_grad.astype(jnp.bfloat16), "dp").astype(jnp.float32),
        lax.psum(self_out_grad.astype(jnp.bfloat16), "dp").astype(jnp.float32),
        lax.psum(cross_query_grad.astype(jnp.bfloat16), "dp").astype(jnp.float32),
        lax.psum(cross_key_grad.astype(jnp.bfloat16), "dp").astype(jnp.float32),
        lax.psum(cross_value_grad.astype(jnp.bfloat16), "dp").astype(jnp.float32),
        lax.psum(cross_out_grad.astype(jnp.bfloat16), "dp").astype(jnp.float32),
        lax.psum(text_weight_grad.astype(jnp.bfloat16), "dp").astype(jnp.float32),
        lax.psum(text_bias_grad.astype(jnp.bfloat16), "dp").astype(jnp.float32),
        lax.psum(feed_in_grad.astype(jnp.bfloat16), "dp").astype(jnp.float32),
        lax.psum(feed_out_grad.astype(jnp.bfloat16), "dp").astype(jnp.float32),
    )
    (
        self_gain_grad,
        self_shift_grad,
        cross_gain_grad,
        cross_shift_grad,
        feed_gain_grad,
        feed_shift_grad,
    ) = lax.psum(
        (
            self_gain_grad,
            self_shift_grad,
            cross_gain_grad,
            cross_shift_grad,
            feed_gain_grad,
            feed_shift_grad,
        ),
        ("dp", "mp"),
    )
    return (
        output.astype(jnp.bfloat16),
        frames_grad,
        text_grad,
        self_gain_grad,
        self_shift_grad,
        self_query_grad,
        self_key_grad,
        self_value_grad,
        self_out_grad,
        cross_gain_grad,
        cross_shift_grad,
        cross_query_grad,
        cross_key_grad,
        cross_value_grad,
        cross_out_grad,
        text_weight_grad,
        text_bias_grad,
        feed_gain_grad,
        feed_shift_grad,
        feed_in_grad,
        feed_out_grad,
    )


LOG2E=1.4426950408889634
SCALE2=LOG2E*HEAD_DIM**-0.5
BQ=256
SPAN=768

def dot(a,b,ca,cb):
    return lax.dot_general(a,b,(((ca,),(cb,)),((),())),preferred_element_type=jnp.float32)

def starts_of(bounds_ref, places):
    start=jnp.zeros_like(places)
    for k in range(3):
        start=jnp.where(places>=bounds_ref[k],bounds_ref[k],start)
    return start

def self_fwd_kernel(bounds_ref,q_ref,k_ref,v_ref,o_ref,lse_ref,*,ahead=2):
    low=lax.broadcasted_iota(jnp.int32,(1,128),1)<HEAD_DIM
    vt=jnp.transpose(v_ref[...])
    pad=jnp.ones((16,ROW_LEN),jnp.bfloat16)
    vts=[jnp.concatenate([vt[64*h:64*h+64],pad],0) for h in range(2)]
    def span(i):
        return max(0,BQ*i-SPAN),BQ*(i+1)
    def scores(i,h):
        k0,k1=span(i)
        q=q_ref[BQ*i:k1,:]
        qh=jnp.where(low==(h==0),q,jnp.zeros_like(q))
        places=BQ*i+lax.broadcasted_iota(jnp.int32,(1,BQ),1)
        keys=k0+lax.broadcasted_iota(jnp.int32,(k1-k0,BQ),0)
        allowed=(keys>=starts_of(bounds_ref,places))&(keys<=places)
        return jnp.where(allowed,dot(k_ref[k0:k1,:],qh,1,1),MASKED)
    items=[(i,h) for i in range(ROW_LEN//BQ) for h in range(2)]
    queue=[scores(*it) for it in items[:ahead]]
    outs=[]
    for n,(i,h) in enumerate(items):
        if n+ahead<len(items):
            queue.append(scores(*items[n+ahead]))
        s=queue.pop(0)
        k0,k1=span(i)
        m=jnp.max(s,axis=0,keepdims=True)
        p=jnp.exp2((s-m)*SCALE2)
        o=dot(vts[h][:,k0:k1],p.astype(jnp.bfloat16),1,0)
        l=o[64:65]
        outs.append(o[:64]*(1.0/l))
        lse_ref[0,h:h+1,BQ*i:k1]=m*SCALE2+jnp.log2(l)
        if h==1:
            o_ref[BQ*i:k1,:]=jnp.transpose(jnp.concatenate(outs,0)).astype(jnp.bfloat16)
            outs=[]

def self_bwd_kernel(bounds_ref,q_ref,k_ref,v_ref,o_ref,g_ref,lse_ref,out_ref,acc_ref,d_ref,*,mode="t",ahead=1):
    low=lax.broadcasted_iota(jnp.int32,(1,128),1)<HEAD_DIM
    n=ROW_LEN//BQ
    pair=pl.program_id(0)
    width=128*pl.num_programs(0)
    def put(which,sl,t):
        at=pl.multiple_of(which*width+pair*128,128)
        out_ref[sl,pl.ds(at,128)]=t.astype(jnp.bfloat16)

    for i in range(n):
        sl=slice(BQ*i,BQ*(i+1))
        t=jnp.transpose(g_ref[sl,:].astype(jnp.float32)*o_ref[sl,:].astype(jnp.float32))
        d_ref[0:1,sl]=jnp.sum(t[:64],axis=0,keepdims=True)
        d_ref[1:2,sl]=jnp.sum(t[64:],axis=0,keepdims=True)
    acc_ref[...]=jnp.zeros_like(acc_ref)
    def span(j):
        return BQ*j,min(ROW_LEN,BQ*(j+1)+SPAN)
    def masked(ref,j,h):
        t=ref[BQ*j:BQ*(j+1),:]
        return jnp.where(low==(h==0),t,jnp.zeros_like(t))
    def scores(j,h):
        q0,q1=span(j)
        places=q0+lax.broadcasted_iota(jnp.int32,(1,q1-q0),1)
        keys=BQ*j+lax.broadcasted_iota(jnp.int32,(BQ,q1-q0),0)
        allowed=(keys>=starts_of(bounds_ref,places))&(keys<=places)
        s=dot(masked(k_ref,j,h),q_ref[q0:q1,:],1,1)*SCALE2-lse_ref[0,h:h+1,q0:q1]
        return jnp.where(allowed,s,MASKED),dot(masked(v_ref,j,h),g_ref[q0:q1,:],1,1)
    items=[(j,h) for j in range(n) for h in range(2)]
    queue=[scores(*it) for it in items[:ahead]]
    dks=[];dvs=[]
    for t,(j,h) in enumerate(items):
        if t+ahead<len(items):
            queue.append(scores(*items[t+ahead]))
        s,dp=queue.pop(0)
        sl=slice(BQ*j,BQ*(j+1))
        q0,q1=span(j)
        p=jnp.exp2(s)
        ds=(p*(dp-d_ref[h:h+1,q0:q1])).astype(jnp.bfloat16)
        dvs.append(dot(p.astype(jnp.bfloat16),g_ref[q0:q1,:],1,0))
        dks.append(dot(ds,q_ref[q0:q1,:],1,0))
        if mode=="t":
            kt=jnp.transpose(k_ref[sl,:])
            acc_ref[64*h:64*h+64,q0:q1]+=dot(kt[64*h:64*h+64],ds,1,0)
        else:
            acc_ref[q0:q1,:]+=dot(ds,masked(k_ref,j,h),0,0)
        if h==1:
            put(1,sl,jnp.where(low,dks[0],dks[1])*HEAD_DIM**-0.5)
            put(2,sl,jnp.where(low,dvs[0],dvs[1]))
            dks=[];dvs=[]
            acc=jnp.transpose(acc_ref[:,sl]) if mode=="t" else acc_ref[sl,:]
            put(0,sl,acc*HEAD_DIM**-0.5)


def group_forward(bounds,qkv):
    width=qkv.shape[1]//3
    pairs=width//128
    spec=lambda t: pl.BlockSpec((ROW_LEN,128),lambda h:(0,t*pairs+h))
    return pl.pallas_call(self_fwd_kernel,grid=(pairs,),
        in_specs=[pl.BlockSpec(memory_space=pltpu.SMEM),spec(0),spec(1),spec(2)],
        out_specs=[spec(0),pl.BlockSpec((1,2,ROW_LEN),lambda h:(h,0,0))],
        out_shape=[jax.ShapeDtypeStruct((ROW_LEN,width),jnp.bfloat16),jax.ShapeDtypeStruct((pairs,2,ROW_LEN),jnp.float32)],
        compiler_params=pltpu.CompilerParams(vmem_limit_bytes=40<<20),
        name="self_forward",
        cost_estimate=pl.CostEstimate(flops=pairs*2*18*256*256*64*4*4,bytes_accessed=pairs*4*1536*256,transcendentals=0),
    )(bounds,qkv,qkv,qkv)

def group_backward(bounds,qkv,o,g,lse,group):
    width=qkv.shape[1]//3
    pairs=width//128
    spec=lambda t: pl.BlockSpec((ROW_LEN,128),lambda h:(0,t*pairs+h))
    return pl.pallas_call(self_bwd_kernel,grid=(pairs,),
        in_specs=[pl.BlockSpec(memory_space=pltpu.SMEM),spec(0),spec(1),spec(2),spec(0),spec(group),pl.BlockSpec((1,2,ROW_LEN),lambda h:(h,0,0))],
        out_specs=pl.BlockSpec((ROW_LEN,3*width),lambda h:(0,0)),
        out_shape=jax.ShapeDtypeStruct(qkv.shape,jnp.bfloat16),
        scratch_shapes=[pltpu.VMEM((128,ROW_LEN),jnp.float32),pltpu.VMEM((8,ROW_LEN),jnp.float32)],
        compiler_params=pltpu.CompilerParams(vmem_limit_bytes=48<<20),
        name="self_backward",
        cost_estimate=pl.CostEstimate(flops=pairs*2*18*256*256*64*10*4,bytes_accessed=pairs*8*1536*256,transcendentals=0),
    )(bounds,qkv,qkv,qkv,o,g,lse)

def token_range(cb_ref,tb_ref,places):
    lo=jnp.zeros_like(places); hi=jnp.full_like(places,0)+tb_ref[0]
    for c in range(3):
        past=places>=cb_ref[c]
        lo=jnp.where(past,tb_ref[c],lo)
        hi=jnp.where(past,tb_ref[c+1],hi)
    return lo,hi


INV_SQRT_2PI = 0.3989422804014327
TB = 256
NB = 512


def mean_row(t):
    return jnp.sum(t, axis=-1, keepdims=True) * (1.0 / t.shape[-1])


def standardise(t):
    centered = t - mean_row(t)
    inverse = lax.rsqrt(mean_row(centered * centered) + EPSILON)
    return centered * inverse, inverse


def norm_input_grad(e, standard, inverse, gain):
    scaled = e * gain
    return inverse * (scaled - mean_row(scaled) - standard * mean_row(scaled * standard))


def column_sums(t):
    return jnp.sum(t, axis=0, keepdims=True)


def gelu_pair(hidden):
    density = jnp.exp2(hidden * hidden * (-0.5 * LOG2E)) * INV_SQRT_2PI
    t = 1.0 / (1.0 + 0.2316419 * jnp.abs(hidden))
    series = t * (
        0.319381530
        + t * (-0.356563782 + t * (1.781477937 + t * (-1.821255978 + t * 1.330274429)))
    )
    tail = density * series
    below = jnp.where(hidden >= 0, 1.0 - tail, tail)
    return hidden * below, below + hidden * density


def mid_forward_kernel(
    count, cb_ref, tb_ref, x_ref, *refs,
):
    ctxs, sos, cqs, cos = [refs[count * t : count * t + count] for t in range(4)]
    (k_ref, v_ref, vec_ref,
     mid_ref, rows_ref, q_ref, cctx_ref, lse_ref, after_ref, feed_ref, feedt_ref, vt_ref) = refs[4 * count :]
    i = pl.program_id(0)
    low = lax.broadcasted_iota(jnp.int32, (1, 128), 1) < HEAD_DIM

    @pl.when(i == 0)
    def _():
        vt_ref[0:1024, :] = jnp.transpose(v_ref[...])
        vt_ref[1024:1040, :] = jnp.ones((16, TXT_ROW), jnp.bfloat16)

    middle = x_ref[...].astype(jnp.float32)
    for c, w in zip(ctxs, sos):
        middle = middle + dot(c[...], w[...], 1, 0)
    mid_ref[...] = middle
    u, _ = standardise(middle)
    rows = (u * vec_ref[0:1, :] + vec_ref[1:2, :]).astype(jnp.bfloat16)
    rows_ref[...] = rows
    at = 0
    for w in cqs:
        n = w.shape[1]
        q_ref[:, at : at + n] = dot(rows, w[...], 1, 0).astype(jnp.bfloat16)
        at += n
    places = TB * i + lax.broadcasted_iota(jnp.int32, (1, TB), 1)
    lo, hi = token_range(cb_ref, tb_ref, places)
    toks = lax.broadcasted_iota(jnp.int32, (TXT_ROW, TB), 0)
    allowed = (toks >= lo) & (toks < hi)

    def scores(head):
        p, h = head // 2, head % 2
        k = k_ref[:, 128 * p : 128 * p + 128]
        kh = jnp.where(low == (h == 0), k, jnp.zeros_like(k))
        return jnp.where(allowed, dot(kh, q_ref[:, 128 * p : 128 * p + 128], 1, 1), MASKED)

    ahead = 3
    queue = [scores(t) for t in range(ahead)]
    outs = []
    ones = vt_ref[1024:1040, :]
    for head in range(16):
        if head + ahead < 16:
            queue.append(scores(head + ahead))
        s = queue.pop(0)
        m = jnp.max(s, axis=0, keepdims=True)
        p = jnp.exp2((s - m) * SCALE2)
        vt = jnp.concatenate([vt_ref[64 * head : 64 * head + 64, :], ones], 0)
        o = dot(vt, p.astype(jnp.bfloat16), 1, 0)
        l = o[64:65]
        outs.append(o[:64] * (1.0 / l))
        lse_ref[head : head + 1, :] = m * SCALE2 + jnp.log2(l)
        if head % 2 == 1:
            pair = head // 2
            cctx_ref[:, 128 * pair : 128 * pair + 128] = jnp.transpose(
                jnp.concatenate(outs, 0)
            ).astype(jnp.bfloat16)
            outs = []
    after = mid_ref[...]
    at = 0
    for w in cos:
        n = w.shape[0]
        after = after + dot(cctx_ref[:, at : at + n], w[...], 1, 0)
        at += n
    after_ref[...] = after
    u, _ = standardise(after)
    feed = (u * vec_ref[2:3, :] + vec_ref[3:4, :]).astype(jnp.bfloat16)
    feed_ref[...] = feed
    feedt_ref[...] = jnp.transpose(feed)


def row_block(n):
    return pl.BlockSpec((TB, n), lambda i: (i, 0))


def whole(t):
    return pl.BlockSpec(t.shape, lambda i: (0,) * t.ndim)


def mid_forward(cb, tb, x, ctxs, sos, cqs, cos, k, v, vec):
    n, d = x.shape
    smem = pl.BlockSpec(memory_space=pltpu.SMEM)
    bf, f = jnp.bfloat16, jnp.float32
    weights = [*sos, *cqs, *cos, k, v, vec]
    return pl.pallas_call(
        functools.partial(mid_forward_kernel, len(ctxs)),
        grid=(n // TB,),
        in_specs=[smem, smem, row_block(d)] + [row_block(c.shape[1]) for c in ctxs] + [whole(w) for w in weights],
        out_specs=[row_block(d)] * 4
        + [pl.BlockSpec((16, TB), lambda i: (0, i))]
        + [row_block(d)] * 2
        + [pl.BlockSpec((d, TB), lambda i: (0, i))],
        out_shape=[jax.ShapeDtypeStruct((n, d), t) for t in (f, bf, bf, bf)]
        + [jax.ShapeDtypeStruct((16, n), f)]
        + [jax.ShapeDtypeStruct((n, d), t) for t in (f, bf)]
        + [jax.ShapeDtypeStruct((d, n), bf)],
        scratch_shapes=[pltpu.VMEM((1040, TXT_ROW), bf)],
        compiler_params=pltpu.CompilerParams(vmem_limit_bytes=56 << 20),
        name="mid_forward",
        cost_estimate=pl.CostEstimate(flops=24 * n * d * d // 2, bytes_accessed=40 * n * d // 2, transcendentals=0),
    )(cb, tb, x, *ctxs, *weights)


def mid_backward_kernel(
    count, cb_ref, tb_ref, e_ref, after_ref, g_ref, mid_ref, q_ref, cctx_ref, lse_ref, *refs,
):
    cos, cqs, sos = [refs[count * t : count * t + count] for t in range(3)]
    (k_ref, v_ref, vec_ref,
     gc_ref, gq_ref, gmid_ref, gs_ref, gctx_ref, dk_ref, dv_ref, sums_ref,
     kt_ref, dka_ref, dva_ref, gcc_ref) = refs[3 * count :]
    i = pl.program_id(0)
    low = lax.broadcasted_iota(jnp.int32, (1, 128), 1) < HEAD_DIM

    @pl.when(i == 0)
    def _():
        kt_ref[...] = jnp.transpose(k_ref[...])
        dka_ref[...] = jnp.zeros_like(dka_ref)
        dva_ref[...] = jnp.zeros_like(dva_ref)
        sums_ref[...] = jnp.zeros_like(sums_ref)

    e = e_ref[...]
    u, inverse = standardise(after_ref[...])
    sums_ref[0:1, :] += column_sums(e * u)
    sums_ref[1:2, :] += column_sums(e)
    g_after = g_ref[...].astype(jnp.float32) + norm_input_grad(e, u, inverse, vec_ref[2:3, :])
    gmid_ref[...] = g_after
    gc = g_after.astype(jnp.bfloat16)
    gc_ref[...] = gc
    at = 0
    for w in cos:
        n = w.shape[0]
        gcc_ref[:, at : at + n] = dot(gc, w[...], 1, 1).astype(jnp.bfloat16)
        at += n
    places = TB * i + lax.broadcasted_iota(jnp.int32, (1, TB), 1)
    lo, hi = token_range(cb_ref, tb_ref, places)
    toks = lax.broadcasted_iota(jnp.int32, (TXT_ROW, TB), 0)
    allowed = (toks >= lo) & (toks < hi)

    def scores(head):
        p, h = head // 2, head % 2
        sl = slice(128 * p, 128 * p + 128)
        pick = lambda t: jnp.where(low == (h == 0), t, jnp.zeros_like(t))
        s = dot(pick(k_ref[:, sl]), q_ref[:, sl], 1, 1) * SCALE2 - lse_ref[head : head + 1, :]
        return jnp.where(allowed, s, MASKED), dot(pick(v_ref[:, sl]), gcc_ref[:, sl], 1, 1)

    ahead = 2
    queue = [scores(t) for t in range(ahead)]
    dqs, dks, dvs = [], [], []
    for head in range(16):
        if head + ahead < 16:
            queue.append(scores(head + ahead))
        p_at, h = head // 2, head % 2
        sl = slice(128 * p_at, 128 * p_at + 128)
        if h == 0:
            t = jnp.transpose(
                gcc_ref[:, sl].astype(jnp.float32) * cctx_ref[:, sl].astype(jnp.float32)
            )
        s, dp = queue.pop(0)
        p = jnp.exp2(s)
        ds = (p * (dp - column_sums(t[64 * h : 64 * h + 64]))).astype(jnp.bfloat16)
        dvs.append(dot(p.astype(jnp.bfloat16), gcc_ref[:, sl], 1, 0))
        dks.append(dot(ds, q_ref[:, sl], 1, 0))
        dqs.append(dot(kt_ref[64 * head : 64 * head + 64, :], ds, 1, 0))
        if h == 1:
            gq_ref[:, sl] = (
                jnp.transpose(jnp.concatenate(dqs, 0)) * HEAD_DIM**-0.5
            ).astype(jnp.bfloat16)
            dka_ref[:, sl] += jnp.where(low, dks[0], dks[1])
            dva_ref[:, sl] += jnp.where(low, dvs[0], dvs[1])
            dqs, dks, dvs = [], [], []
    e = None
    at = 0
    for w in cqs:
        n = w.shape[1]
        part = dot(gq_ref[:, at : at + n], w[...], 1, 1)
        e = part if e is None else e + part
        at += n
    u, inverse = standardise(mid_ref[...])
    sums_ref[2:3, :] += column_sums(e * u)
    sums_ref[3:4, :] += column_sums(e)
    g_middle = gmid_ref[...] + norm_input_grad(e, u, inverse, vec_ref[0:1, :])
    gmid_ref[...] = g_middle
    gs = g_middle.astype(jnp.bfloat16)
    gs_ref[...] = gs
    at = 0
    for w in sos:
        n = w.shape[0]
        gctx_ref[:, at : at + n] = dot(gs, w[...], 1, 1).astype(jnp.bfloat16)
        at += n

    @pl.when(i == pl.num_programs(0) - 1)
    def _():
        dk_ref[...] = (dka_ref[...] * HEAD_DIM**-0.5).astype(jnp.bfloat16)
        dv_ref[...] = dva_ref[...].astype(jnp.bfloat16)


def mid_backward(cb, tb, e, after, g, middle, q, cctx, lse, cos, cqs, sos, k, v, vec):
    n, d = after.shape
    smem = pl.BlockSpec(memory_space=pltpu.SMEM)
    bf, f = jnp.bfloat16, jnp.float32
    weights = [*cos, *cqs, *sos, k, v, vec]
    text = jax.ShapeDtypeStruct((TXT_ROW, d), bf)
    sums = jax.ShapeDtypeStruct((8, d), f)
    return pl.pallas_call(
        functools.partial(mid_backward_kernel, len(cos)),
        grid=(n // TB,),
        in_specs=[smem, smem] + [row_block(d)] * 6 + [pl.BlockSpec((16, TB), lambda i: (0, i))] + [whole(w) for w in weights],
        out_specs=[row_block(d)] * 5 + [whole(text), whole(text), whole(sums)],
        out_shape=[jax.ShapeDtypeStruct((n, d), t) for t in (bf, bf, f, bf, bf)] + [text, text, sums],
        scratch_shapes=[
            pltpu.VMEM((d, TXT_ROW), bf),
            pltpu.VMEM((TXT_ROW, d), f),
            pltpu.VMEM((TXT_ROW, d), f),
            pltpu.VMEM((TB, d), bf),
        ],
        compiler_params=pltpu.CompilerParams(vmem_limit_bytes=58 << 20),
        name="mid_backward",
        cost_estimate=pl.CostEstimate(flops=40 * n * d * d // 2, bytes_accessed=46 * n * d // 2, transcendentals=0),
    )(cb, tb, e, after, g, middle, q, cctx, lse, *weights)


def feed_kernel(idx_ref, fr_ref, frt_ref, cot_ref, o_in, e_in, *refs, own, first, last):
    if own:
        fi_src, fo_src = refs[:2]
        refs = refs[2:]
    else:
        fi_srcs, fo_srcs = refs[:2], refs[2:4]
        refs = refs[4:]
    o_out, e_out, gi_ref, go_ref, acc_o, acc_e, fi_buf, fo_buf, act_s, gh_s, wsem, asem = refs
    p = pl.program_id(0)
    slot = p % 2

    def weights(step, into, act):
        if own:
            at = pl.multiple_of(idx_ref[step] * NB, NB)
            act(pltpu.make_async_copy(fi_src.at[:, pl.ds(at, NB)], fi_buf.at[into], wsem.at[into, 0]))
            act(pltpu.make_async_copy(fo_src.at[pl.ds(at, NB), :], fo_buf.at[into], wsem.at[into, 1]))
        else:
            for s in range(2):
                @pl.when(step == s)
                def _(s=s):
                    act(pltpu.make_async_copy(fi_srcs[s], fi_buf.at[into], wsem.at[into, 0]))
                    act(pltpu.make_async_copy(fo_srcs[s], fo_buf.at[into], wsem.at[into, 1]))

    o_load = pltpu.make_async_copy(o_in, acc_o, asem.at[0])
    if not first:
        e_load = pltpu.make_async_copy(e_in, acc_e, asem.at[1])

    @pl.when(p == 0)
    def _():
        weights(p, slot, lambda c: c.start())
        o_load.start()
        if not first:
            e_load.start()
        else:
            acc_e[...] = jnp.zeros_like(acc_e)

    weights(p, slot, lambda c: c.wait())

    @pl.when(p == 0)
    def _():
        weights(p + 1, 1 - slot, lambda c: c.start())

    @pl.when(p == 0)
    def _():
        o_load.wait()
        if not first:
            e_load.wait()

    fi, fo = fi_buf.at[slot], fo_buf.at[slot]
    rows = 256
    blocks = fr_ref.shape[0] // rows

    def products(r):
        sl = slice(rows * r, rows * r + rows)
        return dot(fr_ref[sl, :], fi[...], 1, 0), dot(cot_ref[sl, :], fo[...], 1, 1)

    ahead = 1
    queue = [products(r) for r in range(ahead)]
    for r in range(blocks):
        if r + ahead < blocks:
            queue.append(products(r + ahead))
        h, g = queue.pop(0)
        sl = slice(rows * r, rows * r + rows)
        active, slope = gelu_pair(h)
        active = active.astype(jnp.bfloat16)
        gh = (g * slope).astype(jnp.bfloat16)
        act_s[sl, :] = active
        gh_s[sl, :] = gh
        acc_o[sl, :] += dot(active, fo[...], 1, 0)
        acc_e[sl, :] += dot(gh, fi[...], 1, 1)
    gi_ref[...] = dot(frt_ref[...], gh_s[...], 1, 0).astype(jnp.bfloat16)
    go_ref[...] = dot(act_s[...], cot_ref[...], 0, 0).astype(jnp.bfloat16)

    @pl.when(p == 1)
    def _():
        e_store = pltpu.make_async_copy(acc_e, e_out, asem.at[1])
        e_store.start()
        if last:
            o_out[...] = acc_o[...].astype(jnp.bfloat16)
        else:
            o_store = pltpu.make_async_copy(acc_o, o_out, asem.at[0])
            o_store.start()
            o_store.wait()
        e_store.wait()


def feed_part(idx, rows, rows_t, cot, o_in, e_in, fis, fos, first, last):
    n, d = rows.shape
    own = len(fis) == 1
    bf, f = jnp.bfloat16, jnp.float32
    hbm = pl.BlockSpec(memory_space=pl.ANY)
    once = lambda shape: pl.BlockSpec(shape, lambda p, idx: (0, 0), pipeline_mode=pl.Buffered(1))
    grad = lambda shape: jax.ShapeDtypeStruct(shape, bf)
    return pl.pallas_call(
        functools.partial(feed_kernel, own=own, first=first, last=last),
        grid_spec=pltpu.PrefetchScalarGridSpec(
            num_scalar_prefetch=1,
            grid=(2,),
            in_specs=[once((n, d)), once((d, n)), once((n, d))] + [hbm] * (2 + 2 * len(fis)),
            out_specs=[
                once((n, d)) if last else hbm,
                hbm,
                pl.BlockSpec((d, NB), lambda p, idx: (0, idx[p] % 2)),
                pl.BlockSpec((NB, d), lambda p, idx: (idx[p] % 2, 0)),
            ],
            scratch_shapes=[
                pltpu.VMEM((n, d), f),
                pltpu.VMEM((n, d), f),
                pltpu.VMEM((2, d, NB), bf),
                pltpu.VMEM((2, NB, d), bf),
                pltpu.VMEM((n, NB), bf),
                pltpu.VMEM((n, NB), bf),
                pltpu.SemaphoreType.DMA((2, 2)),
                pltpu.SemaphoreType.DMA((2,)),
            ],
        ),
        out_shape=[
            jax.ShapeDtypeStruct((n, d), bf if last else f),
            jax.ShapeDtypeStruct((n, d), f),
            grad((d, 2 * NB)),
            grad((2 * NB, d)),
        ],
        compiler_params=pltpu.CompilerParams(vmem_limit_bytes=60 << 20),
        name="feed_last" if last else "feed_first" if first else "feed_more",
        cost_estimate=pl.CostEstimate(flops=24 * n * d * NB, bytes_accessed=48 << 20, transcendentals=0),
    )(idx, rows, rows_t, cot, o_in, e_in, *fis, *fos)


def final_kernel(x_ref, gmid_ref, *refs):
    count = (len(refs) - 3) // 2
    gs, ws = refs[:count], refs[count : 2 * count]
    vec_ref, out_ref, sums_ref = refs[2 * count :]

    @pl.when(pl.program_id(0) == 0)
    def _():
        sums_ref[...] = jnp.zeros_like(sums_ref)

    e = None
    for g, w in zip(gs, ws):
        part = dot(g[...], w[...], 1, 1)
        e = part if e is None else e + part
    u, inverse = standardise(x_ref[...].astype(jnp.float32))
    sums_ref[0:1, :] += column_sums(e * u)
    sums_ref[1:2, :] += column_sums(e)
    out_ref[...] = gmid_ref[...] + norm_input_grad(e, u, inverse, vec_ref[4:5, :])


def final_grads(x, gmid, gs, ws, vec):
    n, d = x.shape
    sums = jax.ShapeDtypeStruct((8, d), jnp.float32)
    return pl.pallas_call(
        final_kernel,
        grid=(n // TB,),
        in_specs=[row_block(d), row_block(d)] + [row_block(g.shape[1]) for g in gs] + [whole(w) for w in ws] + [whole(vec)],
        out_specs=[row_block(d), whole(sums)],
        out_shape=[jax.ShapeDtypeStruct((n, d), jnp.float32), sums],
        compiler_params=pltpu.CompilerParams(vmem_limit_bytes=56 << 20),
        name="frames_gradient",
        cost_estimate=pl.CostEstimate(flops=6 * n * d * d, bytes_accessed=24 * n * d // 2, transcendentals=0),
    )(x, gmid, *gs, *ws, vec)


def pair_at(b):
    return (b % 2) * 4 + (b // 2) % 2 * 2 + b // 4


def spread_feed_kernel(t_ref, in_ref, out_ref):
    n = in_ref.shape[1] // 2
    for c in range(2):
        in_ref[:, n * c : n * c + n] = t_ref[c, :, :n].astype(jnp.float32)
        out_ref[c] = t_ref[c, :, n:].astype(jnp.float32)


def spread_feed(t):
    _, rows, columns = t.shape
    n = columns // 2
    f = jnp.float32
    return pl.pallas_call(
        spread_feed_kernel,
        grid=(8,),
        in_specs=[pl.BlockSpec((2, rows, columns), lambda b: (pair_at(b), 0, 0))],
        out_specs=[
            pl.BlockSpec((rows, 2 * n), lambda b: (b, 0)),
            pl.BlockSpec((2, rows, n), lambda b: (0, b, 0)),
        ],
        out_shape=[
            jax.ShapeDtypeStruct((8 * rows, 2 * n), f),
            jax.ShapeDtypeStruct((2, 8 * rows, n), f),
        ],
        compiler_params=pltpu.CompilerParams(vmem_limit_bytes=32 << 20),
        name="spread_feed",
        cost_estimate=pl.CostEstimate(flops=0, bytes_accessed=6 * t.size, transcendentals=0),
    )(t)


def spread_rest_kernel(t_ref, *refs):
    cq, co, so, ck, cv, tw, q, k, v, tb = refs
    n = cq.shape[1] // 2
    b = pl.program_id(0)

    def both(i):
        return jnp.concatenate(
            [t_ref[c, :, n * i : n * i + n].astype(jnp.float32) for c in range(2)], 1
        )

    for i, ref in ((0, cq), (3, ck), (4, cv), (6, q), (7, k), (8, v)):
        ref[...] = both(i)
    co[...] = jnp.transpose(both(1))
    so[...] = jnp.transpose(both(2))

    @pl.when(b < 6)
    def _():
        tw[...] = both(5)

    @pl.when(b == 6)
    def _():
        tb[...] = both(5)[0:8]


def spread_rest(t, n):
    rows = t.shape[1]
    f = jnp.float32
    wide = pl.BlockSpec((rows, 2 * n), lambda b: (b, 0))
    turned = pl.BlockSpec((2 * n, rows), lambda b: (0, b))
    square = jax.ShapeDtypeStruct((8 * rows, 2 * n), f)
    tall = jax.ShapeDtypeStruct((2 * n, 8 * rows), f)
    return pl.pallas_call(
        spread_rest_kernel,
        grid=(8,),
        in_specs=[pl.BlockSpec((2,) + t.shape[1:], lambda b: (pair_at(b), 0, 0))],
        out_specs=[wide, turned, turned, wide, wide, pl.BlockSpec((rows, 2 * n), lambda b: (jnp.minimum(b, 5), 0))]
        + [wide] * 3
        + [pl.BlockSpec((8, 2 * n), lambda b: (0, 0))],
        out_shape=[square, tall, tall, square, square, jax.ShapeDtypeStruct((6 * rows, 2 * n), f)]
        + [square] * 3
        + [jax.ShapeDtypeStruct((8, 2 * n), f)],
        compiler_params=pltpu.CompilerParams(vmem_limit_bytes=32 << 20),
        name="spread_rest",
        cost_estimate=pl.CostEstimate(flops=0, bytes_accessed=6 * t.size, transcendentals=0),
    )(t)


class Journey:
    def __init__(self, hops):
        self.hops = hops
        self.pending = next(hops)
        self.result = None

    def go(self, tied):
        try:
            self.pending = self.hops.send(tied)
        except StopIteration as end:
            self.pending, self.result = None, end.value


def onward(main, *journeys):
    journeys = [j for j in journeys if j.result is None]
    main, tied = lax.optimization_barrier((main, [j.pending for j in journeys]))
    for journey, sent in zip(journeys, tied):
        journey.go(sent)
    return main


def row_body(dp, *args):
    (
        frames,
        text_states,
        clip_lengths,
        text_lengths,
        cotangent,
        self_gain,
        self_shift,
        self_query,
        self_key,
        self_value,
        self_out,
        cross_gain,
        cross_shift,
        cross_query,
        cross_key,
        cross_value,
        cross_out,
        text_weight,
        text_bias,
        feed_gain,
        feed_shift,
        feed_in,
        feed_out,
    ) = args
    bf16, f32 = jnp.bfloat16, jnp.float32
    me = lax.axis_index("dp")
    half = lax.axis_index("mp")
    core = me % 2
    swap = [(0, 1), (1, 0)]
    steps = [2 << i for i in range(dp.bit_length() - 2)]

    def over_y(t):
        return jax.tree.map(lambda a: lax.ppermute(a, "mp", swap), t)

    def over_bit(t, step):
        return jax.tree.map(lambda a: lax.ppermute(a, "dp", [(i, i ^ step) for i in range(dp)]), t)

    def over_core(t):
        return over_bit(t, 1)

    def piece(t, at, size, axis):
        return lax.dynamic_slice_in_dim(t, at * size, size, axis)

    def ordered(mine_first, mine, theirs, axis):
        return jnp.concatenate(
            [jnp.where(mine_first, mine, theirs), jnp.where(mine_first, theirs, mine)], axis
        )

    def add(*ts):
        return reduce(jnp.add, [t.astype(f32) for t in ts]).astype(bf16)

    def parts_of(ts, step):
        at = (me // step) % 2
        size = ts[0].shape[0] // 2
        return [add(*[piece(t, w, size, 0) for t in ts]) for w in (at, 1 - at)]

    def travel(terms, left):
        for step in left:
            kept, sent = parts_of(terms, step)
            sent = yield sent
            terms = (kept, over_bit(sent, step))
        return add(*terms)

    def travel_y(own, other):
        other = yield other
        return (yield from travel((*own, over_y(other)), steps))

    def travel_small(t):
        for hop in (over_core, over_y, *[functools.partial(over_bit, step=s) for s in steps]):
            t = yield t
            t = t + hop(t)
        return t

    lengths = lax.dynamic_index_in_dim(clip_lengths, half, 0, keepdims=False)
    words = lax.dynamic_index_in_dim(text_lengths, half, 0, keepdims=False)
    clip_bounds, text_bounds = jnp.cumsum(lengths), jnp.cumsum(words)
    zeros = jnp.zeros_like(self_gain)
    vec = jnp.stack(
        [cross_gain, cross_shift, feed_gain, feed_shift, self_gain, zeros, zeros, zeros]
    )

    def quarter(t, which, axis):
        return piece(t, which, t.shape[axis] // 2, axis)

    tie = lax.optimization_barrier
    x_at = (me // 2) % 2

    def shared(mine, axis):
        return quarter(mine, x_at, axis)

    def joined(came, across, axis):
        return ordered(x_at == 0, came, across, axis)

    trio = (self_query, self_key, self_value)
    qkv_c = jnp.concatenate([quarter(t, core, 1) for t in trio], 1)
    qkv_d = jnp.concatenate([quarter(t, 1 - core, 1) for t in trio], 1)
    text_part = (product(text_states, text_weight) + text_bias).astype(bf16)
    qkv_half = shared(qkv_c, 0)
    cut = qkv_half.shape[0] // 2
    frames, text_part, qkv_1, qkv_2 = tie((frames, text_part, qkv_half[:cut], qkv_half[cut:]))
    text_came, qkv_1 = over_y(text_part), over_y(qkv_1)
    standard, _ = norm_parts(frames.astype(f32))
    self_rows = (standard * self_gain + self_shift).astype(bf16)
    qkv, ctx, log = [None] * 4, [None] * 4, [None] * 4
    qkv[0] = product(self_rows, qkv_c).astype(bf16)
    qkv[2] = product(self_rows, qkv_d).astype(bf16)
    qkv[0], qkv[2], text_came, qkv_1, qkv_2 = tie((qkv[0], qkv[2], text_came, qkv_1, qkv_2))
    text_full = ordered(half == 0, text_part, text_came, 1)
    keys_here = product(text_full, cross_key).astype(bf16)
    values_here = product(text_full, cross_value).astype(bf16)
    text_rows = TXT_ROW

    def row_of(t, which):
        return piece(t, which, text_rows, 0)

    kv_send = jnp.concatenate([row_of(keys_here, 1 - half), row_of(values_here, 1 - half)], 1)
    qkv_2, across_1 = over_y(qkv_2), over_bit(qkv_1, 2)
    ctx[0], log[0] = group_forward(clip_bounds, qkv[0])
    so_c, cq_c, co_c = quarter(self_out, core, 0), quarter(cross_query, core, 1), quarter(cross_out, core, 0)
    late = [shared(so_c, 0), shared(cq_c, 0), shared(co_c, 0)]
    ctx[0], qkv[2], qkv_2, across_1, kv_send, late = tie(
        (ctx[0], qkv[2], qkv_2, across_1, kv_send, late)
    )
    across_2 = over_bit(qkv_2, 2)
    kv_came = over_y(kv_send)
    so_h = over_y(late[0])
    ctx[2], log[2] = group_forward(clip_bounds, qkv[2])
    ctx[2], across_2, kv_came, so_h = tie((ctx[2], across_2, kv_came, so_h))
    qkv_oc = joined(jnp.concatenate([qkv_1, qkv_2]), jnp.concatenate([across_1, across_2]), 0)
    qkv_oc, rows_1, so_h = tie((qkv_oc, self_rows, so_h))
    qkv_od = over_core(qkv_oc)
    cq_h, so_x = over_y(late[1]), over_bit(so_h, 2)
    qkv[1] = product(rows_1, qkv_oc).astype(bf16)
    qkv[1], cq_h = tie((qkv[1], cq_h))
    co_h, cq_x = over_y(late[2]), over_bit(cq_h, 2)
    ctx[1], log[1] = group_forward(clip_bounds, qkv[1])
    qkv[3] = product(self_rows, qkv_od).astype(bf16)
    so_oc, cq_oc = joined(so_h, so_x, 0), joined(cq_h, cq_x, 0)
    qkv[3], ctx[1], co_h, so_oc, cq_oc = tie((qkv[3], ctx[1], co_h, so_oc, cq_oc))
    co_x = over_bit(co_h, 2)
    so_od, cq_od = over_core(so_oc), over_core(cq_oc)
    ctx[3], log[3] = group_forward(clip_bounds, qkv[3])
    co_oc = joined(co_h, co_x, 0)
    co_od = over_core(co_oc)
    width = cross_key.shape[1]

    def mixed(mine, theirs):
        mine = row_of(mine, half)
        return jnp.concatenate(
            [quarter(t, w, 1) for w in (core, 1 - core) for t in (mine, theirs)], 1
        )

    keys = mixed(keys_here, kv_came[:, :width])
    values = mixed(values_here, kv_came[:, width:])
    qkv_w = [qkv_c, qkv_oc, qkv_d, qkv_od]
    so = [so_c, so_oc, quarter(self_out, 1 - core, 0), so_od]
    cq = [cq_c, cq_oc, quarter(cross_query, 1 - core, 1), cq_od]
    co = [co_c, co_oc, quarter(cross_out, 1 - core, 0), co_od]
    block = 2 * core + x_at
    fi_s, fo_s = piece(feed_in, block, NB, 1), piece(feed_out, block, NB, 0)
    ctx, so, cq, co, keys, values, fi_s, fo_s = tie((ctx, so, cq, co, keys, values, fi_s, fo_s))
    fi_cx = over_y(fi_s)

    middle, cross_rows, cross_q, cross_ctx, cross_log, after, feed_rows, feed_t = mid_forward(
        clip_bounds, text_bounds, frames, ctx, so, cq, co, keys, values, vec
    )

    feed = (feed_rows, feed_t, cotangent)
    places = lambda *t: jnp.stack(t).astype(jnp.int32)
    feed, fi_cx, fo_s = tie((feed, fi_cx, fo_s))
    fo_cx, fi_cy = over_y(fo_s), over_bit(fi_cx, 2)
    o, e, in_od, out_od = feed_part(
        places(2 - 2 * core, 3 - 2 * core), *feed, after, after, [feed_in], [feed_out], True, False
    )
    o, e, fo_cx, fi_cy = tie((o, e, fo_cx, fi_cy))
    fo_cy = over_bit(fo_cx, 2)
    fi_d = over_core([fi_cx, fi_cy])
    o, e, in_oc, out_oc = feed_part(
        places(2 * core, 2 * core + 1), *feed, o, e, [feed_in], [feed_out], False, False
    )
    o, e, fo_cy, fi_d = tie((o, e, fo_cy, fi_d))
    fo_d = over_core([fo_cx, fo_cy])
    o, e, fo_d, in_od, out_od = tie((o, e, fo_d, in_od, out_od))
    in_og, out_og = over_core([in_od, out_od])
    where = places(x_at, 1 - x_at)
    o, e, in_td, out_td = feed_part(where, *feed, o, e, fi_d, fo_d, False, False)
    o, e, in_og, in_td, out_td = tie((o, e, in_og, in_td, out_td))
    own_low, own_high = parts_of((in_oc, in_og), 2)
    o, e, own_low, own_high = tie((o, e, own_low, own_high))
    in_tg, out_tg = over_core([in_td, out_td])
    own_came = over_bit(own_high, 2)
    output, e, in_tc, out_tc = feed_part(
        where, *feed, o, e, [fi_cx, fi_cy], [fo_cx, fo_cy], False, True
    )
    e, in_tg, out_tg, own_came = tie((e, in_tg, out_tg, own_came))
    other_low, other_high = parts_of((in_tc, in_tg), 2)

    def travel_in():
        sent = yield other_high
        other = yield add(other_low, over_bit(sent, 2))
        return (yield from travel((own_low, own_came, over_y(other)), steps[1:]))

    j_in = Journey(travel_in())
    middle_cut = out_tc.shape[1] // 2
    j_out = []
    for sl in (slice(0, middle_cut), slice(middle_cut, None)):
        j_out.append(
            Journey(
                travel_y((out_oc[:, sl], out_og[:, sl]), add(out_tc[:, sl], out_tg[:, sl]))
            )
        )
    e = onward(e, j_in, j_out[0])

    g_c, grad_q, g_middle, g_s, grad_ctx, grad_k, grad_v, sums = mid_backward(
        clip_bounds,
        text_bounds,
        e,
        after,
        cotangent,
        middle,
        cross_q,
        cross_ctx,
        cross_log,
        co,
        cq,
        so,
        keys,
        values,
        vec,
    )
    small = Journey(travel_small(sums[:4]))
    side = width

    def split_heads_back(t):
        oc, tc, od, td = [t[:, side // 2 * n : side // 2 * (n + 1)] for n in range(4)]
        return ordered(core == 0, oc, od, 1), ordered(core == 0, tc, td, 1)

    dk_own, dk_other = split_heads_back(grad_k)
    dv_own, dv_other = split_heads_back(grad_v)
    g_c, text_hop = tie((g_c, jnp.concatenate([dk_other, dv_other], 1)))
    text_hop = over_y(text_hop)
    (g_c, grad_q, g_s, grad_ctx) = onward(
        (g_c, grad_q, g_s, grad_ctx), j_out[0], j_out[1], small
    )

    def both(big, small):
        out = []
        for at in (0, side):
            t = outer_sum(big, small[:, at : at + side]).astype(bf16)
            out.append((t[:, : side // 2], t[:, side // 2 :]))
        return out

    ctx_all = [jnp.concatenate(ctx[:2], 1), jnp.concatenate(ctx[2:], 1)]
    wide = [both(cross_rows, grad_q), both(g_c, cross_ctx)]
    wide = onward(wide, j_in, *j_out, small)
    so_parts = [outer_sum(g_s, t).astype(bf16) for t in ctx_all]
    wide.append([(t[:, : side // 2], t[:, side // 2 :]) for t in so_parts])
    c_keep, c_send = [
        tuple(jnp.concatenate([w[n][m] for w in wide], 1) for m in range(2)) for n in range(2)
    ]

    def split_heads_back(t):
        oc, tc, od, td = [t[:, side // 2 * n : side // 2 * (n + 1)] for n in range(4)]
        return ordered(core == 0, oc, od, 1), ordered(core == 0, tc, td, 1)

    grad_ctx, c_send, text_hop = tie((grad_ctx, c_send, text_hop))
    c_got = over_core(c_send)
    dk = ordered(half == 0, dk_own, text_hop[:, :width], 0)
    dv = ordered(half == 0, dv_own, text_hop[:, width:], 0)
    grad_text = against(dk, cross_key) + against(dv, cross_value)
    text_mine = piece(grad_text, half, width, 1)
    text_hop = piece(grad_text, 1 - half, width, 1).astype(bf16)
    grad_ctx, text_mine, text_hop = tie((grad_ctx, text_mine, text_hop))
    text_hop = over_y(text_hop)

    grads, parts = [None] * 4, [None] * 4

    def kernel(n, main):
        grads[n] = group_backward(clip_bounds, qkv[n], ctx[n], main, log[n], n)

    def finish(n, main):
        parts[n] = outer_sum(self_rows, grads[n]).astype(bf16)
        main, parts[n] = tie((main, parts[n]))
        return main

    main = grad_ctx
    kernel(3, main)
    grads[3], c_got, text_hop = tie((grads[3], c_got, text_hop))
    grad_text = (text_mine + text_hop.astype(f32)).astype(bf16)
    text_part = against(grad_text, text_weight).astype(bf16)
    tall = text_full.shape[1] - text_states.shape[1]
    text_wide = jnp.concatenate(
        [
            text_states,
            jnp.ones((text_states.shape[0], 1), bf16),
            jnp.zeros((text_states.shape[0], tall - 1), bf16),
        ],
        1,
    )
    text_keep, text_send = [
        jnp.concatenate(
            [
                outer_sum(text_full, quarter(dk, w, 1)),
                outer_sum(text_full, quarter(dv, w, 1)),
                outer_sum(text_wide, quarter(grad_text, w, 1)),
            ],
            1,
        ).astype(bf16)
        for w in (core, 1 - core)
    ]
    c_cut = c_keep[0].shape[1] // 2
    j_wide = [
        Journey(
            travel_y((c_keep[0][:, sl], c_got[0][:, sl]), add(c_keep[1][:, sl], c_got[1][:, sl]))
        )
        for sl in (slice(0, c_cut), slice(c_cut, None))
    ]
    grads[3] = onward(grads[3], j_in, *j_out, j_wide[0], small)
    main = finish(3, main)
    main, parts[3], text_send = tie((main, parts[3], text_send))
    td_got, text_got = over_core(parts[3]), over_core(text_send)
    kernel(1, main)
    grads[1], td_got, text_got = tie((grads[1], td_got, text_got))
    j_text = Journey(travel((text_keep, text_got), steps))
    grads[1] = onward(grads[1], j_in, *j_out, j_text, small)
    main = finish(1, main)
    e_cut = parts[1].shape[0] // 2
    other = add(parts[1], td_got)
    main, other = tie((main, other))
    came_1 = over_y(other[:e_cut])
    def gathered(blocks):
        return lax.all_gather(jnp.concatenate(blocks, 1), "dp", axis=0, tiled=False)

    kernel(2, main)
    grads[2], came_1, text_part, blocks = tie(
        (grads[2], came_1, text_part, [j.result for j in (j_in, *j_out)])
    )
    feed_sum = gathered(blocks)
    grads[2] = onward(grads[2], j_wide[0], j_text)
    main = finish(2, main)
    od_got = over_core(parts[2])
    came_2 = over_y(other[e_cut:])
    kernel(0, main)
    grads[0], came_1, came_2, od_got = tie((grads[0], came_1, came_2, od_got))
    grads[0] = onward(grads[0], *j_wide, j_text)
    main = finish(0, main)
    j_self = Journey(travel((parts[0], od_got, jnp.concatenate([came_1, came_2])), steps))
    grads = onward(grads, j_self)
    frames_grad, self_sums = final_grads(frames, g_middle, grads, qkv_w, vec)
    last = Journey(travel_small(self_sums[:2]))
    everything = [j_in, *j_out, *j_wide, j_text, j_self, small, last]
    frames_grad = onward(frames_grad, *[j for j in everything if j.result is None])
    frames_grad, text_part = tie((frames_grad, text_part))
    text_grad = text_part.astype(f32) + over_y(text_part).astype(f32)
    for journey in everything:
        while journey.result is None:
            journey.go(journey.pending)
    early, late = small.result, last.result
    rest_sum = gathered([j.result for j in (*j_wide, j_text, j_self)])

    feed_in_grad, feed_out_grad = spread_feed(feed_sum)
    cq_g, co_g, so_g, ck_g, cv_g, text_g, q_g, k_g, v_g, bias_g = spread_rest(rest_sum, side // 2)
    return (
        output,
        frames_grad,
        text_grad,
        late[0],
        late[1],
        q_g,
        k_g,
        v_g,
        so_g,
        early[2],
        early[3],
        cq_g,
        ck_g,
        cv_g,
        co_g,
        text_g,
        bias_g[0],
        early[0],
        early[1],
        feed_in_grad,
        feed_out_grad.reshape(feed_out.shape),
    )


def chosen(dp, mp, *args):
    rows_here, frames_here = args[2].shape[0], args[0].shape[0]
    if mp == 2 and dp == 16 and rows_here == mp and frames_here == ROW_LEN:
        return row_body(dp, *args)
    return body(*args)


def solution(mesh):
    return jax.shard_map(
        functools.partial(chosen, mesh.shape["dp"], mesh.shape["mp"]),
        mesh=mesh,
        in_specs=(
            P(("dp", "mp"), None),
            P("dp", None),
            P("dp", None),
            P("dp", None),
            P(("dp", "mp"), None),
            P(),
            P(),
            P(None, "mp"),
            P(None, "mp"),
            P(None, "mp"),
            P("mp", None),
            P(),
            P(),
            P(None, "mp"),
            P(None, "mp"),
            P(None, "mp"),
            P("mp", None),
            P(None, "mp"),
            P("mp"),
            P(),
            P(),
            P(None, "mp"),
            P("mp", None),
        ),
        out_specs=(
            P(("dp", "mp"), None),
            P(("dp", "mp"), None),
            P("dp", None),
            P(),
            P(),
            P(None, "mp"),
            P(None, "mp"),
            P(None, "mp"),
            P("mp", None),
            P(),
            P(),
            P(None, "mp"),
            P(None, "mp"),
            P(None, "mp"),
            P("mp", None),
            P(None, "mp"),
            P("mp"),
            P(),
            P(),
            P(None, "mp"),
            P("mp", None),
        ),
        check_vma=False,
    )
```
